32 devices in a mesh: dp: 8 (over z, x), ctx: 4 (over y, core).
Axes of the slice: x: 2, y: 2, z: 4, core: 2. Of those that a mesh axis runs over, the one named last changes fastest.
Arguments:
- tokens: bfloat16 [16, 1024, 1024], P('dp', 'ctx'), may hold values from -6 to 6
- segments: int32 [16, 1024], P('dp'), may hold values from 0 to 2, as said below
- qkv_weight: bfloat16 [1024, 2048], P(('dp', 'ctx')), may hold values from -0.1875 to 0.1875
- out_weight: bfloat16 [1024, 1024], P(None, ('dp', 'ctx')), may hold values from -1.5 to 1.5
- gate_weight: bfloat16 [1024, 4608], P(('dp', 'ctx')), may hold values from -0.1875 to 0.1875
- up_weight: bfloat16 [1024, 4608], P(('dp', 'ctx')), may hold values from -0.1875 to 0.1875
- down_weight: bfloat16 [4608, 1024], P(None, ('dp', 'ctx')), may hold values from -0.09375 to 0.09375
- norm_gains: bfloat16 [2, 1024], P(None, ('dp', 'ctx')), may hold values from 0.099609375 to 1.8984375
- head_gains: bfloat16 [2, 64], replicated, may hold values from 0.099609375 to 1.8984375
- cotangent: bfloat16 [16, 1024, 1024], P('dp', 'ctx'), may hold values from -6 to 6
Outputs:
- output: bfloat16 [16, 1024, 1024], P('dp', 'ctx')
- input_grad: float32 [16, 1024, 1024], P('dp', 'ctx')
- qkv_grad: float32 [1024, 2048], P(('dp', 'ctx'))
- out_grad: float32 [1024, 1024], P(None, ('dp', 'ctx'))
- gate_grad: float32 [1024, 4608], P(('dp', 'ctx'))
- up_grad: float32 [1024, 4608], P(('dp', 'ctx'))
- down_grad: float32 [4608, 1024], P(None, ('dp', 'ctx'))
- norm_grad: float32 [2, 1024], P(None, ('dp', 'ctx'))
- head_grad: float32 [2, 64], replicated
The draws below stay inside these ranges and needn't reach their ends.
Inputs may be any that keep to these rules, and one draw needn't show every extreme that they name: `segments`: never falling along a sequence.
All inputs are finite; a program needn't handle non-finite values.
Results may differ from the reference program's by a relative error of at most 0.018.
Values may be sent and summed in bfloat16 or wider, within the bound.
No kernel may reach another device: no remote copies, remote signals or barrier semaphores. Data moves between devices by JAX's collectives and lax.ppermute only.
A program may use at most 384 MiB of HBM per device.

```python
import math
import jax
import jax.numpy as jnp
from jax import lax

D = 1024
HEADS = 16
KV_HEADS = 8
HEAD = 64
FF = 4608
SEQ = 1024
SPAN = 256
SEQ_GRP = 2
SEQS = 16


def draw_segments(key, part):
    key = jax.random.fold_in(key, 7)
    cut_key, early_key, late_key, pick_key = jax.random.split(key, 4)
    cut_points = jax.random.randint(cut_key, (SEQS, 2), 1, SEQ)
    early_cut = jax.random.randint(early_key, (SEQS, 1), 1, SPAN)
    late_cut = jax.random.randint(late_key, (SEQS, 1), SEQ - SPAN + 1, SEQ)
    picked = jax.random.randint(pick_key, (SEQS // SEQ_GRP, 1), 0, SEQ_GRP)
    member = jnp.arange(SEQS, dtype=jnp.int32).reshape(SEQS // SEQ_GRP, SEQ_GRP)
    spanning = (member % SEQ_GRP == picked).reshape(SEQS, 1)
    chosen = jnp.where(spanning, jnp.concatenate([early_cut, late_cut], axis=1), cut_points)
    places = jnp.arange(SEQ, dtype=jnp.int32)
    return jnp.sum((places[None, None, :] >= chosen[:, :, None]).astype(jnp.int32), axis=1)


def levels(own_key, shape, cuts, low, largest):
    def one(axis_at, blocks):
        heights = jax.random.uniform(jax.random.fold_in(jax.random.fold_in(own_key, 6), axis_at), (blocks,), jnp.float32, low / len(cuts), largest / len(cuts))
        return jnp.repeat(jnp.exp(heights), shape[axis_at] // blocks).reshape((-1,) + (1,) * (len(shape) - axis_at - 1))

    gain = one(*cuts[0])
    for cut in cuts[1:]:
        gain = gain * one(*cut)
    return gain


def centred(rng, shape, spread, limit, shards=(), kind=jnp.bfloat16):
    values = jax.random.normal(rng, shape, jnp.float32) * spread
    if len(shards) > 0:
        values = levels(rng, shape, shards, -0.22, 0.18) * values
    return jnp.clip(values, min=-limit, max=limit).astype(kind)


def setup_inputs(seed: int = 0) -> dict:
    key_list = jax.random.split(jax.random.key(seed), 11)
    return {
        "tokens": centred(key_list[0], (SEQS, SEQ, D), 1.0, 6.0, ((0, 8), (1, 4))),
        "segments": draw_segments(jax.random.fold_in(key_list[10], 71), 0),
        "qkv_weight": centred(key_list[2], (D, (HEADS + 2 * KV_HEADS) * HEAD), D ** -0.5, 0.1875, ((0, 32),)),
        "out_weight": centred(key_list[3], (HEADS * HEAD, D), (max(HEADS * HEAD // 64, 4)) ** -0.5, 1.5, ((1, 32),)),
        "gate_weight": centred(key_list[4], (D, FF), D ** -0.5, 0.1875, ((0, 32),)),
        "up_weight": centred(key_list[5], (D, FF), D ** -0.5, 0.1875, ((0, 32),)),
        "down_weight": centred(key_list[6], (FF, D), FF ** -0.5, 0.09375, ((1, 32),)),
        "norm_gains": jnp.clip(1.0 + 0.18 * jax.random.normal(key_list[7], (2, D), jnp.float32), 0.099609375, 1.8984375).astype(jnp.bfloat16),
        "head_gains": jnp.clip(1.0 + 0.18 * jax.random.normal(key_list[8], (2, HEAD), jnp.float32), 0.099609375, 1.8984375).astype(jnp.bfloat16),
        "cotangent": centred(key_list[9], (SEQS, SEQ, D), 1.0, 6.0, ((0, 8), (1, 4))),
    }


@jax.custom_vjp
def low(v):
    return lax.optimization_barrier(v.astype(jnp.bfloat16)).astype(jnp.float32)

@jax.custom_vjp
def low_back(v):
    return v

def low_keep(v):
    return (low(v), None)

def low_pass(kept, grad):
    return (grad,)

def back_keep(v):
    return (v, None)

def back_low(kept, grad):
    return (low(grad),)
low.defvjp(low_keep, low_pass)
low_back.defvjp(back_keep, back_low)
epsilon = 1e-05
rope_base = 1000000.0
masked_score = -1e+30
highest = lax.Precision.HIGHEST

def rms_unit(values):
    return values * lax.rsqrt(lax.optimization_barrier(jnp.mean(values * values, axis=-1, keepdims=True)) + epsilon)

def angle_tables(positions, size):
    half_size = size // 2
    frequency = jnp.exp(jnp.arange(half_size, dtype=jnp.float32) * (-2.0 * math.log(rope_base) / size))
    angles = positions[:, None] * frequency[None, :]
    return (jnp.cos(angles)[:, None, :], jnp.sin(angles)[:, None, :])

def rotate(values, cosine_table, sine_table):
    half_size = values.shape[-1] // 2
    lead_half = values[..., :half_size]
    tail_half = values[..., half_size:]
    return jnp.concatenate([lead_half * cosine_table - tail_half * sine_table, tail_half * cosine_table + lead_half * sine_table], axis=-1)

def attend_one(queries, key_heads, value_heads, segment):
    seq_length = queries.shape[0]
    grouped = queries.reshape(seq_length, KV_HEADS, HEADS // KV_HEADS, HEAD)
    scores = low_back(HEAD ** (-0.5) * jnp.einsum('qkgd,pkd->kgqp', grouped, key_heads, precision=highest))
    places = jnp.arange(seq_length, dtype=jnp.int32)
    allowed = (segment[:, None] == segment[None, :]) & (places[None, :] <= places[:, None])
    probability = low(jax.nn.softmax(jnp.where(allowed, scores, masked_score), axis=-1))
    attended = jnp.einsum('kgqp,pkd->qkgd', probability, value_heads, precision=highest)
    return attended.reshape(seq_length, HEADS * HEAD)

def attend_pack(bundle):
    return attend_one(bundle[0], bundle[1], bundle[2], bundle[3])

def forward(inputs, segment, qkv_matrix, out_matrix, gate_matrix, up_matrix, down_matrix, norm_rows, head_rows):
    seq_count, seq_length, model_width = inputs.shape
    query_width = HEADS * HEAD
    pair_width = KV_HEADS * HEAD
    hidden_one = low(rms_unit(inputs) * norm_rows[0])
    projected = low_back(jnp.einsum('bsd,de->bse', hidden_one, qkv_matrix, precision=highest))
    query_raw = projected[..., :query_width].reshape(seq_count, seq_length, HEADS, HEAD)
    key_raw = projected[..., query_width:query_width + pair_width].reshape(seq_count, seq_length, KV_HEADS, HEAD)
    value_heads = low(projected[..., query_width + pair_width:].reshape(seq_count, seq_length, KV_HEADS, HEAD))
    cosine_table, sine_table = angle_tables(jnp.arange(seq_length, dtype=jnp.float32), HEAD)
    query_heads = low(rotate(rms_unit(query_raw) * head_rows[0], cosine_table, sine_table))
    key_heads = low(rotate(rms_unit(key_raw) * head_rows[1], cosine_table, sine_table))
    attended = lax.map(jax.checkpoint(attend_pack), (query_heads, key_heads, value_heads, segment))
    attended = low(low_back(attended))
    middle = inputs + low_back(jnp.einsum('bsh,hd->bsd', attended, out_matrix, precision=highest))
    hidden_two = low(rms_unit(middle) * norm_rows[1])
    gate_value = low_back(jnp.einsum('bsd,df->bsf', hidden_two, gate_matrix, precision=highest))
    up_value = low_back(jnp.einsum('bsd,df->bsf', hidden_two, up_matrix, precision=highest))
    inner_act = low(jax.nn.silu(gate_value) * up_value)
    return middle + jnp.einsum('bsf,fd->bsd', inner_act, down_matrix, precision=highest)

def reference(tokens, segments, qkv_weight, out_weight, gate_weight, up_weight, down_weight, norm_gains, head_gains, cotangent):
    matrices = tuple((matrix.astype(jnp.float32) for matrix in (qkv_weight, out_weight, gate_weight, up_weight, down_weight, norm_gains, head_gains)))
    per_step = math.gcd(SEQS, max(1, 4096 // SEQ))
    step_count = SEQS // per_step
    token_steps = tokens.reshape(step_count, per_step, SEQ, D)
    segment_steps = segments.reshape(step_count, per_step, SEQ)
    cot_steps = cotangent.reshape(step_count, per_step, SEQ, D)

    def one_step(grad_sums, batch):
        token_part, segment_part, cot_part = batch

        def forward_part(inputs, qkv_matrix, out_matrix, gate_matrix, up_matrix, down_matrix, norm_rows, head_rows):
            return forward(inputs, segment_part, qkv_matrix, out_matrix, gate_matrix, up_matrix, down_matrix, norm_rows, head_rows)
        output_part, pullback = jax.vjp(forward_part, token_part.astype(jnp.float32), *matrices)
        pulled = pullback(cot_part.astype(jnp.float32))
        grad_sums = tuple((running_sum + addition for running_sum, addition in zip(grad_sums, pulled[1:])))
        return (grad_sums, (output_part.astype(jnp.bfloat16), pulled[0]))
    zero_sums = tuple((jnp.zeros_like(matrix) for matrix in matrices))
    grad_sums, (outputs, input_grads) = lax.scan(one_step, zero_sums, (token_steps, segment_steps, cot_steps))
    return (outputs.reshape(SEQS, SEQ, D), input_grads.reshape(SEQS, SEQ, D), grad_sums[0], grad_sums[1], grad_sums[2], grad_sums[3], grad_sums[4], grad_sums[5], grad_sums[6])
```

```python
import functools
import math

import jax
import jax.numpy as jnp
from jax import lax
from jax.experimental import pallas as pl
from jax.experimental.pallas import tpu as pltpu
from jax.sharding import PartitionSpec as P

HEADS = 16
KV_HEADS = 8
HEAD = 64
LANES = 128
BLOCK = 256

epsilon = 1e-05
rope_base = 1000000.0


def lanes_of(rows):
    return lax.broadcasted_iota(jnp.int32, (rows, LANES), 1)


def swap_halves(pair):
    lane = lanes_of(pair.shape[0])
    return jnp.where((lane & 32) == 0, pltpu.roll(pair, 96, 1), pltpu.roll(pair, 32, 1))


def flip(pair):
    return pltpu.roll(pair, 64, 1)


def head_sum(pair):
    low = lanes_of(pair.shape[0]) < HEAD
    first = jnp.sum(jnp.where(low, pair, 0.0), axis=1, keepdims=True)
    second = jnp.sum(jnp.where(low, 0.0, pair), axis=1, keepdims=True)
    return jnp.where(low, first, second)


def unit_of(pair):
    scaler = lax.rsqrt(head_sum(pair * pair) * (1.0 / HEAD) + epsilon)
    return pair * scaler, scaler


def roped(unit, gain, cosine, sine):
    scaled = unit * gain
    return scaled * cosine + swap_halves(scaled) * sine


def aligned(pair, side):
    return (pair, flip(pair)) if side == 0 else (flip(pair), pair)


def joined(first, second, side):
    low = lanes_of(first.shape[0]) < HEAD
    if side == 0:
        return jnp.where(low, first, flip(second))
    return jnp.where(low, flip(first), second)


def own_lanes(rows, side):
    lane = lanes_of(rows)
    return (lane < HEAD) if side == 0 else (lane >= HEAD)


def nt(left, right):
    return lax.dot_general(left, right, (((1,), (1,)), ((), ())), preferred_element_type=jnp.float32)


def nn(left, right):
    return jnp.dot(left, right, preferred_element_type=jnp.float32)


def put_keys(proj_ref, cosine, sine, gain, kvl, key_s, val_s, turned_s, want_units):
    rows = proj_ref.shape[1]
    pairs = (kvl + 1) // 2
    lane = lanes_of(rows)
    for g in range(kvl):
        side, at = g % 2, g // 2
        free = HEAD * (1 - side)
        ones = jnp.where((lane >= free) & (lane < free + 3), 1.0, 0.0)
        own = own_lanes(rows, side)
        k0 = (kvl + at) * LANES
        unit, _ = unit_of(proj_ref[0, :, k0 : k0 + LANES])
        keys = roped(unit, gain, cosine, sine)
        keys = jnp.where(own, keys, ones)
        key_s[g] = keys.astype(jnp.bfloat16)
        v0 = (kvl + pairs + at) * LANES
        values = jnp.where(own, proj_ref[0, :, v0 : v0 + LANES], ones)
        val_s[g] = values.astype(jnp.bfloat16)
        turned = keys if want_units else values
        turned_s[g] = jnp.transpose(turned).astype(jnp.bfloat16)


def allowed_here(start_row, i, j):
    shape = (BLOCK, 2 * BLOCK)
    key = lax.broadcasted_iota(jnp.int32, shape, 0)
    allowed = key + j * BLOCK >= start_row
    if i == j:
        allowed = allowed & (key <= (lax.broadcasted_iota(jnp.int32, shape, 1) & (BLOCK - 1)))
    return allowed


def attend_kernel(kvl, proj_ref, start_ref, cos_ref, sin_ref, gain_ref, out_ref, lse_ref, key_s, val_s, turned_s):
    rows = proj_ref.shape[1]
    cosine, sine = cos_ref[...], sin_ref[...]
    put_keys(proj_ref, cosine, sine, gain_ref[1:2, :], kvl, key_s, val_s, turned_s, False)
    for g in range(kvl):
        side = g % 2
        free = HEAD * (1 - side)
        own = own_lanes(BLOCK, side)
        for i in range(rows // BLOCK):
            r = slice(i * BLOCK, (i + 1) * BLOCK)
            unit, _ = unit_of(proj_ref[0, r, g * LANES : (g + 1) * LANES])
            pair = roped(unit, gain_ref[0:1, :], cosine[r], sine[r]) * (HEAD**-0.5)
            stack = jnp.concatenate([jnp.where(own, part, 0.0) for part in aligned(pair, side)], axis=0)
            stack = stack.astype(jnp.bfloat16)
            start_row = start_ref[0, :, r]
            start_row = jnp.concatenate([start_row, start_row], axis=1)
            total = jnp.zeros((LANES, 2 * BLOCK), jnp.float32)
            for j in range(i + 1):
                c = slice(j * BLOCK, (j + 1) * BLOCK)
                scores = nt(key_s[g, c, :], stack)
                weight = jnp.where(allowed_here(start_row, i, j), jnp.exp(scores), 0.0)
                total = total + nn(turned_s[g, :, c], weight.astype(jnp.bfloat16))
            total = jnp.transpose(total)
            first, second = total[:BLOCK], total[BLOCK:]
            mass_one, mass_two = first[:, free : free + 1], second[:, free : free + 1]
            out_ref[0, r, g * LANES : (g + 1) * LANES] = joined(
                first / mass_one, second / mass_two, side
            ).astype(out_ref.dtype)
            low = lanes_of(BLOCK) < HEAD
            lse_ref[0, r, g * LANES : (g + 1) * LANES] = jnp.log(jnp.where(low, mass_one, mass_two))


def pieces(value):
    high = value.astype(jnp.bfloat16).astype(jnp.float32)
    middle = (value - high).astype(jnp.bfloat16).astype(jnp.float32)
    return high, middle, value - high - middle


def stacked(pair, row_term, side):
    lane = lanes_of(pair.shape[0])
    own = own_lanes(pair.shape[0], side)
    free = HEAD * (1 - side)
    parts = []
    for value, term in zip(aligned(pair, side), aligned(-row_term, 1 - side)):
        high, middle, rest = pieces(term)
        extra = jnp.where(lane == free, high, jnp.where(lane == free + 1, middle, jnp.where(lane == free + 2, rest, 0.0)))
        parts.append(jnp.where(own, value, extra))
    return jnp.concatenate(parts, axis=0).astype(jnp.bfloat16)


def attend_back_kernel(
    kvl, proj_ref, start_ref, cos_ref, sin_ref, gain_ref, att_ref, lse_ref, datt_ref,
    dproj_ref, head_ref, key_s, val_s, turned_s, dk_s, dv_s,
):
    rows = proj_ref.shape[1]
    pairs = (kvl + 1) // 2
    cosine, sine = cos_ref[...], sin_ref[...]
    put_keys(proj_ref, cosine, sine, gain_ref[1:2, :], kvl, key_s, val_s, turned_s, True)
    dk_s[...] = jnp.zeros(dk_s.shape, jnp.float32)
    dv_s[...] = jnp.zeros(dv_s.shape, jnp.float32)
    query_terms = jnp.zeros((1, LANES), jnp.float32)
    for g in range(kvl):
        side = g % 2
        for i in range(rows // BLOCK):
            r = slice(i * BLOCK, (i + 1) * BLOCK)
            cols = slice(g * LANES, (g + 1) * LANES)
            unit, scaler = unit_of(proj_ref[0, r, cols])
            gain = gain_ref[0:1, :]
            pair = roped(unit, gain, cosine[r], sine[r]) * (HEAD**-0.5)
            d_att = datt_ref[0, r, cols].astype(jnp.float32)
            delta = head_sum(d_att * att_ref[0, r, cols].astype(jnp.float32))
            query_stack = stacked(pair, lse_ref[0, r, cols], side)
            datt_stack = stacked(d_att, delta, side)
            start_row = start_ref[0, :, r]
            start_row = jnp.concatenate([start_row, start_row], axis=1)
            total = jnp.zeros((LANES, 2 * BLOCK), jnp.float32)
            for j in range(i + 1):
                c = slice(j * BLOCK, (j + 1) * BLOCK)
                scores = nt(key_s[g, c, :], query_stack)
                weight = jnp.where(allowed_here(start_row, i, j), jnp.exp(scores), 0.0)
                d_scores = (weight * nt(val_s[g, c, :], datt_stack)).astype(jnp.bfloat16)
                dv_s[g, c, :] += nn(weight.astype(jnp.bfloat16), datt_stack)
                dk_s[g, c, :] += nn(d_scores, query_stack)
                total = total + nn(turned_s[g, :, c], d_scores)
            total = jnp.transpose(total)
            d_pair = joined(total[:BLOCK], total[BLOCK:], side) * (HEAD**-0.5)
            d_unit = d_pair * cosine[r] - swap_halves(d_pair) * sine[r]
            query_terms = query_terms + jnp.sum(d_unit * unit, axis=0, keepdims=True)
            scaled = d_unit * gain
            inner = head_sum(scaled * unit) * (1.0 / HEAD)
            dproj_ref[0, r, cols] = (scaler * (scaled - unit * inner)).astype(dproj_ref.dtype)
    key_terms = jnp.zeros((1, LANES), jnp.float32)
    low = lanes_of(rows) < HEAD
    for at in range(pairs):
        first, second = 2 * at, 2 * at + 1
        k0, v0 = (kvl + at) * LANES, (kvl + pairs + at) * LANES
        d_keys, d_values = jnp.where(low, dk_s[first], 0.0), jnp.where(low, dv_s[first], 0.0)
        if second < kvl:
            d_keys = jnp.where(low, d_keys, dk_s[second])
            d_values = jnp.where(low, d_values, dv_s[second])
        gain = gain_ref[1:2, :]
        unit, scaler = unit_of(proj_ref[0, :, k0 : k0 + LANES])
        d_unit = d_keys * cosine - swap_halves(d_keys) * sine
        key_terms = key_terms + jnp.sum(d_unit * unit, axis=0, keepdims=True)
        scaled = d_unit * gain
        inner = head_sum(scaled * unit) * (1.0 / HEAD)
        dproj_ref[0, :, k0 : k0 + LANES] = (scaler * (scaled - unit * inner)).astype(dproj_ref.dtype)
        dproj_ref[0, :, v0 : v0 + LANES] = d_values.astype(dproj_ref.dtype)
    head_ref[0] = jnp.concatenate([query_terms, key_terms, jnp.zeros((6, LANES), jnp.float32)], axis=0)


def whole_seq(*shape):
    return pl.BlockSpec((1,) + shape, lambda s: (s, 0, 0))


def shared(*shape):
    return pl.BlockSpec(shape, lambda s: (0, 0))


def attention_cost(seqs, rows, kvl, products):
    scores = seqs * kvl * 2 * rows * (rows + BLOCK) // 2
    return pl.CostEstimate(
        flops=products * 2 * scores * LANES, bytes_accessed=seqs * rows * kvl * 3072, transcendentals=scores
    )


def attend(proj, start, tables, gains, kvl):
    seqs, rows, width = proj.shape
    return pl.pallas_call(
        functools.partial(attend_kernel, kvl),
        grid=(seqs,),
        in_specs=[
            whole_seq(rows, width), whole_seq(1, rows), shared(rows, LANES), shared(rows, LANES), shared(8, LANES),
        ],
        out_specs=[whole_seq(rows, kvl * LANES), whole_seq(rows, kvl * LANES)],
        out_shape=[
            jax.ShapeDtypeStruct((seqs, rows, kvl * LANES), jnp.bfloat16),
            jax.ShapeDtypeStruct((seqs, rows, kvl * LANES), jnp.float32),
        ],
        scratch_shapes=[
            pltpu.VMEM((kvl, rows, LANES), jnp.bfloat16),
            pltpu.VMEM((kvl, rows, LANES), jnp.bfloat16),
            pltpu.VMEM((kvl, LANES, rows), jnp.bfloat16),
        ],
        compiler_params=pltpu.CompilerParams(vmem_limit_bytes=48 << 20),
        cost_estimate=attention_cost(seqs, rows, kvl, 2),
    )(proj, start, *tables, gains)


def attend_back(proj, start, tables, gains, att, lse, d_att, kvl):
    seqs, rows, width = proj.shape
    return pl.pallas_call(
        functools.partial(attend_back_kernel, kvl),
        grid=(seqs,),
        in_specs=[
            whole_seq(rows, width), whole_seq(1, rows), shared(rows, LANES), shared(rows, LANES), shared(8, LANES),
            whole_seq(rows, kvl * LANES), whole_seq(rows, kvl * LANES), whole_seq(rows, kvl * LANES),
        ],
        out_specs=[whole_seq(rows, width), whole_seq(8, LANES)],
        out_shape=[
            jax.ShapeDtypeStruct((seqs, rows, width), jnp.bfloat16),
            jax.ShapeDtypeStruct((seqs, 8, LANES), jnp.float32),
        ],
        scratch_shapes=[
            pltpu.VMEM((kvl, rows, LANES), jnp.bfloat16),
            pltpu.VMEM((kvl, rows, LANES), jnp.bfloat16),
            pltpu.VMEM((kvl, LANES, rows), jnp.bfloat16),
            pltpu.VMEM((kvl, rows, LANES), jnp.float32),
            pltpu.VMEM((kvl, rows, LANES), jnp.float32),
        ],
        compiler_params=pltpu.CompilerParams(vmem_limit_bytes=48 << 20),
        cost_estimate=attention_cost(seqs, rows, kvl, 5),
    )(proj, start, *tables, gains, att, lse, d_att)


def ring_of(size):
    return list(range(0, size, 2)) + list(range(size - 1, 0, -2))


def ring_step(value, size, way):
    order = ring_of(size)
    return lax.ppermute(value, "dp", [(order[i], order[(i + way) % size]) for i in range(size)])


def ring_table(size):
    order = ring_of(size)
    place = {d: i for i, d in enumerate(order)}
    return jnp.array([[order[(place[d] + k) % size] for k in range(size)] for d in range(size)], jnp.int32)


def ring_gather(block, size):
    rows, columns = block.shape
    at = ring_table(size)[lax.axis_index("dp")]
    whole = jnp.zeros((size * rows, columns), block.dtype)
    whole = lax.dynamic_update_slice_in_dim(whole, block, at[0] * rows, 0)
    up, down = block, block
    for k in range(1, size // 2):
        up, down = ring_step(up, size, 1), ring_step(down, size, -1)
        whole = lax.dynamic_update_slice_in_dim(whole, up, at[size - k] * rows, 0)
        whole = lax.dynamic_update_slice_in_dim(whole, down, at[k] * rows, 0)
    half = columns // 2 // LANES * LANES
    left, right = ring_step(up[:, :half], size, 1), ring_step(down[:, half:], size, -1)
    far = at[size // 2] * rows
    whole = lax.dynamic_update_slice(whole, left, (far, 0))
    return lax.dynamic_update_slice(whole, right, (far, half))


def ring_sum(terms, size):
    rows, columns = terms.shape[0] // size, terms.shape[1]
    at = ring_table(size)[lax.axis_index("dp")]
    half = columns // 2 // LANES * LANES

    def part(k, first, last):
        return lax.dynamic_slice(terms, (at[k % size] * rows, first), (rows, last - first)).astype(jnp.float32)

    far = size // 2
    left = ring_step(part(far, 0, half).astype(terms.dtype), size, 1).astype(jnp.float32)
    right = ring_step(part(far, half, columns).astype(terms.dtype), size, -1).astype(jnp.float32)
    pad_left = jnp.pad(left, ((0, 0), (0, columns - half)))
    pad_right = jnp.pad(right, ((0, 0), (half, 0)))
    up, down = pad_left, pad_right
    for k in range(far - 1, 0, -1):
        up = ring_step((up + part(k, 0, columns)).astype(terms.dtype), size, 1).astype(jnp.float32)
        down = ring_step((down + part(-k, 0, columns)).astype(terms.dtype), size, -1).astype(jnp.float32)
    return up + down + part(0, 0, columns)


def ctx_send(value, k, size):
    return lax.ppermute(value, "ctx", [(i, i ^ k) for i in range(size)])


def group_gather(block, size):
    blocks = {0: block, 1: ctx_send(block, 1, size)}
    for k in range(2, size, 2):
        blocks[k] = ctx_send(block, k, size)
        blocks[k + 1] = ctx_send(blocks[k], 1, size)
    return [blocks[k] for k in range(size)]


def group_sum(blocks, size):
    near = [
        blocks[k].astype(jnp.float32) + ctx_send(blocks[k + 1], 1, size).astype(jnp.float32)
        for k in range(0, size, 2)
    ]
    total = near[0]
    for k in range(2, size, 2):
        total = total + ctx_send(near[k // 2].astype(jnp.bfloat16), k, size).astype(jnp.float32)
    return total


def exchange(blocks):
    return lax.all_to_all(blocks, "ctx", 0, 0, tiled=True)


def rms_parts(values):
    scaler = lax.rsqrt(jnp.mean(values * values, axis=-1, keepdims=True) + epsilon)
    return values * scaler, scaler


def norm_back(normed, scaler, upstream, gain):
    scaled = upstream * gain
    return scaler * (scaled - normed * jnp.mean(scaled * normed, axis=-1, keepdims=True))


def tn(left, right):
    return lax.dot_general(left, right, (((0,), (0,)), ((), ())), preferred_element_type=jnp.float32)


def rope_tables(length):
    frequency = jnp.exp(jnp.arange(HEAD // 2, dtype=jnp.float32) * (-2.0 * math.log(rope_base) / HEAD))
    angles = jnp.arange(length, dtype=jnp.float32)[:, None] * frequency[None, :]
    cosine, sine = jnp.cos(angles), jnp.sin(angles)
    return (
        jnp.concatenate([cosine] * 4, axis=1),
        jnp.concatenate([-sine, sine, -sine, sine], axis=1),
    )


def split_heads(matrix, ctx):
    rows = matrix.shape[0]
    kvl = KV_HEADS // ctx
    pad = kvl % 2 * HEAD
    query, key, value = jnp.split(matrix, [HEADS * HEAD, (HEADS + KV_HEADS) * HEAD], axis=1)
    parts = [
        query.reshape(rows, ctx, -1),
        jnp.pad(key.reshape(rows, ctx, -1), ((0, 0), (0, 0), (0, pad))),
        jnp.pad(value.reshape(rows, ctx, -1), ((0, 0), (0, 0), (0, pad))),
    ]
    return jnp.concatenate(parts, axis=2).transpose(1, 0, 2)


def merge_heads(parts):
    ctx, rows, _ = parts.shape
    kvl = KV_HEADS // ctx
    wide = (kvl + 1) // 2 * LANES
    query = parts[:, :, : kvl * LANES]
    key = parts[:, :, kvl * LANES : kvl * LANES + kvl * HEAD]
    value = parts[:, :, kvl * LANES + wide : kvl * LANES + wide + kvl * HEAD]
    return jnp.concatenate([part.transpose(1, 0, 2).reshape(rows, -1) for part in (query, key, value)], axis=1)


def split_columns(matrix, ctx):
    return matrix.reshape(matrix.shape[0], ctx, -1).transpose(1, 0, 2)


def merge_columns(parts):
    return parts.transpose(1, 0, 2).reshape(parts.shape[1], -1)


def local(
    dp, ctx, tokens, segments, qkv_weight, out_weight, gate_weight, up_weight, down_weight,
    norm_gains, head_gains, cotangent,
):
    seqs, span, width = tokens.shape
    rows = seqs * span
    length = segments.shape[1]
    kvl = KV_HEADS // ctx
    ffl = gate_weight.shape[1] // ctx
    shard = qkv_weight.shape[0]
    me = lax.axis_index("ctx")
    bf16, f32 = jnp.bfloat16, jnp.float32

    qkv_split = exchange(split_heads(qkv_weight, ctx)).reshape(ctx * shard, -1)
    qkv_full = ring_gather(qkv_split, dp)
    gains_full = lax.all_gather(norm_gains, ("dp", "ctx"), axis=1, tiled=True).astype(f32)
    out_rows = jnp.transpose(out_weight)
    rest = jnp.concatenate(
        [
            jnp.broadcast_to(out_rows[None], (ctx,) + out_rows.shape),
            split_columns(gate_weight, ctx),
            split_columns(up_weight, ctx),
            split_columns(jnp.transpose(down_weight), ctx),
        ],
        axis=2,
    )
    rest = exchange(rest).reshape(ctx * shard, -1)
    rest_full = ring_gather(rest, dp)
    out_full, gate_full, up_full, down_full = jnp.split(
        rest_full, [HEADS * HEAD, HEADS * HEAD + ffl, HEADS * HEAD + 2 * ffl], axis=1
    )

    token_blocks = jnp.stack(group_gather(tokens, ctx))
    whole = jnp.concatenate(
        [lax.dynamic_index_in_dim(token_blocks, me ^ c, 0, keepdims=False) for c in range(ctx)], axis=1
    )
    upstream = jnp.concatenate(group_gather(cotangent.reshape(rows, width), ctx), axis=0)

    start = jnp.sum((segments[:, None, :] < segments[:, :, None]).astype(jnp.int32), axis=2)[:, None, :]
    tables = rope_tables(length)
    head_gain = head_gains.astype(f32)
    gains = jnp.pad(jnp.concatenate([head_gain, head_gain], axis=1), ((0, 6), (0, 0)))

    hidden_one = (rms_parts(whole.astype(f32))[0] * gains_full[0]).astype(bf16).reshape(seqs * length, width)
    proj = nn(hidden_one, qkv_full).reshape(seqs, length, -1)
    att, lse = attend(proj, start, tables, gains, kvl)

    def to_rows(value):
        parts = value.reshape(seqs, ctx, span, -1).transpose(1, 0, 2, 3)
        return merge_columns(exchange(parts).reshape(ctx, rows, -1))

    def to_heads(value):
        parts = exchange(split_columns(value, ctx)).reshape(ctx, seqs, span, -1)
        return parts.transpose(1, 0, 2, 3).reshape(seqs, length, -1)

    inputs = tokens.reshape(rows, width).astype(f32)
    att_rows = to_rows(att)
    middle = inputs + nt(att_rows, out_full)
    unit_two, scaler_two = rms_parts(middle)
    hidden_two = jnp.concatenate(group_gather((unit_two * gains_full[1]).astype(bf16), ctx), axis=0)
    gate = nn(hidden_two, gate_full)
    up = nn(hidden_two, up_full)
    sigmoid = jax.nn.sigmoid(gate)
    silu = gate * sigmoid
    inner = (silu * up).astype(bf16)
    d_inner = nn(upstream, down_full)
    d_gate = (d_inner * up * sigmoid * (1.0 + gate * (1.0 - sigmoid))).astype(bf16)
    d_up = (d_inner * silu).astype(bf16)
    d_two = (nt(d_gate, gate_full) + nt(d_up, up_full)).astype(bf16)
    d_two = group_sum([d_two[k * rows : (k + 1) * rows] for k in range(ctx)], ctx)
    d_middle = cotangent.reshape(rows, width).astype(f32) + norm_back(unit_two, scaler_two, d_two, gains_full[1])
    d_low = d_middle.astype(bf16)
    d_att = to_heads(nn(d_low, out_full).astype(bf16))

    ffn = nt(inner, down_full).astype(bf16)
    ffn = group_sum([ffn[k * rows : (k + 1) * rows] for k in range(ctx)], ctx)
    output = (middle + ffn).astype(bf16).reshape(seqs, span, width)

    wide = jnp.concatenate(
        [
            tn(d_low, att_rows).astype(bf16),
            tn(hidden_two, d_gate).astype(bf16),
            tn(hidden_two, d_up).astype(bf16),
            tn(upstream, inner).astype(bf16),
        ],
        axis=1,
    )
    wide = ring_sum(wide, dp)

    d_proj, head_terms = attend_back(proj, start, tables, gains, att, lse, d_att, kvl)
    d_proj = d_proj.reshape(seqs * length, -1)
    d_one = nt(d_proj, qkv_full).astype(bf16).reshape(seqs, ctx, span, width)
    d_one = group_sum(
        [lax.dynamic_index_in_dim(d_one, me ^ k, 1, keepdims=False).reshape(rows, width) for k in range(ctx)], ctx
    )
    qkv_terms = ring_sum(tn(hidden_one, d_proj).astype(bf16), dp)

    unit_one, scaler_one = rms_parts(inputs)
    input_grad = d_middle + norm_back(unit_one, scaler_one, d_one, gains_full[0])

    out_terms, ffn_terms = wide[:, : HEADS * HEAD], wide[:, HEADS * HEAD :]
    out_grad = lax.psum_scatter(out_terms, "ctx", scatter_dimension=0, tiled=True)
    ffn_terms = exchange(ffn_terms.reshape(ctx, shard, -1))
    gate_grad = merge_columns(ffn_terms[:, :, :ffl])
    up_grad = merge_columns(ffn_terms[:, :, ffl : 2 * ffl])
    down_grad = merge_columns(ffn_terms[:, :, 2 * ffl :])
    qkv_grad = merge_heads(exchange(qkv_terms.reshape(ctx, shard, -1)))

    own_gain = norm_gains.astype(f32)
    norm_one = jnp.sum(qkv_weight.astype(f32) * qkv_grad, axis=1) / own_gain[0]
    norm_two = jnp.sum(gate_weight.astype(f32) * gate_grad + up_weight.astype(f32) * up_grad, axis=1) / own_gain[1]
    head_terms = jnp.sum(head_terms, axis=0)[:2]
    head_terms = head_terms[:, :HEAD] + head_terms[:, HEAD:]
    head_grad = jnp.sum(lax.all_gather(head_terms, ("dp", "ctx"), axis=0), axis=0)
    return (
        output,
        input_grad.reshape(seqs, span, width),
        qkv_grad,
        jnp.transpose(out_grad),
        gate_grad,
        up_grad,
        jnp.transpose(down_grad),
        jnp.stack([norm_one, norm_two]),
        head_grad,
    )


def solution(mesh):
    both = ("dp", "ctx")
    in_specs = (
        P("dp", "ctx", None),
        P("dp", None),
        P(both, None),
        P(None, both),
        P(both, None),
        P(both, None),
        P(None, both),
        P(None, both),
        P(),
        P("dp", "ctx", None),
    )
    out_specs = (
        P("dp", "ctx", None),
        P("dp", "ctx", None),
        P(both, None),
        P(None, both),
        P(both, None),
        P(both, None),
        P(None, both),
        P(None, both),
        P(),
    )
    body = functools.partial(local, mesh.shape["dp"], mesh.shape["ctx"])
    return jax.shard_map(body, mesh=mesh, in_specs=in_specs, out_specs=out_specs, check_vma=False)
```

```python
import functools
import math

import jax
import jax.numpy as jnp
from jax import lax
from jax.experimental import pallas as pl
from jax.experimental.pallas import tpu as pltpu
from jax.sharding import PartitionSpec as P

HEADS = 16
KV_HEADS = 8
HEAD = 64
LANES = 128
BLOCK = 256

epsilon = 1e-05
rope_base = 1000000.0


def lanes_of(rows):
    return lax.broadcasted_iota(jnp.int32, (rows, LANES), 1)


def swap_halves(pair):
    lane = lanes_of(pair.shape[0])
    return jnp.where((lane & 32) == 0, pltpu.roll(pair, 96, 1), pltpu.roll(pair, 32, 1))


def flip(pair):
    return pltpu.roll(pair, 64, 1)


def head_sum(pair):
    low = lanes_of(pair.shape[0]) < HEAD
    first = jnp.sum(jnp.where(low, pair, 0.0), axis=1, keepdims=True)
    second = jnp.sum(jnp.where(low, 0.0, pair), axis=1, keepdims=True)
    return jnp.where(low, first, second)


def unit_of(pair):
    scaler = lax.rsqrt(head_sum(pair * pair) * (1.0 / HEAD) + epsilon)
    return pair * scaler, scaler


def roped(unit, gain, cosine, sine):
    scaled = unit * gain
    return scaled * cosine + swap_halves(scaled) * sine


def aligned(pair, side):
    return (pair, flip(pair)) if side == 0 else (flip(pair), pair)


def joined(first, second, side):
    low = lanes_of(first.shape[0]) < HEAD
    if side == 0:
        return jnp.where(low, first, flip(second))
    return jnp.where(low, flip(first), second)


def own_lanes(rows, side):
    lane = lanes_of(rows)
    return (lane < HEAD) if side == 0 else (lane >= HEAD)


def nt(left, right):
    return lax.dot_general(left, right, (((1,), (1,)), ((), ())), preferred_element_type=jnp.float32)


def nn(left, right):
    return jnp.dot(left, right, preferred_element_type=jnp.float32)


def put_keys(proj_ref, cosine, sine, gain, kvl, key_s, val_s, turned_s, want_units):
    rows = proj_ref.shape[1]
    pairs = (kvl + 1) // 2
    lane = lanes_of(rows)
    for g in range(kvl):
        side, at = g % 2, g // 2
        free = HEAD * (1 - side)
        ones = jnp.where((lane >= free) & (lane < free + 3), 1.0, 0.0)
        own = own_lanes(rows, side)
        k0 = (kvl + at) * LANES
        unit, _ = unit_of(proj_ref[0, :, k0 : k0 + LANES])
        keys = roped(unit, gain, cosine, sine)
        keys = jnp.where(own, keys, ones)
        key_s[g] = keys.astype(jnp.bfloat16)
        v0 = (kvl + pairs + at) * LANES
        values = jnp.where(own, proj_ref[0, :, v0 : v0 + LANES], ones)
        val_s[g] = values.astype(jnp.bfloat16)
        turned = keys if want_units else values
        turned_s[g] = jnp.transpose(turned).astype(jnp.bfloat16)


def allowed_here(start_row, i, j):
    shape = (BLOCK, 2 * BLOCK)
    key = lax.broadcasted_iota(jnp.int32, shape, 0)
    allowed = key + j * BLOCK >= start_row
    if i == j:
        allowed = allowed & (key <= (lax.broadcasted_iota(jnp.int32, shape, 1) & (BLOCK - 1)))
    return allowed


def attend_kernel(kvl, proj_ref, start_ref, cos_ref, sin_ref, gain_ref, out_ref, lse_ref, key_s, val_s, turned_s):
    rows = proj_ref.shape[1]
    cosine, sine = cos_ref[...], sin_ref[...]
    put_keys(proj_ref, cosine, sine, gain_ref[1:2, :], kvl, key_s, val_s, turned_s, False)
    for g in range(kvl):
        side = g % 2
        free = HEAD * (1 - side)
        own = own_lanes(BLOCK, side)
        for i in range(rows // BLOCK):
            r = slice(i * BLOCK, (i + 1) * BLOCK)
            unit, _ = unit_of(proj_ref[0, r, g * LANES : (g + 1) * LANES])
            pair = roped(unit, gain_ref[0:1, :], cosine[r], sine[r]) * (HEAD**-0.5)
            stack = jnp.concatenate([jnp.where(own, part, 0.0) for part in aligned(pair, side)], axis=0)
            stack = stack.astype(jnp.bfloat16)
            start_row = start_ref[0, :, r]
            start_row = jnp.concatenate([start_row, start_row], axis=1)
            total = jnp.zeros((LANES, 2 * BLOCK), jnp.float32)
            for j in range(i + 1):
                c = slice(j * BLOCK, (j + 1) * BLOCK)
                scores = nt(key_s[g, c, :], stack)
                weight = jnp.where(allowed_here(start_row, i, j), jnp.exp(scores), 0.0)
                total = total + nn(turned_s[g, :, c], weight.astype(jnp.bfloat16))
            total = jnp.transpose(total)
            first, second = total[:BLOCK], total[BLOCK:]
            mass_one, mass_two = first[:, free : free + 1], second[:, free : free + 1]
            out_ref[0, r, g * LANES : (g + 1) * LANES] = joined(
                first / mass_one, second / mass_two, side
            ).astype(out_ref.dtype)
            low = lanes_of(BLOCK) < HEAD
            lse_ref[0, r, g * LANES : (g + 1) * LANES] = jnp.log(jnp.where(low, mass_one, mass_two))


def pieces(value):
    high = value.astype(jnp.bfloat16).astype(jnp.float32)
    middle = (value - high).astype(jnp.bfloat16).astype(jnp.float32)
    return high, middle, value - high - middle


def stacked(pair, row_term, side):
    lane = lanes_of(pair.shape[0])
    own = own_lanes(pair.shape[0], side)
    free = HEAD * (1 - side)
    parts = []
    for value, term in zip(aligned(pair, side), aligned(-row_term, 1 - side)):
        high, middle, rest = pieces(term)
        extra = jnp.where(lane == free, high, jnp.where(lane == free + 1, middle, jnp.where(lane == free + 2, rest, 0.0)))
        parts.append(jnp.where(own, value, extra))
    return jnp.concatenate(parts, axis=0).astype(jnp.bfloat16)


def attend_back_kernel(
    kvl, proj_ref, start_ref, cos_ref, sin_ref, gain_ref, att_ref, lse_ref, datt_ref,
    dproj_ref, head_ref, key_s, val_s, turned_s, dk_s, dv_s,
):
    rows = proj_ref.shape[1]
    pairs = (kvl + 1) // 2
    cosine, sine = cos_ref[...], sin_ref[...]
    put_keys(proj_ref, cosine, sine, gain_ref[1:2, :], kvl, key_s, val_s, turned_s, True)
    dk_s[...] = jnp.zeros(dk_s.shape, jnp.float32)
    dv_s[...] = jnp.zeros(dv_s.shape, jnp.float32)
    query_terms = jnp.zeros((1, LANES), jnp.float32)
    for g in range(kvl):
        side = g % 2
        for i in range(rows // BLOCK):
            r = slice(i * BLOCK, (i + 1) * BLOCK)
            cols = slice(g * LANES, (g + 1) * LANES)
            unit, scaler = unit_of(proj_ref[0, r, cols])
            gain = gain_ref[0:1, :]
            pair = roped(unit, gain, cosine[r], sine[r]) * (HEAD**-0.5)
            d_att = datt_ref[0, r, cols].astype(jnp.float32)
            delta = head_sum(d_att * att_ref[0, r, cols].astype(jnp.float32))
            query_stack = stacked(pair, lse_ref[0, r, cols], side)
            datt_stack = stacked(d_att, delta, side)
            start_row = start_ref[0, :, r]
            start_row = jnp.concatenate([start_row, start_row], axis=1)
            total = jnp.zeros((LANES, 2 * BLOCK), jnp.float32)
            for j in range(i + 1):
                c = slice(j * BLOCK, (j + 1) * BLOCK)
                scores = nt(key_s[g, c, :], query_stack)
                weight = jnp.where(allowed_here(start_row, i, j), jnp.exp(scores), 0.0)
                d_scores = (weight * nt(val_s[g, c, :], datt_stack)).astype(jnp.bfloat16)
                dv_s[g, c, :] += nn(weight.astype(jnp.bfloat16), datt_stack)
                dk_s[g, c, :] += nn(d_scores, query_stack)
                total = total + nn(turned_s[g, :, c], d_scores)
            total = jnp.transpose(total)
            d_pair = joined(total[:BLOCK], total[BLOCK:], side) * (HEAD**-0.5)
            d_unit = d_pair * cosine[r] - swap_halves(d_pair) * sine[r]
            query_terms = query_terms + jnp.sum(d_unit * unit, axis=0, keepdims=True)
            scaled = d_unit * gain
            inner = head_sum(scaled * unit) * (1.0 / HEAD)
            dproj_ref[0, r, cols] = (scaler * (scaled - unit * inner)).astype(dproj_ref.dtype)
    key_terms = jnp.zeros((1, LANES), jnp.float32)
    low = lanes_of(rows) < HEAD
    for at in range(pairs):
        first, second = 2 * at, 2 * at + 1
        k0, v0 = (kvl + at) * LANES, (kvl + pairs + at) * LANES
        d_keys, d_values = jnp.where(low, dk_s[first], 0.0), jnp.where(low, dv_s[first], 0.0)
        if second < kvl:
            d_keys = jnp.where(low, d_keys, dk_s[second])
            d_values = jnp.where(low, d_values, dv_s[second])
        gain = gain_ref[1:2, :]
        unit, scaler = unit_of(proj_ref[0, :, k0 : k0 + LANES])
        d_unit = d_keys * cosine - swap_halves(d_keys) * sine
        key_terms = key_terms + jnp.sum(d_unit * unit, axis=0, keepdims=True)
        scaled = d_unit * gain
        inner = head_sum(scaled * unit) * (1.0 / HEAD)
        dproj_ref[0, :, k0 : k0 + LANES] = (scaler * (scaled - unit * inner)).astype(dproj_ref.dtype)
        dproj_ref[0, :, v0 : v0 + LANES] = d_values.astype(dproj_ref.dtype)
    head_ref[0] = jnp.concatenate([query_terms, key_terms, jnp.zeros((6, LANES), jnp.float32)], axis=0)


def whole_seq(*shape):
    return pl.BlockSpec((1,) + shape, lambda s: (s, 0, 0))


def shared(*shape):
    return pl.BlockSpec(shape, lambda s: (0, 0))


def slight():
    return pl.CostEstimate(flops=1, bytes_accessed=1, transcendentals=0)


def attend(proj, start, tables, gains, kvl):
    seqs, rows, width = proj.shape
    return pl.pallas_call(
        functools.partial(attend_kernel, kvl),
        grid=(seqs,),
        in_specs=[
            whole_seq(rows, width), whole_seq(1, rows), shared(rows, LANES), shared(rows, LANES), shared(8, LANES),
        ],
        out_specs=[whole_seq(rows, kvl * LANES), whole_seq(rows, kvl * LANES)],
        out_shape=[
            jax.ShapeDtypeStruct((seqs, rows, kvl * LANES), jnp.bfloat16),
            jax.ShapeDtypeStruct((seqs, rows, kvl * LANES), jnp.float32),
        ],
        scratch_shapes=[
            pltpu.VMEM((kvl, rows, LANES), jnp.bfloat16),
            pltpu.VMEM((kvl, rows, LANES), jnp.bfloat16),
            pltpu.VMEM((kvl, LANES, rows), jnp.bfloat16),
        ],
        compiler_params=pltpu.CompilerParams(vmem_limit_bytes=48 << 20),
        cost_estimate=slight(),
    )(proj, start, *tables, gains)


def attend_back(proj, start, tables, gains, att, lse, d_att, kvl):
    seqs, rows, width = proj.shape
    return pl.pallas_call(
        functools.partial(attend_back_kernel, kvl),
        grid=(seqs,),
        in_specs=[
            whole_seq(rows, width), whole_seq(1, rows), shared(rows, LANES), shared(rows, LANES), shared(8, LANES),
            whole_seq(rows, kvl * LANES), whole_seq(rows, kvl * LANES), whole_seq(rows, kvl * LANES),
        ],
        out_specs=[whole_seq(rows, width), whole_seq(8, LANES)],
        out_shape=[
            jax.ShapeDtypeStruct((seqs, rows, width), jnp.bfloat16),
            jax.ShapeDtypeStruct((seqs, 8, LANES), jnp.float32),
        ],
        scratch_shapes=[
            pltpu.VMEM((kvl, rows, LANES), jnp.bfloat16),
            pltpu.VMEM((kvl, rows, LANES), jnp.bfloat16),
            pltpu.VMEM((kvl, LANES, rows), jnp.bfloat16),
            pltpu.VMEM((kvl, rows, LANES), jnp.float32),
            pltpu.VMEM((kvl, rows, LANES), jnp.float32),
        ],
        compiler_params=pltpu.CompilerParams(vmem_limit_bytes=48 << 20),
        cost_estimate=slight(),
    )(proj, start, *tables, gains, att, lse, d_att)


def ffn_kernel(near_tiles, count, *refs):
    near_h, far_h, near_c, far_c = refs[:4]
    blocks = refs[4 : 4 + count]
    acts, near_d, far_d, near_o, far_o = refs[4 + count : 9 + count]
    weights, sems = refs[9 + count :]
    rows = blocks[0].shape[0]
    wide = weights.shape[1] // 3
    step = pl.program_id(0)

    @pl.when(step == 0)
    def _():
        copies, row, column = [], 0, 0
        for n, block in enumerate(blocks):
            columns = block.shape[1]
            place = weights.at[pl.ds(row, rows), pl.ds(column, columns)]
            copies.append(pltpu.make_async_copy(block, place, sems.at[n]))
            copies[-1].start()
            column += columns
            if column == 3 * wide:
                row, column = row + rows, 0
        for copy in copies:
            copy.wait()

    near = step < near_tiles
    hidden = jnp.where(near, near_h[...], far_h[...])
    upstream = jnp.where(near, near_c[...], far_c[...])
    gate_w, up_w, down_w = weights[:, :wide], weights[:, wide : 2 * wide], weights[:, 2 * wide :]
    gate = nn(hidden, gate_w)
    up = nn(hidden, up_w)
    d_inner = nn(upstream, down_w)
    sigmoid = 1.0 / (1.0 + jnp.exp(-gate))
    silu = gate * sigmoid
    inner = (silu * up).astype(jnp.bfloat16)
    d_gate = (d_inner * up * (sigmoid * (1.0 + gate * (1.0 - sigmoid)))).astype(jnp.bfloat16)
    d_up = (d_inner * silu).astype(jnp.bfloat16)
    acts[0] = d_gate
    acts[1] = d_up
    acts[2] = inner
    d_hidden = (nt(d_gate, gate_w) + nt(d_up, up_w)).astype(jnp.bfloat16)
    out = nt(inner, down_w).astype(jnp.bfloat16)

    @pl.when(near)
    def _():
        near_d[...] = d_hidden
        near_o[...] = out

    @pl.when(jnp.logical_not(near))
    def _():
        far_d[...] = d_hidden
        far_o[...] = out


def feed_forward(hidden, upstream, blocks, wide):
    rows, width = hidden[0].shape
    tile = min(BLOCK, rows)
    tiles = rows // tile
    near = pl.BlockSpec((tile, width), lambda i: (jnp.minimum(i, tiles - 1), 0))
    far = pl.BlockSpec((tile, width), lambda i: (jnp.maximum(i - tiles, 0), 0))
    thin = pl.BlockSpec((3, tile, wide), lambda i: (0, i, 0))
    low = functools.partial(jax.ShapeDtypeStruct, dtype=jnp.bfloat16)
    return pl.pallas_call(
        functools.partial(ffn_kernel, tiles, len(blocks)),
        grid=(2 * tiles,),
        in_specs=[near, far, near, far] + [pl.BlockSpec(memory_space=pl.ANY)] * len(blocks),
        out_specs=[thin, near, far, near, far],
        out_shape=[low((3, 2 * rows, wide))] + [low((rows, width))] * 4,
        scratch_shapes=[pltpu.VMEM((width, 3 * wide), jnp.bfloat16), pltpu.SemaphoreType.DMA((len(blocks),))],
        compiler_params=pltpu.CompilerParams(vmem_limit_bytes=56 << 20),
        cost_estimate=slight(),
    )(*hidden, *upstream, *blocks)


def grad_kernel(count, *refs):
    hidden, upstream, acts, out_ref = refs[:count], refs[count : 2 * count], refs[2 * count : -1], refs[-1]
    rows = hidden[0].shape[1]

    def put(left):
        total = None
        for n in range(count):
            half = slice(n % 2 * rows, (n % 2 + 1) * rows)
            term = nn(left[n][...], acts[n // 2][0, half, :])
            total = term if total is None else total + term
        out_ref[...] = total.astype(out_ref.dtype)

    @pl.when(pl.program_id(0) < 2)
    def _():
        put(hidden)

    @pl.when(pl.program_id(0) == 2)
    def _():
        put(upstream)


def weight_grads(hidden, upstream, acts):
    count = len(hidden)
    width, rows = hidden[0].shape
    wide = acts[0].shape[2]
    tile = min(BLOCK, width)
    last = width // tile - 1
    early = pl.BlockSpec((tile, rows), lambda w, i: (jnp.where(w < 2, i, last), 0))
    late = pl.BlockSpec((tile, rows), lambda w, i: (jnp.where(w < 2, 0, i), 0))
    return pl.pallas_call(
        functools.partial(grad_kernel, count),
        grid=(3, width // tile),
        in_specs=[early] * count + [late] * count + [pl.BlockSpec((1, 2 * rows, wide), lambda w, i: (w, 0, 0))] * len(acts),
        out_specs=pl.BlockSpec((tile, wide), lambda w, i: (i, w)),
        out_shape=jax.ShapeDtypeStruct((width, 3 * wide), jnp.bfloat16),
        compiler_params=pltpu.CompilerParams(vmem_limit_bytes=48 << 20),
        cost_estimate=slight(),
    )(*hidden, *upstream, *acts)


def order_kernel(places_ref, value_ref, out_ref):
    size = places_ref.shape[0]
    wide = value_ref.shape[1] // size
    for k in range(size):
        out_ref[:, k * wide : (k + 1) * wide] = value_ref[:, pl.ds(pl.multiple_of(places_ref[k] * wide, wide), wide)]


def finish_kernel(places_ref, base_ref, *refs):
    out_ref = refs[-1]
    total = base_ref[...]
    for part in refs[:-1]:
        total = total + part[...].astype(jnp.float32)
    put_back(places_ref, total, out_ref)


def put_back(places_ref, total, out_ref):
    size = places_ref.shape[0]
    wide = total.shape[1] // size
    for k in range(size):
        at = pl.multiple_of(places_ref[k] * wide, wide)
        out_ref[:, pl.ds(at, wide)] = total[:, k * wide : (k + 1) * wide].astype(out_ref.dtype)


def input_grad_kernel(places_ref, base_ref, inputs_ref, gain_ref, *refs):
    out_ref = refs[-1]
    upstream = refs[0][...].astype(jnp.float32)
    for part in refs[1:-1]:
        upstream = upstream + part[...].astype(jnp.float32)
    normed, scaler = rms_parts(inputs_ref[...].astype(jnp.float32))
    put_back(places_ref, base_ref[...] + norm_back(normed, scaler, upstream, gain_ref[0:1, :]), out_ref)


def by_rows(kernel, places, operands, dtype):
    rows, width = operands[0].shape
    tile = min(128, rows)
    if width // places.shape[0] % LANES != 0:
        return None

    def spec(shape):
        if shape[0] == rows:
            return pl.BlockSpec((tile, shape[1]), lambda i, places: (i, 0))
        return pl.BlockSpec(shape, lambda i, places: (0, 0))

    return pl.pallas_call(
        kernel,
        grid_spec=pltpu.PrefetchScalarGridSpec(
            num_scalar_prefetch=1,
            grid=(rows // tile,),
            in_specs=[spec(value.shape) for value in operands],
            out_specs=spec((rows, width)),
        ),
        out_shape=jax.ShapeDtypeStruct((rows, width), dtype),
        cost_estimate=slight(),
    )(places, *operands)


def after(value, *others):
    return lax.optimization_barrier((value,) + others)[0]


def ring_of(size):
    return list(range(0, size, 2)) + list(range(size - 1, 0, -2))


def ring_step(value, size, way):
    order = ring_of(size)
    return lax.ppermute(value, "dp", [(order[i], order[(i + way) % size]) for i in range(size)])


def ring_places(size):
    order = ring_of(size)
    place = {d: i for i, d in enumerate(order)}
    table = [[order[(place[d] + k) % size] for k in range(size)] for d in range(size)]
    return jnp.array(table, jnp.int32)[lax.axis_index("dp")]


def to_ring_order(value, places):
    ordered = by_rows(order_kernel, places, [value], value.dtype)
    if ordered is not None:
        return ordered
    size = places.shape[0]
    return value.reshape(value.shape[0], size, -1)[:, places].reshape(value.shape)


def from_ring_order(value, places):
    size = places.shape[0]
    back = jnp.zeros((size,), jnp.int32).at[places].set(jnp.arange(size, dtype=jnp.int32))
    return value.reshape(value.shape[0], size, -1)[:, back].reshape(value.shape)


def finish(kernel, places, operands, dtype):
    done = by_rows(kernel, places, operands, dtype)
    if done is not None:
        return done
    if kernel is finish_kernel:
        total = operands[0] + total_of(operands[1:])
    else:
        normed, scaler = rms_parts(operands[1].astype(jnp.float32))
        total = operands[0] + norm_back(normed, scaler, total_of(operands[3:]), operands[2][0])
    return from_ring_order(total.astype(dtype), places)


def ring_gather(block, size, holds=None):
    blocks = {0: block}
    up, down = block, block
    for k in range(1, size // 2):
        up, down = ring_step(up, size, 1), ring_step(down, size, -1)
        blocks[size - k], blocks[k] = up, down
        if holds and k in holds:
            up, down, _ = lax.optimization_barrier((up, down, holds[k](up, down)))
    half = block.shape[1] // 2 // LANES * LANES
    left, right = ring_step(up[:, :half], size, 1), ring_step(down[:, half:], size, -1)
    whole = []
    for k in range(size):
        whole.extend([left, right] if k == size // 2 else [blocks[k]])
    return whole


def stitched(blocks):
    columns = blocks[0].shape[1]
    rows, at = [], 0
    while at < len(blocks):
        if blocks[at].shape[1] == columns:
            rows.append(blocks[at])
            at += 1
        else:
            rows.append(jnp.concatenate(blocks[at : at + 2], axis=1))
            at += 2
    return jnp.concatenate(lax.optimization_barrier(rows), axis=0)


def ring_sum_steps(terms, size, step, up=None, down=None):
    rows, columns = terms.shape[0] // size, terms.shape[1]
    half = columns // 2 // LANES * LANES
    f32 = jnp.float32

    def part(k):
        k = k % size
        return terms[k * rows : (k + 1) * rows].astype(f32)

    if step == 1:
        far = terms[size // 2 * rows : (size // 2 + 1) * rows]
        left = ring_step(far[:, :half], size, 1)
        right = ring_step(far[:, half:], size, -1)
        up = jnp.pad(left.astype(f32), ((0, 0), (0, columns - half)))
        down = jnp.pad(right.astype(f32), ((0, 0), (half, 0)))
    else:
        up, down = ring_step(up, size, 1), ring_step(down, size, -1)
    k = size // 2 - step
    if k == 0:
        return up, down
    return tuple((sent.astype(f32) + part(m)).astype(terms.dtype) for sent, m in ((up, k), (down, -k)))


def ring_sum(terms, size):
    up = down = None
    for step in range(1, size // 2 + 1):
        up, down = ring_sum_steps(terms, size, step, up, down)
    f32 = jnp.float32
    return up.astype(f32) + down.astype(f32) + terms[: terms.shape[0] // size].astype(f32)


def sum_everywhere(value, size):
    sent = jnp.broadcast_to(value[None], (size,) + value.shape)
    return jnp.sum(lax.all_to_all(sent, ("dp", "ctx"), 0, 0, tiled=True), axis=0)


def ctx_send(value, k, size):
    return lax.ppermute(value, "ctx", [(i, i ^ k) for i in range(size)])


def group_gather(block, size):
    blocks = {0: block, 1: ctx_send(block, 1, size)}
    for k in range(2, size, 2):
        blocks[k] = ctx_send(block, k, size)
        blocks[k + 1] = ctx_send(blocks[k], 1, size)
    return [blocks[k] for k in range(size)]


def far_sums(blocks, chips, size):
    return {
        k: (blocks[k].astype(jnp.float32) + ctx_send(blocks[k + 1], 1, size).astype(jnp.float32)).astype(jnp.bfloat16)
        for k in chips
    }


def group_parts(blocks, size, far=None):
    far = far_sums(blocks, range(2, size, 2), size) if far is None else far
    return [blocks[0], ctx_send(blocks[1], 1, size)] + [ctx_send(far[k], k, size) for k in far]


def total_of(parts):
    total = parts[0].astype(jnp.float32)
    for part in parts[1:]:
        total = total + part.astype(jnp.float32)
    return total


def exchange(blocks):
    return lax.all_to_all(blocks, "ctx", 0, 0, tiled=True)


def rms_parts(values):
    scaler = lax.rsqrt(jnp.mean(values * values, axis=-1, keepdims=True) + epsilon)
    return values * scaler, scaler


def norm_back(normed, scaler, upstream, gain):
    scaled = upstream * gain
    return scaler * (scaled - normed * jnp.mean(scaled * normed, axis=-1, keepdims=True))


def tn(left, right):
    return lax.dot_general(left, right, (((0,), (0,)), ((), ())), preferred_element_type=jnp.float32)


def rope_tables(length):
    frequency = jnp.exp(jnp.arange(HEAD // 2, dtype=jnp.float32) * (-2.0 * math.log(rope_base) / HEAD))
    angles = jnp.arange(length, dtype=jnp.float32)[:, None] * frequency[None, :]
    cosine, sine = jnp.cos(angles), jnp.sin(angles)
    return (
        jnp.concatenate([cosine] * 4, axis=1),
        jnp.concatenate([-sine, sine, -sine, sine], axis=1),
    )


def split_heads(matrix, ctx):
    rows = matrix.shape[0]
    kvl = KV_HEADS // ctx
    pad = kvl % 2 * HEAD
    query, key, value = jnp.split(matrix, [HEADS * HEAD, (HEADS + KV_HEADS) * HEAD], axis=1)
    parts = [
        query.reshape(rows, ctx, -1),
        jnp.pad(key.reshape(rows, ctx, -1), ((0, 0), (0, 0), (0, pad))),
        jnp.pad(value.reshape(rows, ctx, -1), ((0, 0), (0, 0), (0, pad))),
    ]
    return jnp.concatenate(parts, axis=2).transpose(1, 0, 2)


def merge_heads(parts):
    ctx, rows, _ = parts.shape
    kvl = KV_HEADS // ctx
    wide = (kvl + 1) // 2 * LANES
    query = parts[:, :, : kvl * LANES]
    key = parts[:, :, kvl * LANES : kvl * LANES + kvl * HEAD]
    value = parts[:, :, kvl * LANES + wide : kvl * LANES + wide + kvl * HEAD]
    return jnp.concatenate([part.transpose(1, 0, 2).reshape(rows, -1) for part in (query, key, value)], axis=1)


def split_columns(matrix, ctx, wide):
    parts = matrix.reshape(matrix.shape[0], ctx, -1).transpose(1, 0, 2)
    return jnp.pad(parts, ((0, 0), (0, 0), (0, wide - parts.shape[2])))


def merge_columns(parts, keep):
    return parts[:, :, :keep].transpose(1, 0, 2).reshape(parts.shape[1], -1)


def local(
    dp, ctx, tokens, segments, qkv_weight, out_weight, gate_weight, up_weight, down_weight,
    norm_gains, head_gains, cotangent,
):
    seqs, span, width = tokens.shape
    rows = seqs * span
    length = segments.shape[1]
    kvl = KV_HEADS // ctx
    ffl = gate_weight.shape[1] // ctx
    shard = qkv_weight.shape[0]
    me = lax.axis_index("ctx")
    bf16, f32 = jnp.bfloat16, jnp.float32

    places = ring_places(dp)
    ffp = -(-ffl // LANES) * LANES
    hpl = HEADS * HEAD // ctx
    head_wide = (kvl + 2 * ((kvl + 1) // 2)) * LANES
    gain_rows = jnp.pad(jnp.transpose(norm_gains), ((0, 0), (0, LANES - 2)))
    first = [
        split_heads(qkv_weight, ctx),
        split_columns(jnp.transpose(out_weight), ctx, hpl),
        jnp.broadcast_to(gain_rows[None], (ctx, shard, LANES)),
    ]
    first_in = jnp.concatenate(first, axis=2)
    first = ring_gather(exchange(first_in).reshape(ctx * shard, -1), dp)
    first_last = first[-1]
    first = stitched(first)
    qkv_full = first[:, :head_wide]
    gains_full = jnp.transpose(first[:, head_wide + hpl : head_wide + hpl + 2]).astype(f32)
    out_full = group_gather(first[:, head_wide : head_wide + hpl], ctx)

    inputs_low = to_ring_order(after(tokens.reshape(rows, width), first_in), places)
    rest = [gate_weight, up_weight, jnp.transpose(down_weight)]
    rest = exchange(after(jnp.concatenate([split_columns(part, ctx, ffp) for part in rest], axis=2), inputs_low))
    rest = after(rest.reshape(ctx * shard, -1), first_last)
    token_blocks = jnp.stack(group_gather(inputs_low, ctx)).reshape(ctx, seqs, span, width)
    whole = jnp.concatenate(
        [lax.dynamic_index_in_dim(token_blocks, me ^ c, 0, keepdims=False) for c in range(ctx)], axis=1
    )
    cotangent = to_ring_order(after(cotangent.reshape(rows, width), whole), places)
    upstream = group_gather(cotangent, ctx)

    start = jnp.sum((segments[:, None, :] < segments[:, :, None]).astype(jnp.int32), axis=2)[:, None, :]
    tables = rope_tables(length)
    head_gain = head_gains.astype(f32)
    gains = jnp.pad(jnp.concatenate([head_gain, head_gain], axis=1), ((0, 6), (0, 0)))

    whole = after(whole, cotangent)
    hidden_one = (rms_parts(whole.astype(f32))[0] * gains_full[0]).astype(bf16).reshape(seqs * length, width)
    proj = nn(hidden_one, qkv_full).reshape(seqs, length, -1)

    kept = {}

    def attention_now(*ready):
        kept["att"], kept["lse"] = attend(after(proj, *ready), start, tables, gains, kvl)
        return proj

    def middle_now(*ready):
        parts = kept["att"].reshape(seqs, ctx, span, -1)
        parts = [lax.dynamic_index_in_dim(parts, me ^ k, 1, keepdims=False).reshape(rows, -1) for k in range(ctx)]
        kept["parts"] = [parts[0]] + [ctx_send(parts[k], k, ctx) for k in range(1, ctx)]
        return tuple(kept["parts"])

    rest_blocks = ring_gather(rest, dp, {1: attention_now, 2: middle_now} if dp > 4 else None)
    if not kept:
        attention_now()
        middle_now()
    att, lse, att_parts = kept["att"], kept["lse"], kept["parts"]
    att_rows = jnp.concatenate(lax.optimization_barrier((*att_parts, upstream[ctx - 2]))[:ctx], axis=1)
    inputs = inputs_low.astype(f32)
    out_full = jnp.concatenate(out_full, axis=1)
    middle = inputs + nt(att_rows, out_full)
    unit_two, scaler_two = rms_parts(middle)
    hidden_two = group_gather((unit_two * gains_full[1]).astype(bf16), ctx)

    turned = lax.optimization_barrier([jnp.transpose(block) for block in hidden_two + upstream])
    *hidden_two, _ = lax.optimization_barrier((*hidden_two, *turned))[: ctx + 1]
    done, far_two, far_out = {}, {}, {}
    for k in range(ctx - 2, 0, -2):
        done[k] = feed_forward(hidden_two[k : k + 2], upstream[k : k + 2], rest_blocks, ffp)
        far_two.update(far_sums({k: done[k][1], k + 1: done[k][2]}, (k,), ctx))
        far_out.update(far_sums({k: done[k][3], k + 1: done[k][4]}, (k,), ctx))
    own_hidden = lax.optimization_barrier((hidden_two[0], hidden_two[1], *far_two.values(), *far_out.values()))[:2]
    done[0] = feed_forward(own_hidden, upstream[:2], rest_blocks, ffp)
    two_got = [ctx_send(far_two[k], k, ctx) for k in far_two]
    two_own, two_near = lax.optimization_barrier((done[0][1], done[0][2], *two_got))[:2]
    two_near = ctx_send(two_near, 1, ctx)
    out_got = [ctx_send(after(far_out[k], *two_got), k, ctx) for k in far_out]
    out_near = ctx_send(done[0][4], 1, ctx)

    wide = weight_grads(turned[:ctx], turned[ctx:], [done[k][0] for k in range(0, ctx, 2)])
    two_own, two_near, *two_got = lax.optimization_barrier((two_own, two_near, *two_got, wide, *out_got))[: 1 + ctx // 2]
    d_two = total_of([two_own, two_near, *two_got])
    d_middle = cotangent.astype(f32) + norm_back(unit_two, scaler_two, d_two, gains_full[1])
    d_low = d_middle.astype(bf16)
    d_att = nn(d_low, out_full).astype(bf16)
    d_att = [d_att[:, k * hpl : (k + 1) * hpl] for k in range(ctx)]
    late_low = after(d_low, *d_att)
    d_att = [d_att[0]] + [ctx_send(d_att[k], k, ctx) for k in range(1, ctx)]
    out_terms = tn(late_low, att_rows).astype(bf16)
    out_terms = {k: out_terms[:, k * hpl : (k + 1) * hpl] for k in range(ctx)}
    far_terms = far_sums(out_terms, range(2, ctx, 2), ctx)

    def back_now(*ready):
        n = len(backs)
        blocks = lax.optimization_barrier((*d_att, *ready))[:ctx]
        blocks = jnp.stack(blocks).reshape(ctx, seqs, span, -1)[:, n]
        blocks = [lax.dynamic_index_in_dim(blocks, me ^ c, 0, keepdims=False) for c in range(ctx)]
        n = slice(n, n + 1)
        grads = jnp.concatenate(blocks, axis=0)[None]
        backs.append(attend_back(proj[n], start[n], tables, gains, att[n], lse[n], grads, kvl))
        return backs[-1][0]

    backs = []
    if dp > 4:
        up, down, *_ = ring_sum_steps(wide, dp, 1)
        up, down, *_ = lax.optimization_barrier((up, down, *d_att))
        back_now(up, down, *far_terms.values())
        up, down = ring_sum_steps(wide, dp, 2, up, down)
        up, down, _ = lax.optimization_barrier((up, down, backs[0][0]))
        terms_got = group_parts(out_terms, ctx, far_terms)
        while len(backs) < seqs:
            back_now(up, down, *terms_got)
        up, down = ring_sum_steps(wide, dp, 3, up, down)
        ready = (up, down)
        for n in range(4, dp // 2 + 1):
            up, down = ring_sum_steps(wide, dp, n, up, down)
        wide = up.astype(f32) + down.astype(f32) + wide[: ctx * shard].astype(f32)
    else:
        while len(backs) < seqs:
            back_now()
        terms_got = group_parts(out_terms, ctx, far_terms)
        ready = ()
        wide = ring_sum(wide, dp)
    out_terms = total_of(terms_got).astype(bf16)
    output = finish(finish_kernel, places, [middle, done[0][3], out_near, *out_got], bf16)

    d_proj = jnp.concatenate([back[0] for back in backs], axis=0).reshape(seqs * length, -1)
    d_proj = after(d_proj, *ready)
    d_one = nt(d_proj, qkv_full).astype(bf16).reshape(seqs, ctx, span, width)
    d_one = [lax.dynamic_index_in_dim(d_one, me ^ k, 1, keepdims=False).reshape(rows, width) for k in range(ctx)]
    far_one = far_sums(d_one, range(2, ctx, 2), ctx)
    d_one = group_parts(d_one, ctx, far_one)
    d_proj, *head_parts = lax.optimization_barrier((d_proj, *[back[1][0] for back in backs], *far_one.values()))[: 1 + seqs]
    head_terms = sum_everywhere(sum(head_parts), dp * ctx)[:2]
    last = ring_sum(jnp.concatenate([tn(hidden_one, d_proj).astype(bf16), out_terms], axis=1), dp)
    input_grad = finish(input_grad_kernel, places, [d_middle, inputs_low, gains_full] + d_one, f32)

    wide = exchange(wide.astype(bf16).reshape(ctx, shard, -1)).astype(f32)
    gate_grad = merge_columns(wide[:, :, :ffp], ffl)
    up_grad = merge_columns(wide[:, :, ffp : 2 * ffp], ffl)
    down_grad = merge_columns(wide[:, :, 2 * ffp :], ffl)
    last = exchange(last.astype(bf16).reshape(ctx, shard, -1)).astype(f32)
    qkv_grad = merge_heads(last[:, :, :head_wide])
    out_grad = merge_columns(last[:, :, head_wide:], hpl)

    own_gain = norm_gains.astype(f32)
    norm_one = jnp.sum(qkv_weight.astype(f32) * qkv_grad, axis=1) / own_gain[0]
    norm_two = jnp.sum(gate_weight.astype(f32) * gate_grad + up_weight.astype(f32) * up_grad, axis=1) / own_gain[1]
    head_grad = head_terms[:, :HEAD] + head_terms[:, HEAD:]
    return (
        output.reshape(seqs, span, width),
        input_grad.reshape(seqs, span, width),
        qkv_grad,
        jnp.transpose(out_grad),
        gate_grad,
        up_grad,
        jnp.transpose(down_grad),
        jnp.stack([norm_one, norm_two]),
        head_grad,
    )


def solution(mesh):
    both = ("dp", "ctx")
    in_specs = (
        P("dp", "ctx", None),
        P("dp", None),
        P(both, None),
        P(None, both),
        P(both, None),
        P(both, None),
        P(None, both),
        P(None, both),
        P(),
        P("dp", "ctx", None),
    )
    out_specs = (
        P("dp", "ctx", None),
        P("dp", "ctx", None),
        P(both, None),
        P(None, both),
        P(both, None),
        P(both, None),
        P(None, both),
        P(None, both),
        P(),
    )
    body = functools.partial(local, mesh.shape["dp"], mesh.shape["ctx"])
    return jax.shard_map(body, mesh=mesh, in_specs=in_specs, out_specs=out_specs, check_vma=False)
```

```python
import functools
import math

import jax
import jax.numpy as jnp
from jax import lax
from jax.experimental import pallas as pl
from jax.experimental.pallas import tpu as pltpu
from jax.sharding import PartitionSpec as P

HEADS = 16
KV_HEADS = 8
HEAD = 64
LANES = 128
BLOCK = 256

epsilon = 1e-05
rope_base = 1000000.0


def lanes_of(rows):
    return lax.broadcasted_iota(jnp.int32, (rows, LANES), 1)


def swap_halves(pair):
    lane = lanes_of(pair.shape[0])
    return jnp.where((lane & 32) == 0, pltpu.roll(pair, 96, 1), pltpu.roll(pair, 32, 1))


def flip(pair):
    return pltpu.roll(pair, 64, 1)


def head_sum(pair):
    low = lanes_of(pair.shape[0]) < HEAD
    first = jnp.sum(jnp.where(low, pair, 0.0), axis=1, keepdims=True)
    second = jnp.sum(jnp.where(low, 0.0, pair), axis=1, keepdims=True)
    return jnp.where(low, first, second)


def unit_of(pair):
    scaler = lax.rsqrt(head_sum(pair * pair) * (1.0 / HEAD) + epsilon)
    return pair * scaler, scaler


def roped(unit, gain, cosine, sine):
    scaled = unit * gain
    return scaled * cosine + swap_halves(scaled) * sine


def aligned(pair, side):
    return (pair, flip(pair)) if side == 0 else (flip(pair), pair)


def joined(first, second, side):
    low = lanes_of(first.shape[0]) < HEAD
    if side == 0:
        return jnp.where(low, first, flip(second))
    return jnp.where(low, flip(first), second)


def own_lanes(rows, side):
    lane = lanes_of(rows)
    return (lane < HEAD) if side == 0 else (lane >= HEAD)


def nt(left, right):
    return lax.dot_general(left, right, (((1,), (1,)), ((), ())), preferred_element_type=jnp.float32)


def nn(left, right):
    return jnp.dot(left, right, preferred_element_type=jnp.float32)


def put_keys(proj_ref, cosine, sine, gain, kvl, key_s, val_s, turned_s, want_units):
    rows = proj_ref.shape[1]
    pairs = (kvl + 1) // 2
    lane = lanes_of(rows)
    for g in range(kvl):
        side, at = g % 2, g // 2
        free = HEAD * (1 - side)
        ones = jnp.where((lane >= free) & (lane < free + 3), 1.0, 0.0)
        own = own_lanes(rows, side)
        k0 = (kvl + at) * LANES
        unit, _ = unit_of(proj_ref[0, :, k0 : k0 + LANES])
        keys = roped(unit, gain, cosine, sine)
        keys = jnp.where(own, keys, ones)
        key_s[g] = keys.astype(jnp.bfloat16)
        v0 = (kvl + pairs + at) * LANES
        values = jnp.where(own, proj_ref[0, :, v0 : v0 + LANES], ones)
        val_s[g] = values.astype(jnp.bfloat16)
        turned = keys if want_units else values
        turned_s[g] = jnp.transpose(turned).astype(jnp.bfloat16)


def allowed_here(start_row, i, j):
    shape = (BLOCK, 2 * BLOCK)
    key = lax.broadcasted_iota(jnp.int32, shape, 0)
    allowed = key + j * BLOCK >= start_row
    if i == j:
        allowed = allowed & (key <= (lax.broadcasted_iota(jnp.int32, shape, 1) & (BLOCK - 1)))
    return allowed


def attend_kernel(kvl, proj_ref, start_ref, cos_ref, sin_ref, gain_ref, out_ref, lse_ref, key_s, val_s, turned_s):
    rows = proj_ref.shape[1]
    cosine, sine = cos_ref[...], sin_ref[...]
    put_keys(proj_ref, cosine, sine, gain_ref[1:2, :], kvl, key_s, val_s, turned_s, False)
    for g in range(kvl):
        side = g % 2
        free = HEAD * (1 - side)
        own = own_lanes(BLOCK, side)
        for i in range(rows // BLOCK):
            r = slice(i * BLOCK, (i + 1) * BLOCK)
            unit, _ = unit_of(proj_ref[0, r, g * LANES : (g + 1) * LANES])
            pair = roped(unit, gain_ref[0:1, :], cosine[r], sine[r]) * (HEAD**-0.5)
            stack = jnp.concatenate([jnp.where(own, part, 0.0) for part in aligned(pair, side)], axis=0)
            stack = stack.astype(jnp.bfloat16)
            start_row = start_ref[0, :, r]
            start_row = jnp.concatenate([start_row, start_row], axis=1)
            total = jnp.zeros((LANES, 2 * BLOCK), jnp.float32)
            for j in range(i + 1):
                c = slice(j * BLOCK, (j + 1) * BLOCK)
                scores = nt(key_s[g, c, :], stack)
                weight = jnp.where(allowed_here(start_row, i, j), jnp.exp(scores), 0.0)
                total = total + nn(turned_s[g, :, c], weight.astype(jnp.bfloat16))
            total = jnp.transpose(total)
            first, second = total[:BLOCK], total[BLOCK:]
            mass_one, mass_two = first[:, free : free + 1], second[:, free : free + 1]
            out_ref[0, r, g * LANES : (g + 1) * LANES] = joined(
                first / mass_one, second / mass_two, side
            ).astype(out_ref.dtype)
            low = lanes_of(BLOCK) < HEAD
            lse_ref[0, r, g * LANES : (g + 1) * LANES] = jnp.log(jnp.where(low, mass_one, mass_two))


def pieces(value):
    high = value.astype(jnp.bfloat16).astype(jnp.float32)
    middle = (value - high).astype(jnp.bfloat16).astype(jnp.float32)
    return high, middle, value - high - middle


def stacked(pair, row_term, side):
    lane = lanes_of(pair.shape[0])
    own = own_lanes(pair.shape[0], side)
    free = HEAD * (1 - side)
    parts = []
    for value, term in zip(aligned(pair, side), aligned(-row_term, 1 - side)):
        high, middle, rest = pieces(term)
        extra = jnp.where(lane == free, high, jnp.where(lane == free + 1, middle, jnp.where(lane == free + 2, rest, 0.0)))
        parts.append(jnp.where(own, value, extra))
    return jnp.concatenate(parts, axis=0).astype(jnp.bfloat16)


def attend_back_kernel(
    kvl, proj_ref, start_ref, cos_ref, sin_ref, gain_ref, att_ref, lse_ref, datt_ref,
    dproj_ref, head_ref, key_s, val_s, turned_s, dk_s, dv_s,
):
    rows = proj_ref.shape[1]
    pairs = (kvl + 1) // 2
    cosine, sine = cos_ref[...], sin_ref[...]
    put_keys(proj_ref, cosine, sine, gain_ref[1:2, :], kvl, key_s, val_s, turned_s, True)
    dk_s[...] = jnp.zeros(dk_s.shape, jnp.float32)
    dv_s[...] = jnp.zeros(dv_s.shape, jnp.float32)
    query_terms = jnp.zeros((1, LANES), jnp.float32)
    for g in range(kvl):
        side = g % 2
        for i in range(rows // BLOCK):
            r = slice(i * BLOCK, (i + 1) * BLOCK)
            cols = slice(g * LANES, (g + 1) * LANES)
            unit, scaler = unit_of(proj_ref[0, r, cols])
            gain = gain_ref[0:1, :]
            pair = roped(unit, gain, cosine[r], sine[r]) * (HEAD**-0.5)
            d_att = datt_ref[0, r, cols].astype(jnp.float32)
            delta = head_sum(d_att * att_ref[0, r, cols].astype(jnp.float32))
            query_stack = stacked(pair, lse_ref[0, r, cols], side)
            datt_stack = stacked(d_att, delta, side)
            start_row = start_ref[0, :, r]
            start_row = jnp.concatenate([start_row, start_row], axis=1)
            total = jnp.zeros((LANES, 2 * BLOCK), jnp.float32)
            for j in range(i + 1):
                c = slice(j * BLOCK, (j + 1) * BLOCK)
                scores = nt(key_s[g, c, :], query_stack)
                weight = jnp.where(allowed_here(start_row, i, j), jnp.exp(scores), 0.0)
                d_scores = (weight * nt(val_s[g, c, :], datt_stack)).astype(jnp.bfloat16)
                dv_s[g, c, :] += nn(weight.astype(jnp.bfloat16), datt_stack)
                dk_s[g, c, :] += nn(d_scores, query_stack)
                total = total + nn(turned_s[g, :, c], d_scores)
            total = jnp.transpose(total)
            d_pair = joined(total[:BLOCK], total[BLOCK:], side) * (HEAD**-0.5)
            d_unit = d_pair * cosine[r] - swap_halves(d_pair) * sine[r]
            query_terms = query_terms + jnp.sum(d_unit * unit, axis=0, keepdims=True)
            scaled = d_unit * gain
            inner = head_sum(scaled * unit) * (1.0 / HEAD)
            dproj_ref[0, r, cols] = (scaler * (scaled - unit * inner)).astype(dproj_ref.dtype)
    key_terms = jnp.zeros((1, LANES), jnp.float32)
    low = lanes_of(rows) < HEAD
    for at in range(pairs):
        first, second = 2 * at, 2 * at + 1
        k0, v0 = (kvl + at) * LANES, (kvl + pairs + at) * LANES
        d_keys, d_values = jnp.where(low, dk_s[first], 0.0), jnp.where(low, dv_s[first], 0.0)
        if second < kvl:
            d_keys = jnp.where(low, d_keys, dk_s[second])
            d_values = jnp.where(low, d_values, dv_s[second])
        gain = gain_ref[1:2, :]
        unit, scaler = unit_of(proj_ref[0, :, k0 : k0 + LANES])
        d_unit = d_keys * cosine - swap_halves(d_keys) * sine
        key_terms = key_terms + jnp.sum(d_unit * unit, axis=0, keepdims=True)
        scaled = d_unit * gain
        inner = head_sum(scaled * unit) * (1.0 / HEAD)
        dproj_ref[0, :, k0 : k0 + LANES] = (scaler * (scaled - unit * inner)).astype(dproj_ref.dtype)
        dproj_ref[0, :, v0 : v0 + LANES] = d_values.astype(dproj_ref.dtype)
    head_ref[0] = jnp.concatenate([query_terms, key_terms, jnp.zeros((6, LANES), jnp.float32)], axis=0)


def whole_seq(*shape, at=0):
    return pl.BlockSpec((1,) + shape, lambda s: (s + at, 0, 0))


def shared(*shape):
    return pl.BlockSpec(shape, lambda s: (0, 0))


def slight():
    return pl.CostEstimate(flops=1, bytes_accessed=1, transcendentals=0)


def attend(proj, start, tables, gains, kvl, at):
    _, rows, width = proj.shape
    here = functools.partial(whole_seq, at=at)
    return pl.pallas_call(
        functools.partial(attend_kernel, kvl),
        grid=(1,),
        in_specs=[
            here(rows, width), here(1, rows), shared(rows, LANES), shared(rows, LANES), shared(8, LANES),
        ],
        out_specs=[whole_seq(rows, kvl * LANES), whole_seq(rows, kvl * LANES)],
        out_shape=[
            jax.ShapeDtypeStruct((1, rows, kvl * LANES), jnp.bfloat16),
            jax.ShapeDtypeStruct((1, rows, kvl * LANES), jnp.float32),
        ],
        scratch_shapes=[
            pltpu.VMEM((kvl, rows, LANES), jnp.bfloat16),
            pltpu.VMEM((kvl, rows, LANES), jnp.bfloat16),
            pltpu.VMEM((kvl, LANES, rows), jnp.bfloat16),
        ],
        compiler_params=pltpu.CompilerParams(vmem_limit_bytes=48 << 20),
        cost_estimate=slight(),
    )(proj, start, *tables, gains)


def attend_back(proj, start, tables, gains, att, lse, d_att, kvl, at):
    _, rows, width = proj.shape
    here = functools.partial(whole_seq, at=at)
    return pl.pallas_call(
        functools.partial(attend_back_kernel, kvl),
        grid=(1,),
        in_specs=[
            here(rows, width), here(1, rows), shared(rows, LANES), shared(rows, LANES), shared(8, LANES),
            whole_seq(rows, kvl * LANES), whole_seq(rows, kvl * LANES), whole_seq(rows, kvl * LANES),
        ],
        out_specs=[whole_seq(rows, width), whole_seq(8, LANES)],
        out_shape=[
            jax.ShapeDtypeStruct((1, rows, width), jnp.bfloat16),
            jax.ShapeDtypeStruct((1, 8, LANES), jnp.float32),
        ],
        scratch_shapes=[
            pltpu.VMEM((kvl, rows, LANES), jnp.bfloat16),
            pltpu.VMEM((kvl, rows, LANES), jnp.bfloat16),
            pltpu.VMEM((kvl, LANES, rows), jnp.bfloat16),
            pltpu.VMEM((kvl, rows, LANES), jnp.float32),
            pltpu.VMEM((kvl, rows, LANES), jnp.float32),
        ],
        compiler_params=pltpu.CompilerParams(vmem_limit_bytes=48 << 20),
        cost_estimate=slight(),
    )(proj, start, *tables, gains, att, lse, d_att)


def ffn_kernel(near_tiles, count, *refs):
    near_h, far_h, near_c, far_c = refs[:4]
    blocks = refs[4 : 4 + count]
    acts, near_d, far_d, near_o, far_o, turned_h, turned_c = refs[4 + count : 11 + count]
    weights, sems = refs[11 + count :]
    wide = weights.shape[1] // 3
    step = pl.program_id(0)

    def copies(which):
        return column_copies(blocks, which * wide, (which + 1) * wide, weights, sems.at[which])

    @pl.when(step == 0)
    def _():
        for which in range(3):
            for copy in copies(which):
                copy.start()

    def ready(which):
        @pl.when(step == 0)
        def _():
            for copy in copies(which):
                copy.wait()

    near = step < near_tiles
    hidden = jnp.where(near, near_h[...], far_h[...])
    upstream = jnp.where(near, near_c[...], far_c[...])
    ready(0)
    gate_w = weights[:, :wide]
    gate = nn(hidden, gate_w)
    ready(1)
    up_w = weights[:, wide : 2 * wide]
    up = nn(hidden, up_w)
    ready(2)
    down_w = weights[:, 2 * wide :]
    d_inner = nn(upstream, down_w)
    sigmoid = 1.0 / (1.0 + jnp.exp(-gate))
    silu = gate * sigmoid
    inner = (silu * up).astype(jnp.bfloat16)
    d_gate = (d_inner * up * (sigmoid * (1.0 + gate * (1.0 - sigmoid)))).astype(jnp.bfloat16)
    d_up = (d_inner * silu).astype(jnp.bfloat16)
    turned_h[...] = jnp.transpose(hidden)
    turned_c[...] = jnp.transpose(upstream)
    acts[0] = d_gate
    acts[1] = d_up
    acts[2] = inner
    d_hidden = (nt(d_gate, gate_w) + nt(d_up, up_w)).astype(jnp.bfloat16)
    out = nt(inner, down_w).astype(jnp.bfloat16)

    @pl.when(near)
    def _():
        near_d[...] = d_hidden
        near_o[...] = out

    @pl.when(jnp.logical_not(near))
    def _():
        far_d[...] = d_hidden
        far_o[...] = out


def feed_forward(hidden, upstream, blocks, wide):
    rows, width = hidden[0].shape
    tile = min(BLOCK, rows)
    tiles = rows // tile
    near = pl.BlockSpec((tile, width), lambda i: (jnp.minimum(i, tiles - 1), 0))
    far = pl.BlockSpec((tile, width), lambda i: (jnp.maximum(i - tiles, 0), 0))
    thin = pl.BlockSpec((3, tile, wide), lambda i: (0, i, 0))
    turned = pl.BlockSpec((width, tile), lambda i: (0, i))
    low = functools.partial(jax.ShapeDtypeStruct, dtype=jnp.bfloat16)
    return pl.pallas_call(
        functools.partial(ffn_kernel, tiles, len(blocks)),
        grid=(2 * tiles,),
        in_specs=[near, far, near, far] + [pl.BlockSpec(memory_space=pl.ANY)] * len(blocks),
        out_specs=[thin, near, far, near, far, turned, turned],
        out_shape=[low((3, 2 * rows, wide))] + [low((rows, width))] * 4 + [low((width, 2 * rows))] * 2,
        scratch_shapes=[pltpu.VMEM((width, 3 * wide), jnp.bfloat16), pltpu.SemaphoreType.DMA((3, len(blocks)))],
        compiler_params=pltpu.CompilerParams(vmem_limit_bytes=56 << 20),
        cost_estimate=slight(),
    )(*hidden, *upstream, *blocks)


def grad_kernel(count, *refs):
    hidden, upstream, acts, out_ref = refs[:count], refs[count : 2 * count], refs[2 * count : -1], refs[-1]

    def put(left):
        total = nn(left[0][...], acts[0][0])
        for n in range(1, count):
            total = total + nn(left[n][...], acts[n][0])
        out_ref[...] = total.astype(out_ref.dtype)

    @pl.when(pl.program_id(0) < 2)
    def _():
        put(hidden)

    @pl.when(pl.program_id(0) == 2)
    def _():
        put(upstream)


def weight_grads(hidden, upstream, acts):
    count = len(hidden)
    width, rows = hidden[0].shape
    wide = acts[0].shape[2]
    tile = min(2 * BLOCK, width)
    last = width // tile - 1
    early = pl.BlockSpec((tile, rows), lambda w, i: (jnp.where(w < 2, i, last), 0))
    late = pl.BlockSpec((tile, rows), lambda w, i: (jnp.where(w < 2, 0, i), 0))
    return pl.pallas_call(
        functools.partial(grad_kernel, count),
        grid=(3, width // tile),
        in_specs=[early] * count + [late] * count + [pl.BlockSpec((1, rows, wide), lambda w, i: (w, 0, 0))] * count,
        out_specs=pl.BlockSpec((tile, wide), lambda w, i: (i, w)),
        out_shape=jax.ShapeDtypeStruct((width, 3 * wide), jnp.bfloat16),
        compiler_params=pltpu.CompilerParams(vmem_limit_bytes=56 << 20),
        cost_estimate=slight(),
    )(*hidden, *upstream, *acts)


def order_kernel(places_ref, value_ref, out_ref):
    size = places_ref.shape[0]
    wide = value_ref.shape[1] // size
    for k in range(size):
        out_ref[:, k * wide : (k + 1) * wide] = value_ref[:, pl.ds(pl.multiple_of(places_ref[k] * wide, wide), wide)]


def finish_kernel(places_ref, base_ref, *refs):
    out_ref = refs[-1]
    total = base_ref[...]
    for part in refs[:-1]:
        total = total + part[...].astype(jnp.float32)
    put_back(places_ref, total, out_ref)


def put_back(places_ref, total, out_ref):
    size = places_ref.shape[0]
    wide = total.shape[1] // size
    for k in range(size):
        at = pl.multiple_of(places_ref[k] * wide, wide)
        out_ref[:, pl.ds(at, wide)] = total[:, k * wide : (k + 1) * wide].astype(out_ref.dtype)


def input_grad_kernel(places_ref, base_ref, inputs_ref, gain_ref, *refs):
    out_ref = refs[-1]
    upstream = refs[0][...].astype(jnp.float32)
    for part in refs[1:-1]:
        upstream = upstream + part[...].astype(jnp.float32)
    normed, scaler = rms_parts(inputs_ref[...].astype(jnp.float32))
    put_back(places_ref, base_ref[...] + norm_back(normed, scaler, upstream, gain_ref[0:1, :]), out_ref)


def column_copies(blocks, first, last, target, sems, origin=0):
    rows = blocks[0].shape[0]
    columns = max(block.shape[1] for block in blocks)
    made, row, column = [], 0, 0
    for n, block in enumerate(blocks):
        low, high = max(first, column), min(last, column + block.shape[1])
        if low < high:
            source = block.at[:, pl.ds(low - column, high - low)]
            place = target.at[pl.ds(row, rows), pl.ds(low - origin, high - low)]
            made.append(pltpu.make_async_copy(source, place, sems.at[n]))
        column += block.shape[1]
        if column == columns:
            row, column = row + rows, 0
    return made


def assemble_kernel(count, edges, *refs):
    blocks, outs = refs[:count], refs[count:]
    rows, columns = blocks[0].shape[0], max(block.shape[1] for block in blocks)
    row, column = 0, 0
    for block in blocks:
        for out, first, last in zip(outs, edges, edges[1:]):
            low, high = max(first, column), min(last, column + block.shape[1])
            if low < high:
                out[row : row + rows, low - first : high - first] = block[:, low - column : high - column]
        column += block.shape[1]
        if column == columns:
            row, column = row + rows, 0


def assemble(blocks, edges):
    rows = blocks[0].shape[0] * (len(blocks) - 1)
    return pl.pallas_call(
        functools.partial(assemble_kernel, len(blocks), edges),
        out_shape=[
            jax.ShapeDtypeStruct((rows, last - first), blocks[0].dtype) for first, last in zip(edges, edges[1:])
        ],
        compiler_params=pltpu.CompilerParams(vmem_limit_bytes=48 << 20),
        cost_estimate=pl.CostEstimate(flops=0, bytes_accessed=4 * rows * edges[-1], transcendentals=0),
    )(*blocks)


def project_kernel(count, me_ref, gain_ref, weight_ref, *refs):
    blocks, hidden_ref, proj_ref = refs[:count], refs[-2], refs[-1]
    which = me_ref[0] ^ pl.program_id(1)
    value = blocks[0][...]
    for k in range(1, count):
        value = jnp.where(which == k, blocks[k][...], value)
    hidden = (rms_parts(value.astype(jnp.float32))[0] * gain_ref[0:1, :]).astype(jnp.bfloat16)
    hidden_ref[...] = hidden
    proj_ref[0] = nn(hidden, weight_ref[...])


def project(blocks, gains, weight, me, span):
    rows, width = blocks[0].shape
    count, seqs, columns = len(blocks), rows // span, weight.shape[1]
    block = pl.BlockSpec((span, width), lambda s, c, _: (s, 0))

    def held(value):
        return pl.BlockSpec(value.shape, lambda s, c, _: (0, 0))

    return pl.pallas_call(
        functools.partial(project_kernel, count),
        grid_spec=pltpu.PrefetchScalarGridSpec(
            num_scalar_prefetch=1,
            grid=(seqs, count),
            in_specs=[held(gains), held(weight)] + [block] * count,
            out_specs=[
                pl.BlockSpec((span, width), lambda s, c, _: (s * count + c, 0)),
                pl.BlockSpec((1, span, columns), lambda s, c, _: (s, c, 0)),
            ],
        ),
        out_shape=[
            jax.ShapeDtypeStruct((count * rows, width), jnp.bfloat16),
            jax.ShapeDtypeStruct((seqs, count * span, columns), jnp.float32),
        ],
        compiler_params=pltpu.CompilerParams(vmem_limit_bytes=48 << 20),
        cost_estimate=slight(),
    )(me.reshape(1).astype(jnp.int32), gains, weight, *blocks)


def by_rows(kernel, places, operands, dtype):
    rows, width = operands[0].shape
    tile = min(512 if kernel is order_kernel else 256, rows)
    if width // places.shape[0] % LANES != 0:
        return None

    def spec(shape):
        if shape[0] == rows:
            return pl.BlockSpec((tile, shape[1]), lambda i, places: (i, 0))
        return pl.BlockSpec(shape, lambda i, places: (0, 0))

    return pl.pallas_call(
        kernel,
        grid_spec=pltpu.PrefetchScalarGridSpec(
            num_scalar_prefetch=1,
            grid=(rows // tile,),
            in_specs=[spec(value.shape) for value in operands],
            out_specs=spec((rows, width)),
        ),
        out_shape=jax.ShapeDtypeStruct((rows, width), dtype),
        compiler_params=pltpu.CompilerParams(vmem_limit_bytes=48 << 20),
        cost_estimate=slight(),
    )(places, *operands)


def tied(*values):
    return lax.optimization_barrier(values)


def ring_of(size):
    return list(range(0, size, 2)) + list(range(size - 1, 0, -2))


def ring_step(value, size, way):
    order = ring_of(size)
    return lax.ppermute(value, "dp", [(order[i], order[(i + way) % size]) for i in range(size)])


def ring_places(size):
    order = ring_of(size)
    place = {d: i for i, d in enumerate(order)}
    table = [[order[(place[d] + k) % size] for k in range(size)] for d in range(size)]
    return jnp.array(table, jnp.int32)[lax.axis_index("dp")]


def to_ring_order(value, places):
    ordered = by_rows(order_kernel, places, [value], value.dtype)
    if ordered is not None:
        return ordered
    size = places.shape[0]
    return value.reshape(value.shape[0], size, -1)[:, places].reshape(value.shape)


def from_ring_order(value, places):
    size = places.shape[0]
    back = jnp.zeros((size,), jnp.int32).at[places].set(jnp.arange(size, dtype=jnp.int32))
    return value.reshape(value.shape[0], size, -1)[:, back].reshape(value.shape)


def finish(kernel, places, operands, dtype):
    done = by_rows(kernel, places, operands, dtype)
    if done is not None:
        return done
    if kernel is finish_kernel:
        total = operands[0] + total_of(operands[1:])
    else:
        normed, scaler = rms_parts(operands[1].astype(jnp.float32))
        total = operands[0] + norm_back(normed, scaler, total_of(operands[3:]), operands[2][0])
    return from_ring_order(total.astype(dtype), places)


class Gathering:
    def __init__(self, block, size):
        self.size, self.taken, self.columns = size, 0, block.shape[1]
        self.blocks = {0: block}
        self.up = self.down = block

    def step(self):
        self.taken += 1
        if self.taken < self.size // 2:
            self.up, self.down = ring_step(self.up, self.size, 1), ring_step(self.down, self.size, -1)
        else:
            half = self.columns // 2 // LANES * LANES
            self.up = ring_step(self.up[:, :half], self.size, 1)
            self.down = ring_step(self.down[:, half:], self.size, -1)
        self.keep()

    def keep(self):
        if self.taken < self.size // 2:
            self.blocks[self.size - self.taken], self.blocks[self.taken] = self.up, self.down
        else:
            self.blocks[self.taken] = (self.up, self.down)

    def hold(self, *others):
        self.up, self.down, *others = tied(self.up, self.down, *others)
        self.keep()
        return others

    def all(self):
        while self.taken < self.size // 2:
            self.step()
        whole = []
        for k in range(self.size):
            whole.extend(self.blocks[k] if k == self.size // 2 else [self.blocks[k]])
        return whole


class Summing:
    def __init__(self, terms, size):
        self.terms, self.size, self.taken = terms, size, 0
        self.rows, self.columns = terms.shape[0] // size, terms.shape[1]
        self.up = self.down = None

    def part(self, k):
        k = k % self.size
        return self.terms[k * self.rows : (k + 1) * self.rows]

    def send(self):
        self.taken += 1
        if self.taken == 1:
            half = self.columns // 2 // LANES * LANES
            far = self.part(self.size // 2)
            self.up, self.down = far[:, :half], far[:, half:]
        self.up, self.down = ring_step(self.up, self.size, 1), ring_step(self.down, self.size, -1)

    def hold(self, *others):
        self.up, self.down, *others = tied(self.up, self.down, *others)
        return others

    def add(self):
        f32 = jnp.float32
        up, down = self.up.astype(f32), self.down.astype(f32)
        if self.taken == 1:
            up = jnp.pad(up, ((0, 0), (0, self.columns - up.shape[1])))
            down = jnp.pad(down, ((0, 0), (self.columns - down.shape[1], 0)))
        k = self.size // 2 - self.taken
        if k == 0:
            return up + down + self.part(0).astype(f32)
        low = self.terms.dtype
        self.up, self.down = (up + self.part(k).astype(f32)).astype(low), (down + self.part(-k).astype(f32)).astype(low)

    def total(self):
        while self.taken < self.size // 2 - 1:
            self.send()
            self.add()
        if self.taken < self.size // 2:
            self.send()
        return self.add()


def sum_everywhere(value, size):
    sent = jnp.broadcast_to(value[None], (size,) + value.shape)
    return jnp.sum(lax.all_to_all(sent, ("dp", "ctx"), 0, 0, tiled=True), axis=0)


def ctx_send(value, k, size):
    return lax.ppermute(value, "ctx", [(i, i ^ k) for i in range(size)])


def to_chips(block, size):
    return {k: ctx_send(block, k, size) for k in range(2, size, 2)}


def from_pairs(far, size):
    return {k + 1: ctx_send(far[k], 1, size) for k in far}


def far_sums(blocks, chips, size):
    return {
        k: (blocks[k].astype(jnp.float32) + ctx_send(blocks[k + 1], 1, size).astype(jnp.float32)).astype(jnp.bfloat16)
        for k in chips
    }


def group_parts(blocks, size, far=None):
    far = far_sums(blocks, range(2, size, 2), size) if far is None else far
    return [blocks[0], ctx_send(blocks[1], 1, size)] + [ctx_send(far[k], k, size) for k in far]


def total_of(parts):
    total = parts[0].astype(jnp.float32)
    for part in parts[1:]:
        total = total + part.astype(jnp.float32)
    return total


def exchange(blocks):
    return lax.all_to_all(blocks, "ctx", 0, 0, tiled=True)


def rms_parts(values):
    scaler = lax.rsqrt(jnp.mean(values * values, axis=-1, keepdims=True) + epsilon)
    return values * scaler, scaler


def norm_back(normed, scaler, upstream, gain):
    scaled = upstream * gain
    return scaler * (scaled - normed * jnp.mean(scaled * normed, axis=-1, keepdims=True))


def tn(left, right):
    return lax.dot_general(left, right, (((0,), (0,)), ((), ())), preferred_element_type=jnp.float32)


def rope_tables(length):
    frequency = jnp.exp(jnp.arange(HEAD // 2, dtype=jnp.float32) * (-2.0 * math.log(rope_base) / HEAD))
    angles = jnp.arange(length, dtype=jnp.float32)[:, None] * frequency[None, :]
    cosine, sine = jnp.cos(angles), jnp.sin(angles)
    return (
        jnp.concatenate([cosine] * 4, axis=1),
        jnp.concatenate([-sine, sine, -sine, sine], axis=1),
    )


def split_heads(matrix, ctx):
    rows = matrix.shape[0]
    kvl = KV_HEADS // ctx
    pad = kvl % 2 * HEAD
    query, key, value = jnp.split(matrix, [HEADS * HEAD, (HEADS + KV_HEADS) * HEAD], axis=1)
    parts = [
        query.reshape(rows, ctx, -1),
        jnp.pad(key.reshape(rows, ctx, -1), ((0, 0), (0, 0), (0, pad))),
        jnp.pad(value.reshape(rows, ctx, -1), ((0, 0), (0, 0), (0, pad))),
    ]
    return jnp.concatenate(parts, axis=2).transpose(1, 0, 2)


def merge_heads(parts):
    ctx, rows, _ = parts.shape
    kvl = KV_HEADS // ctx
    wide = (kvl + 1) // 2 * LANES
    query = parts[:, :, : kvl * LANES]
    key = parts[:, :, kvl * LANES : kvl * LANES + kvl * HEAD]
    value = parts[:, :, kvl * LANES + wide : kvl * LANES + wide + kvl * HEAD]
    return jnp.concatenate([part.transpose(1, 0, 2).reshape(rows, -1) for part in (query, key, value)], axis=1)


def split_columns(matrix, ctx, wide):
    parts = matrix.reshape(matrix.shape[0], ctx, -1).transpose(1, 0, 2)
    return jnp.pad(parts, ((0, 0), (0, 0), (0, wide - parts.shape[2])))


def merge_columns(parts, keep):
    return parts[:, :, :keep].transpose(1, 0, 2).reshape(parts.shape[1], -1)


def local(
    dp, ctx, tokens, segments, qkv_weight, out_weight, gate_weight, up_weight, down_weight,
    norm_gains, head_gains, cotangent,
):
    seqs, span, width = tokens.shape
    rows = seqs * span
    length = segments.shape[1]
    kvl = KV_HEADS // ctx
    ffl = gate_weight.shape[1] // ctx
    shard = qkv_weight.shape[0]
    me = lax.axis_index("ctx")
    bf16, f32 = jnp.bfloat16, jnp.float32

    places = ring_places(dp)
    ffp = -(-ffl // LANES) * LANES
    hpl = HEADS * HEAD // ctx
    head_wide = (kvl + 2 * ((kvl + 1) // 2)) * LANES
    gain_rows = jnp.pad(jnp.transpose(norm_gains), ((0, 0), (0, LANES - 2)))
    first = [
        split_heads(qkv_weight, ctx),
        split_columns(jnp.transpose(out_weight), ctx, hpl),
        jnp.broadcast_to(gain_rows[None], (ctx, shard, LANES)),
    ]
    rest = [split_columns(part, ctx, ffp) for part in (gate_weight, up_weight, jnp.transpose(down_weight))]
    first, rest = tied(jnp.concatenate(first, axis=2), jnp.concatenate(rest, axis=2))
    first = Gathering(exchange(first).reshape(ctx * shard, -1), dp)
    rest = exchange(rest).reshape(ctx * shard, -1)
    inputs_low = to_ring_order(tokens.reshape(rows, width), places)
    cotangent = to_ring_order(cotangent.reshape(rows, width), places)
    start = jnp.sum((segments[:, None, :] < segments[:, :, None]).astype(jnp.int32), axis=2)[:, None, :]
    tables = rope_tables(length)
    head_gain = head_gains.astype(f32)
    gains = jnp.pad(jnp.concatenate([head_gain, head_gain], axis=1), ((0, 6), (0, 0)))
    first.step()
    first.step()
    rest, start, tables, cotangent = first.hold(rest, start, tables, cotangent)
    inputs_low, rest = tied(inputs_low, rest)
    first.step()
    while first.taken < dp // 2:
        first.step()
    x_far, x_near = to_chips(inputs_low, ctx), ctx_send(inputs_low, 1, ctx)
    rest, x_near = first.hold(rest, x_near)
    rest = Gathering(rest, dp)
    rest.step()
    edges = (0, head_wide, head_wide + hpl, head_wide + hpl + LANES)
    qkv_full, out_own, gains_full = assemble(first.all(), edges)
    gains_full = jnp.transpose(gains_full[:, :2]).astype(f32)

    out_far, out_near = to_chips(out_own, ctx), ctx_send(out_own, 1, ctx)
    c_near = ctx_send(cotangent, 1, ctx)
    x_far, out_far, qkv_full, out_near, c_near = rest.hold(x_far, out_far, qkv_full, out_near, c_near)
    x_far, cotangent = tied(x_far, cotangent)
    rest.step()
    x_all = {0: inputs_low, 1: x_near, **x_far, **from_pairs(x_far, ctx)}
    c_far = to_chips(cotangent, ctx)
    out_full = {0: out_own, 1: out_near, **out_far, **from_pairs(out_far, ctx)}
    hidden_one, proj = project([x_all[k] for k in range(ctx)], gains_full, qkv_full, me, span)

    kept = [attend(proj, start, tables, gains, kvl, n) for n in range(seqs)]
    atts, c_far, out_full = rest.hold([att for att, _ in kept], c_far, out_full)
    rest.step()
    kept = [(att, lse) for att, (_, lse) in zip(atts, kept)]
    parts = jnp.concatenate(atts, axis=0).reshape(seqs, ctx, span, -1)
    parts = [lax.dynamic_index_in_dim(parts, me ^ k, 1, keepdims=False).reshape(rows, -1) for k in range(ctx)]
    parts = [parts[0]] + [ctx_send(parts[k], k, ctx) for k in range(1, ctx)]
    att_rows = jnp.concatenate(parts, axis=1)
    inputs = inputs_low.astype(f32)
    out_full = jnp.concatenate([out_full[k] for k in range(ctx)], axis=1)
    middle = inputs + nt(att_rows, out_full)
    unit_two, scaler_two = rms_parts(middle)
    hidden_two = (unit_two * gains_full[1]).astype(bf16)
    hidden_two, c_far = rest.hold(hidden_two, c_far)
    upstream = {0: cotangent, 1: c_near, **c_far, **from_pairs(c_far, ctx)}
    rest_blocks = rest.all()
    hidden_two = {k: ctx_send(hidden_two, k, ctx) if k else hidden_two for k in [0, 1, *range(2, ctx, 2)]}

    done = {}
    for k in range(0, ctx, 2):
        if k:
            done[0][0], hidden_two[k] = tied(done[0][0], hidden_two[k])
            hidden_two[k + 1] = ctx_send(hidden_two[k], 1, ctx)
        done[k] = list(feed_forward((hidden_two[k], hidden_two[k + 1]), (upstream[k], upstream[k + 1]), rest_blocks, ffp))
    chips = list(range(2, ctx, 2))
    far_two = far_sums({k + n: done[k][1 + n] for k in done for n in (0, 1)}, chips, ctx)
    far_out = far_sums({k + n: done[k][3 + n] for k in done for n in (0, 1)}, chips, ctx)
    two_near = ctx_send(done[0][2], 1, ctx)
    acts, far_two, far_out, two_near = tied([done[k][0] for k in done], far_two, far_out, two_near)
    wide = weight_grads([done[k][5] for k in done], [done[k][6] for k in done], acts)
    two_got = [ctx_send(far_two[k], k, ctx) for k in chips]
    wide, two_got = tied(wide, two_got)
    wide = Summing(wide, dp)
    wide.send()
    d_two = total_of([done[0][1], two_near, *two_got])
    d_middle = cotangent.astype(f32) + norm_back(unit_two, scaler_two, d_two, gains_full[1])
    d_low = d_middle.astype(bf16)
    d_att = nn(d_low, out_full).astype(bf16)
    d_att, d_low = tied([d_att[:, k * hpl : (k + 1) * hpl] for k in range(ctx)], d_low)
    d_att = [d_att[0]] + [ctx_send(d_att[k], k, ctx) for k in range(1, ctx)]
    out_terms = tn(d_low, att_rows).astype(bf16)
    out_terms = {k: out_terms[:, k * hpl : (k + 1) * hpl] for k in range(ctx)}
    (out_terms,) = wide.hold(out_terms)
    wide.add()
    (out_terms,) = wide.hold(out_terms)
    wide.send()
    d_att, out_terms, far_out = tied(d_att, out_terms, far_out)
    out_got = [ctx_send(far_out[k], k, ctx) for k in chips]
    far_terms = far_sums(out_terms, chips, ctx)

    def back(n):
        blocks = jnp.stack(d_att).reshape(ctx, seqs, span, -1)[:, n]
        blocks = [lax.dynamic_index_in_dim(blocks, me ^ c, 0, keepdims=False) for c in range(ctx)]
        grads = jnp.concatenate(blocks, axis=0)[None]
        return list(attend_back(proj, start, tables, gains, *kept[n], grads, kvl, n))

    backs = [back(0)]
    backs[0], far_terms = wide.hold(backs[0], far_terms)
    wide.add()
    d_att, out_got = wide.hold(d_att, out_got)
    wide.send()
    terms_got = group_parts(out_terms, ctx, far_terms)
    out_near = ctx_send(done[0][4], 1, ctx)
    backs.extend(back(n) for n in range(1, seqs))
    backs[1:], terms_got, out_near = wide.hold(backs[1:], terms_got, out_near)
    wide.add()
    (backs,) = wide.hold(backs)
    wide.send()

    d_proj = jnp.concatenate([part[0] for part in backs], axis=0).reshape(seqs * length, -1)
    d_one = nt(d_proj, qkv_full).astype(bf16).reshape(seqs, ctx, span, width)
    d_one = [lax.dynamic_index_in_dim(d_one, me ^ k, 1, keepdims=False).reshape(rows, width) for k in range(ctx)]
    far_one = far_sums(d_one, chips, ctx)
    d_proj, far_one = tied(d_proj, far_one)
    d_one = group_parts(d_one, ctx, far_one)
    out_terms = total_of(terms_got).astype(bf16)
    last, heads = tied(tn(hidden_one, d_proj).astype(bf16), sum(part[1][0] for part in backs))
    (last,) = wide.hold(last)
    last = Summing(jnp.concatenate([last, out_terms], axis=1), dp)
    last.send()
    head_terms = sum_everywhere(heads, dp * ctx)
    output = finish(finish_kernel, places, [middle, done[0][3], out_near, *out_got], bf16)
    output, d_middle = tied(output, d_middle)
    input_grad = finish(input_grad_kernel, places, [d_middle, inputs_low, gains_full] + d_one, f32)
    last.add()
    last.send()
    (input_grad,) = last.hold(input_grad)
    last.add()
    last.send()
    wide = wide.total().astype(bf16)
    wide = exchange(wide.reshape(ctx, shard, -1))
    while last.taken < dp // 2:
        last.add()
        last.send()
    wide, head_terms = last.hold(wide, head_terms)
    last = last.add()
    head_terms = head_terms[:2]

    wide = wide.astype(f32)
    gate_grad = merge_columns(wide[:, :, :ffp], ffl)
    up_grad = merge_columns(wide[:, :, ffp : 2 * ffp], ffl)
    down_grad = merge_columns(wide[:, :, 2 * ffp :], ffl)
    last = exchange(last.astype(bf16).reshape(ctx, shard, -1)).astype(f32)
    qkv_grad = merge_heads(last[:, :, :head_wide])
    out_grad = merge_columns(last[:, :, head_wide:], hpl)

    own_gain = norm_gains.astype(f32)
    norm_one = jnp.sum(qkv_weight.astype(f32) * qkv_grad, axis=1) / own_gain[0]
    norm_two = jnp.sum(gate_weight.astype(f32) * gate_grad + up_weight.astype(f32) * up_grad, axis=1) / own_gain[1]
    head_grad = head_terms[:, :HEAD] + head_terms[:, HEAD:]
    return (
        output.reshape(seqs, span, width),
        input_grad.reshape(seqs, span, width),
        qkv_grad,
        jnp.transpose(out_grad),
        gate_grad,
        up_grad,
        jnp.transpose(down_grad),
        jnp.stack([norm_one, norm_two]),
        head_grad,
    )


def solution(mesh):
    both = ("dp", "ctx")
    in_specs = (
        P("dp", "ctx", None),
        P("dp", None),
        P(both, None),
        P(None, both),
        P(both, None),
        P(both, None),
        P(None, both),
        P(None, both),
        P(),
        P("dp", "ctx", None),
    )
    out_specs = (
        P("dp", "ctx", None),
        P("dp", "ctx", None),
        P(both, None),
        P(None, both),
        P(both, None),
        P(both, None),
        P(None, both),
        P(None, both),
        P(),
    )
    body = functools.partial(local, mesh.shape["dp"], mesh.shape["ctx"])
    return jax.shard_map(body, mesh=mesh, in_specs=in_specs, out_specs=out_specs, check_vma=False)
```

```python
import functools
import math

import jax
import jax.numpy as jnp
from jax import lax
from jax.experimental import pallas as pl
from jax.experimental.pallas import tpu as pltpu
from jax.sharding import PartitionSpec as P

HEADS = 16
KV_HEADS = 8
HEAD = 64
LANES = 128
BLOCK = 256

epsilon = 1e-05
rope_base = 1000000.0


def lanes_of(rows):
    return lax.broadcasted_iota(jnp.int32, (rows, LANES), 1)


def swap_halves(pair):
    lane = lanes_of(pair.shape[0])
    return jnp.where((lane & 32) == 0, pltpu.roll(pair, 96, 1), pltpu.roll(pair, 32, 1))


def flip(pair):
    return pltpu.roll(pair, 64, 1)


def head_sum(pair):
    low = lanes_of(pair.shape[0]) < HEAD
    first = jnp.sum(jnp.where(low, pair, 0.0), axis=1, keepdims=True)
    second = jnp.sum(jnp.where(low, 0.0, pair), axis=1, keepdims=True)
    return jnp.where(low, first, second)


def unit_of(pair):
    scaler = lax.rsqrt(head_sum(pair * pair) * (1.0 / HEAD) + epsilon)
    return pair * scaler, scaler


def roped(unit, gain, cosine, sine):
    scaled = unit * gain
    return scaled * cosine + swap_halves(scaled) * sine


def aligned(pair, side):
    return (pair, flip(pair)) if side == 0 else (flip(pair), pair)


def joined(first, second, side):
    low = lanes_of(first.shape[0]) < HEAD
    if side == 0:
        return jnp.where(low, first, flip(second))
    return jnp.where(low, flip(first), second)


def own_lanes(rows, side):
    lane = lanes_of(rows)
    return (lane < HEAD) if side == 0 else (lane >= HEAD)


def nt(left, right):
    return lax.dot_general(left, right, (((1,), (1,)), ((), ())), preferred_element_type=jnp.float32)


def nn(left, right):
    return jnp.dot(left, right, preferred_element_type=jnp.float32)


def put_keys(proj_ref, cosine, sine, gain, kvl, key_s, val_s, turned_s, want_units):
    rows = proj_ref.shape[1]
    pairs = (kvl + 1) // 2
    lane = lanes_of(rows)
    for g in range(kvl):
        side, at = g % 2, g // 2
        free = HEAD * (1 - side)
        ones = jnp.where((lane >= free) & (lane < free + 3), 1.0, 0.0)
        own = own_lanes(rows, side)
        k0 = (kvl + at) * LANES
        unit, _ = unit_of(proj_ref[0, :, k0 : k0 + LANES])
        keys = roped(unit, gain, cosine, sine)
        keys = jnp.where(own, keys, ones)
        key_s[g] = keys.astype(jnp.bfloat16)
        v0 = (kvl + pairs + at) * LANES
        values = jnp.where(own, proj_ref[0, :, v0 : v0 + LANES], ones)
        val_s[g] = values.astype(jnp.bfloat16)
        turned = keys if want_units else values
        turned_s[g] = jnp.transpose(turned).astype(jnp.bfloat16)


def allowed_here(start_row, i, j):
    shape = (BLOCK, 2 * BLOCK)
    key = lax.broadcasted_iota(jnp.int32, shape, 0)
    allowed = key + j * BLOCK >= start_row
    if i == j:
        allowed = allowed & (key <= (lax.broadcasted_iota(jnp.int32, shape, 1) & (BLOCK - 1)))
    return allowed


def attend_kernel(kvl, proj_ref, start_ref, cos_ref, sin_ref, gain_ref, out_ref, lse_ref, key_s, val_s, turned_s):
    rows = proj_ref.shape[1]
    cosine, sine = cos_ref[...], sin_ref[...]
    put_keys(proj_ref, cosine, sine, gain_ref[1:2, :], kvl, key_s, val_s, turned_s, False)
    for g in range(kvl):
        side = g % 2
        free = HEAD * (1 - side)
        own = own_lanes(BLOCK, side)
        for i in range(rows // BLOCK):
            r = slice(i * BLOCK, (i + 1) * BLOCK)
            unit, _ = unit_of(proj_ref[0, r, g * LANES : (g + 1) * LANES])
            pair = roped(unit, gain_ref[0:1, :], cosine[r], sine[r]) * (HEAD**-0.5)
            stack = jnp.concatenate([jnp.where(own, part, 0.0) for part in aligned(pair, side)], axis=0)
            stack = stack.astype(jnp.bfloat16)
            start_row = start_ref[0, :, r]
            start_row = jnp.concatenate([start_row, start_row], axis=1)
            total = jnp.zeros((LANES, 2 * BLOCK), jnp.float32)
            for j in range(i + 1):
                c = slice(j * BLOCK, (j + 1) * BLOCK)
                scores = nt(key_s[g, c, :], stack)
                weight = jnp.where(allowed_here(start_row, i, j), jnp.exp(scores), 0.0)
                total = total + nn(turned_s[g, :, c], weight.astype(jnp.bfloat16))
            total = jnp.transpose(total)
            first, second = total[:BLOCK], total[BLOCK:]
            mass_one, mass_two = first[:, free : free + 1], second[:, free : free + 1]
            out_ref[0, r, g * LANES : (g + 1) * LANES] = joined(
                first / mass_one, second / mass_two, side
            ).astype(out_ref.dtype)
            low = lanes_of(BLOCK) < HEAD
            lse_ref[0, r, g * LANES : (g + 1) * LANES] = jnp.log(jnp.where(low, mass_one, mass_two))


def pieces(value):
    high = value.astype(jnp.bfloat16).astype(jnp.float32)
    middle = (value - high).astype(jnp.bfloat16).astype(jnp.float32)
    return high, middle, value - high - middle


def stacked(pair, row_term, side):
    lane = lanes_of(pair.shape[0])
    own = own_lanes(pair.shape[0], side)
    free = HEAD * (1 - side)
    parts = []
    for value, term in zip(aligned(pair, side), aligned(-row_term, 1 - side)):
        high, middle, rest = pieces(term)
        extra = jnp.where(lane == free, high, jnp.where(lane == free + 1, middle, jnp.where(lane == free + 2, rest, 0.0)))
        parts.append(jnp.where(own, value, extra))
    return jnp.concatenate(parts, axis=0).astype(jnp.bfloat16)


def attend_back_kernel(
    kvl, proj_ref, start_ref, cos_ref, sin_ref, gain_ref, att_ref, lse_ref, datt_ref,
    dproj_ref, head_ref, key_s, val_s, turned_s, dk_s, dv_s,
):
    rows = proj_ref.shape[1]
    pairs = (kvl + 1) // 2
    cosine, sine = cos_ref[...], sin_ref[...]
    put_keys(proj_ref, cosine, sine, gain_ref[1:2, :], kvl, key_s, val_s, turned_s, True)
    dk_s[...] = jnp.zeros(dk_s.shape, jnp.float32)
    dv_s[...] = jnp.zeros(dv_s.shape, jnp.float32)
    query_terms = jnp.zeros((1, LANES), jnp.float32)
    for g in range(kvl):
        side = g % 2
        for i in range(rows // BLOCK):
            r = slice(i * BLOCK, (i + 1) * BLOCK)
            cols = slice(g * LANES, (g + 1) * LANES)
            unit, scaler = unit_of(proj_ref[0, r, cols])
            gain = gain_ref[0:1, :]
            pair = roped(unit, gain, cosine[r], sine[r]) * (HEAD**-0.5)
            d_att = datt_ref[0, r, cols].astype(jnp.float32)
            delta = head_sum(d_att * att_ref[0, r, cols].astype(jnp.float32))
            query_stack = stacked(pair, lse_ref[0, r, cols], side)
            datt_stack = stacked(d_att, delta, side)
            start_row = start_ref[0, :, r]
            start_row = jnp.concatenate([start_row, start_row], axis=1)
            total = jnp.zeros((LANES, 2 * BLOCK), jnp.float32)
            for j in range(i + 1):
                c = slice(j * BLOCK, (j + 1) * BLOCK)
                scores = nt(key_s[g, c, :], query_stack)
                weight = jnp.where(allowed_here(start_row, i, j), jnp.exp(scores), 0.0)
                d_scores = (weight * nt(val_s[g, c, :], datt_stack)).astype(jnp.bfloat16)
                dv_s[g, c, :] += nn(weight.astype(jnp.bfloat16), datt_stack)
                dk_s[g, c, :] += nn(d_scores, query_stack)
                total = total + nn(turned_s[g, :, c], d_scores)
            total = jnp.transpose(total)
            d_pair = joined(total[:BLOCK], total[BLOCK:], side) * (HEAD**-0.5)
            d_unit = d_pair * cosine[r] - swap_halves(d_pair) * sine[r]
            query_terms = query_terms + jnp.sum(d_unit * unit, axis=0, keepdims=True)
            scaled = d_unit * gain
            inner = head_sum(scaled * unit) * (1.0 / HEAD)
            dproj_ref[0, r, cols] = (scaler * (scaled - unit * inner)).astype(dproj_ref.dtype)
    key_terms = jnp.zeros((1, LANES), jnp.float32)
    low = lanes_of(rows) < HEAD
    for at in range(pairs):
        first, second = 2 * at, 2 * at + 1
        k0, v0 = (kvl + at) * LANES, (kvl + pairs + at) * LANES
        d_keys, d_values = jnp.where(low, dk_s[first], 0.0), jnp.where(low, dv_s[first], 0.0)
        if second < kvl:
            d_keys = jnp.where(low, d_keys, dk_s[second])
            d_values = jnp.where(low, d_values, dv_s[second])
        gain = gain_ref[1:2, :]
        unit, scaler = unit_of(proj_ref[0, :, k0 : k0 + LANES])
        d_unit = d_keys * cosine - swap_halves(d_keys) * sine
        key_terms = key_terms + jnp.sum(d_unit * unit, axis=0, keepdims=True)
        scaled = d_unit * gain
        inner = head_sum(scaled * unit) * (1.0 / HEAD)
        dproj_ref[0, :, k0 : k0 + LANES] = (scaler * (scaled - unit * inner)).astype(dproj_ref.dtype)
        dproj_ref[0, :, v0 : v0 + LANES] = d_values.astype(dproj_ref.dtype)
    head_ref[0] = jnp.concatenate([query_terms, key_terms, jnp.zeros((6, LANES), jnp.float32)], axis=0)


def whole_seq(*shape, at=0):
    return pl.BlockSpec((1,) + shape, lambda s: (s + at, 0, 0))


def shared(*shape):
    return pl.BlockSpec(shape, lambda s: (0, 0))


def slight():
    return pl.CostEstimate(flops=1, bytes_accessed=1, transcendentals=0)


def attend(proj, start, tables, gains, kvl, at):
    _, rows, width = proj.shape
    here = functools.partial(whole_seq, at=at)
    return pl.pallas_call(
        functools.partial(attend_kernel, kvl),
        grid=(1,),
        in_specs=[
            here(rows, width), here(1, rows), shared(rows, LANES), shared(rows, LANES), shared(8, LANES),
        ],
        out_specs=[whole_seq(rows, kvl * LANES), whole_seq(rows, kvl * LANES)],
        out_shape=[
            jax.ShapeDtypeStruct((1, rows, kvl * LANES), jnp.bfloat16),
            jax.ShapeDtypeStruct((1, rows, kvl * LANES), jnp.float32),
        ],
        scratch_shapes=[
            pltpu.VMEM((kvl, rows, LANES), jnp.bfloat16),
            pltpu.VMEM((kvl, rows, LANES), jnp.bfloat16),
            pltpu.VMEM((kvl, LANES, rows), jnp.bfloat16),
        ],
        compiler_params=pltpu.CompilerParams(vmem_limit_bytes=48 << 20),
        cost_estimate=slight(),
    )(proj, start, *tables, gains)


def attend_back(proj, start, tables, gains, att, lse, d_att, kvl, at):
    _, rows, width = proj.shape
    here = functools.partial(whole_seq, at=at)
    return pl.pallas_call(
        functools.partial(attend_back_kernel, kvl),
        grid=(1,),
        in_specs=[
            here(rows, width), here(1, rows), shared(rows, LANES), shared(rows, LANES), shared(8, LANES),
            whole_seq(rows, kvl * LANES), whole_seq(rows, kvl * LANES), whole_seq(rows, kvl * LANES),
        ],
        out_specs=[whole_seq(rows, width), whole_seq(8, LANES)],
        out_shape=[
            jax.ShapeDtypeStruct((1, rows, width), jnp.bfloat16),
            jax.ShapeDtypeStruct((1, 8, LANES), jnp.float32),
        ],
        scratch_shapes=[
            pltpu.VMEM((kvl, rows, LANES), jnp.bfloat16),
            pltpu.VMEM((kvl, rows, LANES), jnp.bfloat16),
            pltpu.VMEM((kvl, LANES, rows), jnp.bfloat16),
            pltpu.VMEM((kvl, rows, LANES), jnp.float32),
            pltpu.VMEM((kvl, rows, LANES), jnp.float32),
        ],
        compiler_params=pltpu.CompilerParams(vmem_limit_bytes=48 << 20),
        cost_estimate=slight(),
    )(proj, start, *tables, gains, att, lse, d_att)


def ffn_kernel(near_tiles, count, *refs):
    near_h, far_h, near_c, far_c = refs[:4]
    blocks = refs[4 : 4 + count]
    acts, near_d, far_d, near_o, far_o, turned_h, turned_c = refs[4 + count : 11 + count]
    weights, sems = refs[11 + count :]
    wide = weights.shape[1] // 3
    step = pl.program_id(0)

    def copies(which):
        return column_copies(blocks, which * wide, (which + 1) * wide, weights, sems.at[which])

    @pl.when(step == 0)
    def _():
        for which in range(3):
            for copy in copies(which):
                copy.start()

    def ready(which):
        @pl.when(step == 0)
        def _():
            for copy in copies(which):
                copy.wait()

    near = step < near_tiles
    hidden = jnp.where(near, near_h[...], far_h[...])
    upstream = jnp.where(near, near_c[...], far_c[...])
    ready(0)
    gate_w = weights[:, :wide]
    gate = nn(hidden, gate_w)
    ready(1)
    up_w = weights[:, wide : 2 * wide]
    up = nn(hidden, up_w)
    ready(2)
    down_w = weights[:, 2 * wide :]
    d_inner = nn(upstream, down_w)
    sigmoid = 1.0 / (1.0 + jnp.exp(-gate))
    silu = gate * sigmoid
    inner = (silu * up).astype(jnp.bfloat16)
    d_gate = (d_inner * up * (sigmoid * (1.0 + gate * (1.0 - sigmoid)))).astype(jnp.bfloat16)
    d_up = (d_inner * silu).astype(jnp.bfloat16)
    turned_h[...] = jnp.transpose(hidden)
    turned_c[...] = jnp.transpose(upstream)
    acts[0] = d_gate
    acts[1] = d_up
    acts[2] = inner
    d_hidden = (nt(d_gate, gate_w) + nt(d_up, up_w)).astype(jnp.bfloat16)
    out = nt(inner, down_w).astype(jnp.bfloat16)

    @pl.when(near)
    def _():
        near_d[...] = d_hidden
        near_o[...] = out

    @pl.when(jnp.logical_not(near))
    def _():
        far_d[...] = d_hidden
        far_o[...] = out


def feed_forward(hidden, upstream, blocks, wide):
    rows, width = hidden[0].shape
    tile = min(BLOCK, rows)
    tiles = rows // tile
    near = pl.BlockSpec((tile, width), lambda i: (jnp.minimum(i, tiles - 1), 0))
    far = pl.BlockSpec((tile, width), lambda i: (jnp.maximum(i - tiles, 0), 0))
    thin = pl.BlockSpec((3, tile, wide), lambda i: (0, i, 0))
    turned = pl.BlockSpec((width, tile), lambda i: (0, i))
    low = functools.partial(jax.ShapeDtypeStruct, dtype=jnp.bfloat16)
    return pl.pallas_call(
        functools.partial(ffn_kernel, tiles, len(blocks)),
        grid=(2 * tiles,),
        in_specs=[near, far, near, far] + [pl.BlockSpec(memory_space=pl.ANY)] * len(blocks),
        out_specs=[thin, near, far, near, far, turned, turned],
        out_shape=[low((3, 2 * rows, wide))] + [low((rows, width))] * 4 + [low((width, 2 * rows))] * 2,
        scratch_shapes=[pltpu.VMEM((width, 3 * wide), jnp.bfloat16), pltpu.SemaphoreType.DMA((3, len(blocks)))],
        compiler_params=pltpu.CompilerParams(vmem_limit_bytes=56 << 20),
        cost_estimate=slight(),
    )(*hidden, *upstream, *blocks)


def grad_kernel(count, *refs):
    hidden, upstream, acts, out_ref = refs[:count], refs[count : 2 * count], refs[2 * count : -1], refs[-1]

    def put(left):
        total = nn(left[0][...], acts[0][0])
        for n in range(1, count):
            total = total + nn(left[n][...], acts[n][0])
        out_ref[...] = total.astype(out_ref.dtype)

    @pl.when(pl.program_id(0) < 2)
    def _():
        put(hidden)

    @pl.when(pl.program_id(0) == 2)
    def _():
        put(upstream)


def weight_grads(hidden, upstream, acts):
    count = len(hidden)
    width, rows = hidden[0].shape
    wide = acts[0].shape[2]
    tile = min(2 * BLOCK, width)
    last = width // tile - 1
    early = pl.BlockSpec((tile, rows), lambda w, i: (jnp.where(w < 2, i, last), 0))
    late = pl.BlockSpec((tile, rows), lambda w, i: (jnp.where(w < 2, 0, i), 0))
    return pl.pallas_call(
        functools.partial(grad_kernel, count),
        grid=(3, width // tile),
        in_specs=[early] * count + [late] * count + [pl.BlockSpec((1, rows, wide), lambda w, i: (w, 0, 0))] * count,
        out_specs=pl.BlockSpec((tile, wide), lambda w, i: (i, w)),
        out_shape=jax.ShapeDtypeStruct((width, 3 * wide), jnp.bfloat16),
        compiler_params=pltpu.CompilerParams(vmem_limit_bytes=56 << 20),
        cost_estimate=slight(),
    )(*hidden, *upstream, *acts)


def order_kernel(places_ref, value_ref, out_ref):
    size = places_ref.shape[0]
    wide = value_ref.shape[1] // size
    for k in range(size):
        out_ref[:, k * wide : (k + 1) * wide] = value_ref[:, pl.ds(pl.multiple_of(places_ref[k] * wide, wide), wide)]


def finish_kernel(places_ref, base_ref, *refs):
    out_ref = refs[-1]
    total = base_ref[...]
    for part in refs[:-1]:
        total = total + part[...].astype(jnp.float32)
    put_back(places_ref, total, out_ref)


def put_back(places_ref, total, out_ref):
    size = places_ref.shape[0]
    wide = total.shape[1] // size
    for k in range(size):
        at = pl.multiple_of(places_ref[k] * wide, wide)
        out_ref[:, pl.ds(at, wide)] = total[:, k * wide : (k + 1) * wide].astype(out_ref.dtype)


def input_grad_kernel(places_ref, base_ref, inputs_ref, gain_ref, *refs):
    out_ref = refs[-1]
    upstream = refs[0][...].astype(jnp.float32)
    for part in refs[1:-1]:
        upstream = upstream + part[...].astype(jnp.float32)
    normed, scaler = rms_parts(inputs_ref[...].astype(jnp.float32))
    put_back(places_ref, base_ref[...] + norm_back(normed, scaler, upstream, gain_ref[0:1, :]), out_ref)


def column_copies(blocks, first, last, target, sems, origin=0):
    rows = blocks[0].shape[0]
    columns = max(block.shape[1] for block in blocks)
    made, row, column = [], 0, 0
    for n, block in enumerate(blocks):
        low, high = max(first, column), min(last, column + block.shape[1])
        if low < high:
            source = block.at[:, pl.ds(low - column, high - low)]
            place = target.at[pl.ds(row, rows), pl.ds(low - origin, high - low)]
            made.append(pltpu.make_async_copy(source, place, sems.at[n]))
        column += block.shape[1]
        if column == columns:
            row, column = row + rows, 0
    return made


def assemble_kernel(count, edges, *refs):
    blocks, outs = refs[:count], refs[count:]
    rows, columns = blocks[0].shape[0], max(block.shape[1] for block in blocks)
    row, column = 0, 0
    for block in blocks:
        for out, first, last in zip(outs, edges, edges[1:]):
            low, high = max(first, column), min(last, column + block.shape[1])
            if low < high:
                out[row : row + rows, low - first : high - first] = block[:, low - column : high - column]
        column += block.shape[1]
        if column == columns:
            row, column = row + rows, 0


def assemble(blocks, edges):
    rows = blocks[0].shape[0] * (len(blocks) - 1)
    return pl.pallas_call(
        functools.partial(assemble_kernel, len(blocks), edges),
        out_shape=[
            jax.ShapeDtypeStruct((rows, last - first), blocks[0].dtype) for first, last in zip(edges, edges[1:])
        ],
        compiler_params=pltpu.CompilerParams(vmem_limit_bytes=48 << 20),
        cost_estimate=pl.CostEstimate(flops=0, bytes_accessed=4 * rows * edges[-1], transcendentals=0),
    )(*blocks)


def project_kernel(count, me_ref, gain_ref, weight_ref, *refs):
    blocks, hidden_ref, proj_ref = refs[:count], refs[-2], refs[-1]
    which = me_ref[0] ^ pl.program_id(0)
    value = blocks[0][...]
    for k in range(1, count):
        value = jnp.where(which == k, blocks[k][...], value)
    hidden = (rms_parts(value.astype(jnp.float32))[0] * gain_ref[0:1, :]).astype(jnp.bfloat16)
    hidden_ref[...] = hidden.reshape(hidden_ref.shape)
    proj_ref[...] = nn(hidden, weight_ref[...]).reshape(proj_ref.shape)


def project(blocks, gains, weight, me, span):
    rows, width = blocks[0].shape
    count, seqs, columns = len(blocks), rows // span, weight.shape[1]

    def held(value):
        return pl.BlockSpec(value.shape, lambda c, _: (0, 0))

    return pl.pallas_call(
        functools.partial(project_kernel, count),
        grid_spec=pltpu.PrefetchScalarGridSpec(
            num_scalar_prefetch=1,
            grid=(count,),
            in_specs=[held(value) for value in (gains, weight, *blocks)],
            out_specs=[
                pl.BlockSpec((seqs, span, width), lambda c, _: (0, c, 0)),
                pl.BlockSpec((seqs, span, columns), lambda c, _: (0, c, 0)),
            ],
        ),
        out_shape=[
            jax.ShapeDtypeStruct((seqs, count * span, width), jnp.bfloat16),
            jax.ShapeDtypeStruct((seqs, count * span, columns), jnp.float32),
        ],
        compiler_params=pltpu.CompilerParams(vmem_limit_bytes=48 << 20),
        cost_estimate=slight(),
    )(me.reshape(1).astype(jnp.int32), gains, weight, *blocks)


def by_rows(kernel, places, operands, dtype):
    rows, width = operands[0].shape
    tile = min(512 if kernel is order_kernel else 256, rows)
    if width // places.shape[0] % LANES != 0:
        return None

    def spec(shape):
        if shape[0] == rows:
            return pl.BlockSpec((tile, shape[1]), lambda i, places: (i, 0))
        return pl.BlockSpec(shape, lambda i, places: (0, 0))

    return pl.pallas_call(
        kernel,
        grid_spec=pltpu.PrefetchScalarGridSpec(
            num_scalar_prefetch=1,
            grid=(rows // tile,),
            in_specs=[spec(value.shape) for value in operands],
            out_specs=spec((rows, width)),
        ),
        out_shape=jax.ShapeDtypeStruct((rows, width), dtype),
        compiler_params=pltpu.CompilerParams(vmem_limit_bytes=48 << 20),
        cost_estimate=slight(),
    )(places, *operands)


def tied(*values):
    return lax.optimization_barrier(values)


def ring_of(size):
    return list(range(0, size, 2)) + list(range(size - 1, 0, -2))


def ring_step(value, size, way):
    order = ring_of(size)
    return lax.ppermute(value, "dp", [(order[i], order[(i + way) % size]) for i in range(size)])


def ring_places(size):
    order = ring_of(size)
    place = {d: i for i, d in enumerate(order)}
    table = [[order[(place[d] + k) % size] for k in range(size)] for d in range(size)]
    return jnp.array(table, jnp.int32)[lax.axis_index("dp")]


def to_ring_order(value, places):
    ordered = by_rows(order_kernel, places, [value], value.dtype)
    if ordered is not None:
        return ordered
    size = places.shape[0]
    return value.reshape(value.shape[0], size, -1)[:, places].reshape(value.shape)


def from_ring_order(value, places):
    size = places.shape[0]
    back = jnp.zeros((size,), jnp.int32).at[places].set(jnp.arange(size, dtype=jnp.int32))
    return value.reshape(value.shape[0], size, -1)[:, back].reshape(value.shape)


def finish(kernel, places, operands, dtype):
    done = by_rows(kernel, places, operands, dtype)
    if done is not None:
        return done
    if kernel is finish_kernel:
        total = operands[0] + total_of(operands[1:])
    else:
        normed, scaler = rms_parts(operands[1].astype(jnp.float32))
        total = operands[0] + norm_back(normed, scaler, total_of(operands[3:]), operands[2][0])
    return from_ring_order(total.astype(dtype), places)


class Gathering:
    def __init__(self, block, size):
        self.size, self.taken, self.columns = size, 0, block.shape[1]
        self.blocks = {0: block}
        self.up = self.down = block

    def step(self):
        self.taken += 1
        if self.taken < self.size // 2:
            self.up, self.down = ring_step(self.up, self.size, 1), ring_step(self.down, self.size, -1)
        else:
            half = self.columns // 2 // LANES * LANES
            self.up = ring_step(self.up[:, :half], self.size, 1)
            self.down = ring_step(self.down[:, half:], self.size, -1)
        self.keep()

    def keep(self):
        if self.taken < self.size // 2:
            self.blocks[self.size - self.taken], self.blocks[self.taken] = self.up, self.down
        else:
            self.blocks[self.taken] = (self.up, self.down)

    def hold(self, *others):
        self.up, self.down, *others = tied(self.up, self.down, *others)
        self.keep()
        return others

    def all(self):
        while self.taken < self.size // 2:
            self.step()
        whole = []
        for k in range(self.size):
            whole.extend(self.blocks[k] if k == self.size // 2 else [self.blocks[k]])
        return whole


class Summing:
    def __init__(self, terms, size):
        self.terms, self.size, self.taken = terms, size, 0
        self.rows, self.columns = terms.shape[0] // size, terms.shape[1]
        self.up = self.down = None

    def part(self, k):
        k = k % self.size
        return self.terms[k * self.rows : (k + 1) * self.rows]

    def send(self):
        self.taken += 1
        if self.taken == 1:
            half = self.columns // 2 // LANES * LANES
            far = self.part(self.size // 2)
            self.up, self.down = far[:, :half], far[:, half:]
        self.up, self.down = ring_step(self.up, self.size, 1), ring_step(self.down, self.size, -1)

    def hold(self, *others):
        self.up, self.down, *others = tied(self.up, self.down, *others)
        return others

    def add(self):
        f32 = jnp.float32
        up, down = self.up.astype(f32), self.down.astype(f32)
        if self.taken == 1:
            up = jnp.pad(up, ((0, 0), (0, self.columns - up.shape[1])))
            down = jnp.pad(down, ((0, 0), (self.columns - down.shape[1], 0)))
        k = self.size // 2 - self.taken
        if k == 0:
            return up + down + self.part(0).astype(f32)
        low = self.terms.dtype
        self.up, self.down = (up + self.part(k).astype(f32)).astype(low), (down + self.part(-k).astype(f32)).astype(low)

    def total(self):
        while self.taken < self.size // 2 - 1:
            self.send()
            self.add()
        if self.taken < self.size // 2:
            self.send()
        return self.add()


def sum_everywhere(value, size):
    sent = jnp.broadcast_to(value[None], (size,) + value.shape)
    return jnp.sum(lax.all_to_all(sent, ("dp", "ctx"), 0, 0, tiled=True), axis=0)


def ctx_send(value, k, size):
    return lax.ppermute(value, "ctx", [(i, i ^ k) for i in range(size)])


def to_chips(block, size):
    return {k: ctx_send(block, k, size) for k in range(2, size, 2)}


def from_pairs(far, size):
    return {k + 1: ctx_send(far[k], 1, size) for k in far}


def far_sums(blocks, chips, size):
    return {
        k: (blocks[k].astype(jnp.float32) + ctx_send(blocks[k + 1], 1, size).astype(jnp.float32)).astype(jnp.bfloat16)
        for k in chips
    }


def group_parts(blocks, size, far=None):
    far = far_sums(blocks, range(2, size, 2), size) if far is None else far
    return [blocks[0], ctx_send(blocks[1], 1, size)] + [ctx_send(far[k], k, size) for k in far]


def total_of(parts):
    total = parts[0].astype(jnp.float32)
    for part in parts[1:]:
        total = total + part.astype(jnp.float32)
    return total


def exchange(blocks):
    return lax.all_to_all(blocks, "ctx", 0, 0, tiled=True)


def rms_parts(values):
    scaler = lax.rsqrt(jnp.mean(values * values, axis=-1, keepdims=True) + epsilon)
    return values * scaler, scaler


def norm_back(normed, scaler, upstream, gain):
    scaled = upstream * gain
    return scaler * (scaled - normed * jnp.mean(scaled * normed, axis=-1, keepdims=True))


def tn(left, right):
    return lax.dot_general(left, right, (((0,), (0,)), ((), ())), preferred_element_type=jnp.float32)


def rope_tables(length):
    frequency = jnp.exp(jnp.arange(HEAD // 2, dtype=jnp.float32) * (-2.0 * math.log(rope_base) / HEAD))
    angles = jnp.arange(length, dtype=jnp.float32)[:, None] * frequency[None, :]
    cosine, sine = jnp.cos(angles), jnp.sin(angles)
    return (
        jnp.concatenate([cosine] * 4, axis=1),
        jnp.concatenate([-sine, sine, -sine, sine], axis=1),
    )


def split_heads(matrix, ctx):
    rows = matrix.shape[0]
    kvl = KV_HEADS // ctx
    pad = kvl % 2 * HEAD
    query, key, value = jnp.split(matrix, [HEADS * HEAD, (HEADS + KV_HEADS) * HEAD], axis=1)
    parts = [
        query.reshape(rows, ctx, -1),
        jnp.pad(key.reshape(rows, ctx, -1), ((0, 0), (0, 0), (0, pad))),
        jnp.pad(value.reshape(rows, ctx, -1), ((0, 0), (0, 0), (0, pad))),
    ]
    return jnp.concatenate(parts, axis=2).transpose(1, 0, 2)


def merge_heads(parts):
    ctx, rows, _ = parts.shape
    kvl = KV_HEADS // ctx
    wide = (kvl + 1) // 2 * LANES
    query = parts[:, :, : kvl * LANES]
    key = parts[:, :, kvl * LANES : kvl * LANES + kvl * HEAD]
    value = parts[:, :, kvl * LANES + wide : kvl * LANES + wide + kvl * HEAD]
    return jnp.concatenate([part.transpose(1, 0, 2).reshape(rows, -1) for part in (query, key, value)], axis=1)


def split_columns(matrix, ctx, wide):
    parts = matrix.reshape(matrix.shape[0], ctx, -1).transpose(1, 0, 2)
    return jnp.pad(parts, ((0, 0), (0, 0), (0, wide - parts.shape[2])))


def merge_columns(parts, keep):
    return parts[:, :, :keep].transpose(1, 0, 2).reshape(parts.shape[1], -1)


def local(
    dp, ctx, tokens, segments, qkv_weight, out_weight, gate_weight, up_weight, down_weight,
    norm_gains, head_gains, cotangent,
):
    seqs, span, width = tokens.shape
    rows = seqs * span
    length = segments.shape[1]
    kvl = KV_HEADS // ctx
    ffl = gate_weight.shape[1] // ctx
    shard = qkv_weight.shape[0]
    me = lax.axis_index("ctx")
    bf16, f32 = jnp.bfloat16, jnp.float32

    places = ring_places(dp)
    ffp = -(-ffl // LANES) * LANES
    hpl = HEADS * HEAD // ctx
    head_wide = (kvl + 2 * ((kvl + 1) // 2)) * LANES
    gain_rows = jnp.pad(jnp.transpose(norm_gains), ((0, 0), (0, LANES - 2)))
    first = [
        split_heads(qkv_weight, ctx),
        split_columns(jnp.transpose(out_weight), ctx, hpl),
        jnp.broadcast_to(gain_rows[None], (ctx, shard, LANES)),
    ]
    rest = [split_columns(part, ctx, ffp) for part in (gate_weight, up_weight, jnp.transpose(down_weight))]
    first, rest = jnp.concatenate(first, axis=2), jnp.concatenate(rest, axis=2)
    first = Gathering(exchange(first).reshape(ctx * shard, -1), dp)
    rest = exchange(rest).reshape(ctx * shard, -1)
    inputs_low = to_ring_order(tokens.reshape(rows, width), places)
    cotangent = to_ring_order(cotangent.reshape(rows, width), places)
    start = jnp.sum((segments[:, None, :] < segments[:, :, None]).astype(jnp.int32), axis=2)[:, None, :]
    tables = rope_tables(length)
    head_gain = head_gains.astype(f32)
    gains = jnp.pad(jnp.concatenate([head_gain, head_gain], axis=1), ((0, 6), (0, 0)))
    first.step()
    first.step()
    rest, start, tables, cotangent = first.hold(rest, start, tables, cotangent)
    inputs_low, rest = tied(inputs_low, rest)
    first.step()
    while first.taken < dp // 2:
        first.step()
    x_far, x_near = to_chips(inputs_low, ctx), ctx_send(inputs_low, 1, ctx)
    rest, x_near = first.hold(rest, x_near)
    rest = Gathering(rest, dp)
    rest.step()
    edges = (0, head_wide, head_wide + hpl, head_wide + hpl + LANES)
    qkv_full, out_own, gains_full = assemble(first.all(), edges)
    gains_full = jnp.transpose(gains_full[:, :2]).astype(f32)

    out_far, out_near = to_chips(out_own, ctx), ctx_send(out_own, 1, ctx)
    c_near = ctx_send(cotangent, 1, ctx)
    x_far, out_far, qkv_full, gains_full, c_near, out_near = rest.hold(
        x_far, out_far, qkv_full, gains_full, c_near, out_near
    )
    out_full = {0: out_own, 1: out_near, **out_far, **from_pairs(out_far, ctx)}
    x_far, cotangent = tied(x_far, cotangent)
    rest.step()
    x_all = {0: inputs_low, 1: x_near, **x_far, **from_pairs(x_far, ctx)}
    c_far = to_chips(cotangent, ctx)
    hidden_one, proj = project([x_all[k] for k in range(ctx)], gains_full, qkv_full, me, span)

    kept = [attend(proj, start, tables, gains, kvl, 0)]
    out_full = jnp.concatenate([out_full[k] for k in range(ctx)], axis=1)
    kept[0], proj, out_full = rest.hold(kept[0], proj, out_full)
    rest.step()
    kept.extend(attend(proj, start, tables, gains, kvl, n) for n in range(1, seqs))
    atts, c_far = tied([att for att, _ in kept], c_far)
    kept = [(att, lse) for att, (_, lse) in zip(atts, kept)]
    parts = jnp.concatenate(atts, axis=0).reshape(seqs, ctx, span, -1)
    parts = [lax.dynamic_index_in_dim(parts, me ^ k, 1, keepdims=False).reshape(rows, -1) for k in range(ctx)]
    parts = [parts[0]] + [ctx_send(parts[k], k, ctx) for k in range(1, ctx)]
    (parts,) = rest.hold(parts)
    att_rows = jnp.concatenate(parts, axis=1)
    inputs = inputs_low.astype(f32)
    middle = inputs + nt(att_rows, out_full)
    unit_two, scaler_two = rms_parts(middle)
    hidden_two = (unit_two * gains_full[1]).astype(bf16)
    hidden_two, c_far = tied(hidden_two, c_far)
    upstream = {0: cotangent, 1: c_near, **c_far, **from_pairs(c_far, ctx)}
    rest_blocks = rest.all()
    hidden_two = {k: ctx_send(hidden_two, k, ctx) if k else hidden_two for k in [0, 1, *range(2, ctx, 2)]}

    done = {}
    for k in range(0, ctx, 2):
        if k:
            done[0][0], hidden_two[k] = tied(done[0][0], hidden_two[k])
            hidden_two[k + 1] = ctx_send(hidden_two[k], 1, ctx)
        done[k] = list(feed_forward((hidden_two[k], hidden_two[k + 1]), (upstream[k], upstream[k + 1]), rest_blocks, ffp))
    chips = list(range(2, ctx, 2))
    far_two = far_sums({k + n: done[k][1 + n] for k in done for n in (0, 1)}, chips, ctx)
    two_near = ctx_send(done[0][2], 1, ctx)
    ffn_out = {k + n: done[k][3 + n] for k in done for n in (0, 1)}
    out_hop = {k: ctx_send(ffn_out[k + 1], 1, ctx) for k in chips}
    acts, far_two, two_near, out_hop = tied([done[k][0] for k in done], far_two, two_near, out_hop)
    wide = weight_grads([done[k][5] for k in done], [done[k][6] for k in done], acts)
    two_got = [ctx_send(far_two[k], k, ctx) for k in chips]
    wide, two_got = tied(wide, two_got)
    wide = Summing(wide, dp)
    wide.send()
    d_two = total_of([done[0][1], two_near, *two_got])
    d_middle = cotangent.astype(f32) + norm_back(unit_two, scaler_two, d_two, gains_full[1])
    d_low = d_middle.astype(bf16)
    d_att = nn(d_low, out_full).astype(bf16)
    d_att, d_low = tied([d_att[:, k * hpl : (k + 1) * hpl] for k in range(ctx)], d_low)
    d_att = [d_att[0]] + [ctx_send(d_att[k], k, ctx) for k in range(1, ctx)]
    out_terms = tn(d_low, att_rows).astype(bf16)
    out_terms = {k: out_terms[:, k * hpl : (k + 1) * hpl] for k in range(ctx)}
    (out_terms,) = wide.hold(out_terms)
    wide.add()
    (out_terms,) = wide.hold(out_terms)
    wide.send()
    far_out = {k: total_of([ffn_out[k], out_hop[k]]).astype(bf16) for k in chips}
    d_att, out_terms, far_out, near_out = tied(d_att, out_terms, far_out, ffn_out[1])
    out_got = [ctx_send(far_out[k], k, ctx) for k in chips]
    far_terms = far_sums(out_terms, chips, ctx)
    out_near = ctx_send(near_out, 1, ctx)

    def back(n):
        blocks = jnp.stack(d_att).reshape(ctx, seqs, span, -1)[:, n]
        blocks = [lax.dynamic_index_in_dim(blocks, me ^ c, 0, keepdims=False) for c in range(ctx)]
        grads = jnp.concatenate(blocks, axis=0)[None]
        return list(attend_back(proj, start, tables, gains, *kept[n], grads, kvl, n))

    backs = [back(0)]
    backs[0], far_terms, out_near = wide.hold(backs[0], far_terms, out_near)
    wide.add()
    (d_att,) = wide.hold(d_att)
    wide.send()
    terms_got = group_parts(out_terms, ctx, far_terms)
    backs.extend(back(n) for n in range(1, seqs))
    backs[1:], terms_got, out_got = wide.hold(backs[1:], terms_got, out_got)
    wide.add()
    (backs,) = wide.hold(backs)
    wide.send()

    d_proj = jnp.concatenate([part[0] for part in backs], axis=0).reshape(seqs * length, -1)
    d_one = nt(d_proj, qkv_full).astype(bf16).reshape(seqs, ctx, span, width)
    d_one = [lax.dynamic_index_in_dim(d_one, me ^ k, 1, keepdims=False).reshape(rows, width) for k in range(ctx)]
    far_one = far_sums(d_one, chips, ctx)
    d_proj, far_one = tied(d_proj, far_one)
    d_one = group_parts(d_one, ctx, far_one)
    out_terms = total_of(terms_got).astype(bf16)
    heads = sum(part[1][0] for part in backs)
    last = (tn(hidden_one.reshape(seqs * length, width), d_proj).astype(bf16))
    head_terms = sum_everywhere(heads, dp * ctx)
    last, head_terms = wide.hold(last, head_terms)
    last = Summing(jnp.concatenate([last, out_terms], axis=1), dp)
    last.send()
    output = finish(finish_kernel, places, [middle, done[0][3], out_near, *out_got], bf16)
    output, d_middle = tied(output, d_middle)
    input_grad = finish(input_grad_kernel, places, [d_middle, inputs_low, gains_full] + d_one, f32)
    last.add()
    last.send()
    (input_grad,) = last.hold(input_grad)
    (input_grad,) = wide.hold(input_grad)
    last.add()
    last.send()
    wide = wide.total().astype(bf16)
    wide = exchange(wide.reshape(ctx, shard, -1))
    while last.taken < dp // 2:
        last.hold()
        last.add()
        last.send()
    wide, head_terms = last.hold(wide, head_terms)
    last = last.add()
    head_terms = head_terms[:2]

    wide = wide.astype(f32)
    gate_grad = merge_columns(wide[:, :, :ffp], ffl)
    up_grad = merge_columns(wide[:, :, ffp : 2 * ffp], ffl)
    down_grad = merge_columns(wide[:, :, 2 * ffp :], ffl)
    last = exchange(last.astype(bf16).reshape(ctx, shard, -1)).astype(f32)
    qkv_grad = merge_heads(last[:, :, :head_wide])
    out_grad = merge_columns(last[:, :, head_wide:], hpl)

    own_gain = norm_gains.astype(f32)
    norm_one = jnp.sum(qkv_weight.astype(f32) * qkv_grad, axis=1) / own_gain[0]
    norm_two = jnp.sum(gate_weight.astype(f32) * gate_grad + up_weight.astype(f32) * up_grad, axis=1) / own_gain[1]
    head_grad = head_terms[:, :HEAD] + head_terms[:, HEAD:]
    return (
        output.reshape(seqs, span, width),
        input_grad.reshape(seqs, span, width),
        qkv_grad,
        jnp.transpose(out_grad),
        gate_grad,
        up_grad,
        jnp.transpose(down_grad),
        jnp.stack([norm_one, norm_two]),
        head_grad,
    )


def solution(mesh):
    both = ("dp", "ctx")
    in_specs = (
        P("dp", "ctx", None),
        P("dp", None),
        P(both, None),
        P(None, both),
        P(both, None),
        P(both, None),
        P(None, both),
        P(None, both),
        P(),
        P("dp", "ctx", None),
    )
    out_specs = (
        P("dp", "ctx", None),
        P("dp", "ctx", None),
        P(both, None),
        P(None, both),
        P(both, None),
        P(both, None),
        P(None, both),
        P(None, both),
        P(),
    )
    body = functools.partial(local, mesh.shape["dp"], mesh.shape["ctx"])
    return jax.shard_map(body, mesh=mesh, in_specs=in_specs, out_specs=out_specs, check_vma=False)
```

```python
import functools
import math

import jax
import jax.numpy as jnp
from jax import lax
from jax.experimental import pallas as pl
from jax.experimental.pallas import tpu as pltpu
from jax.sharding import PartitionSpec as P

HEADS = 16
KV_HEADS = 8
HEAD = 64
LANES = 128
BLOCK = 256

epsilon = 1e-05
rope_base = 1000000.0


def lanes_of(rows):
    return lax.broadcasted_iota(jnp.int32, (rows, LANES), 1)


def swap_halves(pair):
    lane = lanes_of(pair.shape[0])
    return jnp.where((lane & 32) == 0, pltpu.roll(pair, 96, 1), pltpu.roll(pair, 32, 1))


def flip(pair):
    return pltpu.roll(pair, 64, 1)


def head_sum(pair):
    low = lanes_of(pair.shape[0]) < HEAD
    first = jnp.sum(jnp.where(low, pair, 0.0), axis=1, keepdims=True)
    second = jnp.sum(jnp.where(low, 0.0, pair), axis=1, keepdims=True)
    return jnp.where(low, first, second)


def unit_of(pair):
    scaler = lax.rsqrt(head_sum(pair * pair) * (1.0 / HEAD) + epsilon)
    return pair * scaler, scaler


def roped(unit, gain, cosine, sine):
    scaled = unit * gain
    return scaled * cosine + swap_halves(scaled) * sine


def aligned(pair, side):
    return (pair, flip(pair)) if side == 0 else (flip(pair), pair)


def joined(first, second, side):
    low = lanes_of(first.shape[0]) < HEAD
    if side == 0:
        return jnp.where(low, first, flip(second))
    return jnp.where(low, flip(first), second)


def own_lanes(rows, side):
    lane = lanes_of(rows)
    return (lane < HEAD) if side == 0 else (lane >= HEAD)


def nt(left, right):
    return lax.dot_general(left, right, (((1,), (1,)), ((), ())), preferred_element_type=jnp.float32)


def nn(left, right):
    return jnp.dot(left, right, preferred_element_type=jnp.float32)


def put_keys(proj_ref, cosine, sine, gain, kvl, key_s, val_s, turned_s, want_units):
    rows = proj_ref.shape[1]
    pairs = (kvl + 1) // 2
    lane = lanes_of(rows)
    for g in range(kvl):
        side, at = g % 2, g // 2
        free = HEAD * (1 - side)
        ones = jnp.where((lane >= free) & (lane < free + 3), 1.0, 0.0)
        own = own_lanes(rows, side)
        k0 = (kvl + at) * LANES
        unit, _ = unit_of(proj_ref[0, :, k0 : k0 + LANES])
        keys = roped(unit, gain, cosine, sine)
        keys = jnp.where(own, keys, ones)
        key_s[g] = keys.astype(jnp.bfloat16)
        v0 = (kvl + pairs + at) * LANES
        values = jnp.where(own, proj_ref[0, :, v0 : v0 + LANES], ones)
        val_s[g] = values.astype(jnp.bfloat16)
        turned = keys if want_units else values
        turned_s[g] = jnp.transpose(turned).astype(jnp.bfloat16)


def allowed_here(start_row, i, j):
    shape = (BLOCK, 2 * BLOCK)
    key = lax.broadcasted_iota(jnp.int32, shape, 0)
    allowed = key + j * BLOCK >= start_row
    if i == j:
        allowed = allowed & (key <= (lax.broadcasted_iota(jnp.int32, shape, 1) & (BLOCK - 1)))
    return allowed


def attend_kernel(kvl, proj_ref, start_ref, cos_ref, sin_ref, gain_ref, out_ref, lse_ref, key_s, val_s, turned_s):
    rows = proj_ref.shape[1]
    cosine, sine = cos_ref[...], sin_ref[...]
    put_keys(proj_ref, cosine, sine, gain_ref[1:2, :], kvl, key_s, val_s, turned_s, False)
    for g in range(kvl):
        side = g % 2
        free = HEAD * (1 - side)
        own = own_lanes(BLOCK, side)
        for i in range(rows // BLOCK):
            r = slice(i * BLOCK, (i + 1) * BLOCK)
            unit, _ = unit_of(proj_ref[0, r, g * LANES : (g + 1) * LANES])
            pair = roped(unit, gain_ref[0:1, :], cosine[r], sine[r]) * (HEAD**-0.5)
            stack = jnp.concatenate([jnp.where(own, part, 0.0) for part in aligned(pair, side)], axis=0)
            stack = stack.astype(jnp.bfloat16)
            start_row = start_ref[0, :, r]
            start_row = jnp.concatenate([start_row, start_row], axis=1)
            total = jnp.zeros((LANES, 2 * BLOCK), jnp.float32)
            for j in range(i + 1):
                c = slice(j * BLOCK, (j + 1) * BLOCK)
                scores = nt(key_s[g, c, :], stack)
                weight = jnp.where(allowed_here(start_row, i, j), jnp.exp(scores), 0.0)
                total = total + nn(turned_s[g, :, c], weight.astype(jnp.bfloat16))
            total = jnp.transpose(total)
            first, second = total[:BLOCK], total[BLOCK:]
            mass_one, mass_two = first[:, free : free + 1], second[:, free : free + 1]
            out_ref[0, r, g * LANES : (g + 1) * LANES] = joined(
                first / mass_one, second / mass_two, side
            ).astype(out_ref.dtype)
            low = lanes_of(BLOCK) < HEAD
            lse_ref[0, r, g * LANES : (g + 1) * LANES] = jnp.log(jnp.where(low, mass_one, mass_two))


def pieces(value):
    high = value.astype(jnp.bfloat16).astype(jnp.float32)
    middle = (value - high).astype(jnp.bfloat16).astype(jnp.float32)
    return high, middle, value - high - middle


def stacked(pair, row_term, side):
    lane = lanes_of(pair.shape[0])
    own = own_lanes(pair.shape[0], side)
    free = HEAD * (1 - side)
    parts = []
    for value, term in zip(aligned(pair, side), aligned(-row_term, 1 - side)):
        high, middle, rest = pieces(term)
        extra = jnp.where(lane == free, high, jnp.where(lane == free + 1, middle, jnp.where(lane == free + 2, rest, 0.0)))
        parts.append(jnp.where(own, value, extra))
    return jnp.concatenate(parts, axis=0).astype(jnp.bfloat16)


def attend_back_kernel(
    kvl, proj_ref, start_ref, cos_ref, sin_ref, gain_ref, att_ref, lse_ref, datt_ref,
    dproj_ref, head_ref, key_s, val_s, turned_s, dk_s, dv_s,
):
    rows = proj_ref.shape[1]
    pairs = (kvl + 1) // 2
    cosine, sine = cos_ref[...], sin_ref[...]
    put_keys(proj_ref, cosine, sine, gain_ref[1:2, :], kvl, key_s, val_s, turned_s, True)
    dk_s[...] = jnp.zeros(dk_s.shape, jnp.float32)
    dv_s[...] = jnp.zeros(dv_s.shape, jnp.float32)
    query_terms = jnp.zeros((1, LANES), jnp.float32)
    for g in range(kvl):
        side = g % 2
        for i in range(rows // BLOCK):
            r = slice(i * BLOCK, (i + 1) * BLOCK)
            cols = slice(g * LANES, (g + 1) * LANES)
            unit, scaler = unit_of(proj_ref[0, r, cols])
            gain = gain_ref[0:1, :]
            pair = roped(unit, gain, cosine[r], sine[r]) * (HEAD**-0.5)
            d_att = datt_ref[0, r, cols].astype(jnp.float32)
            delta = head_sum(d_att * att_ref[0, r, cols].astype(jnp.float32))
            query_stack = stacked(pair, lse_ref[0, r, cols], side)
            datt_stack = stacked(d_att, delta, side)
            start_row = start_ref[0, :, r]
            start_row = jnp.concatenate([start_row, start_row], axis=1)
            total = jnp.zeros((LANES, 2 * BLOCK), jnp.float32)
            for j in range(i + 1):
                c = slice(j * BLOCK, (j + 1) * BLOCK)
                scores = nt(key_s[g, c, :], query_stack)
                weight = jnp.where(allowed_here(start_row, i, j), jnp.exp(scores), 0.0)
                d_scores = (weight * nt(val_s[g, c, :], datt_stack)).astype(jnp.bfloat16)
                dv_s[g, c, :] += nn(weight.astype(jnp.bfloat16), datt_stack)
                dk_s[g, c, :] += nn(d_scores, query_stack)
                total = total + nn(turned_s[g, :, c], d_scores)
            total = jnp.transpose(total)
            d_pair = joined(total[:BLOCK], total[BLOCK:], side) * (HEAD**-0.5)
            d_unit = d_pair * cosine[r] - swap_halves(d_pair) * sine[r]
            query_terms = query_terms + jnp.sum(d_unit * unit, axis=0, keepdims=True)
            scaled = d_unit * gain
            inner = head_sum(scaled * unit) * (1.0 / HEAD)
            dproj_ref[0, r, cols] = (scaler * (scaled - unit * inner)).astype(dproj_ref.dtype)
    key_terms = jnp.zeros((1, LANES), jnp.float32)
    low = lanes_of(rows) < HEAD
    for at in range(pairs):
        first, second = 2 * at, 2 * at + 1
        k0, v0 = (kvl + at) * LANES, (kvl + pairs + at) * LANES
        d_keys, d_values = jnp.where(low, dk_s[first], 0.0), jnp.where(low, dv_s[first], 0.0)
        if second < kvl:
            d_keys = jnp.where(low, d_keys, dk_s[second])
            d_values = jnp.where(low, d_values, dv_s[second])
        gain = gain_ref[1:2, :]
        unit, scaler = unit_of(proj_ref[0, :, k0 : k0 + LANES])
        d_unit = d_keys * cosine - swap_halves(d_keys) * sine
        key_terms = key_terms + jnp.sum(d_unit * unit, axis=0, keepdims=True)
        scaled = d_unit * gain
        inner = head_sum(scaled * unit) * (1.0 / HEAD)
        dproj_ref[0, :, k0 : k0 + LANES] = (scaler * (scaled - unit * inner)).astype(dproj_ref.dtype)
        dproj_ref[0, :, v0 : v0 + LANES] = d_values.astype(dproj_ref.dtype)
    head_ref[0] = jnp.concatenate([query_terms, key_terms, jnp.zeros((6, LANES), jnp.float32)], axis=0)


def whole_seq(*shape, at=0):
    return pl.BlockSpec((1,) + shape, lambda s: (s + at, 0, 0))


def shared(*shape):
    return pl.BlockSpec(shape, lambda s: (0, 0))


def slight():
    return pl.CostEstimate(flops=1, bytes_accessed=1, transcendentals=0)


def attend(proj, start, tables, gains, kvl, at):
    _, rows, width = proj.shape
    here = functools.partial(whole_seq, at=at)
    return pl.pallas_call(
        functools.partial(attend_kernel, kvl),
        grid=(1,),
        in_specs=[
            here(rows, width), here(1, rows), shared(rows, LANES), shared(rows, LANES), shared(8, LANES),
        ],
        out_specs=[whole_seq(rows, kvl * LANES), whole_seq(rows, kvl * LANES)],
        out_shape=[
            jax.ShapeDtypeStruct((1, rows, kvl * LANES), jnp.bfloat16),
            jax.ShapeDtypeStruct((1, rows, kvl * LANES), jnp.float32),
        ],
        scratch_shapes=[
            pltpu.VMEM((kvl, rows, LANES), jnp.bfloat16),
            pltpu.VMEM((kvl, rows, LANES), jnp.bfloat16),
            pltpu.VMEM((kvl, LANES, rows), jnp.bfloat16),
        ],
        compiler_params=pltpu.CompilerParams(vmem_limit_bytes=48 << 20),
        cost_estimate=slight(),
    )(proj, start, *tables, gains)


def attend_back(proj, start, tables, gains, att, lse, d_att, kvl, at):
    _, rows, width = proj.shape
    here = functools.partial(whole_seq, at=at)
    return pl.pallas_call(
        functools.partial(attend_back_kernel, kvl),
        grid=(1,),
        in_specs=[
            here(rows, width), here(1, rows), shared(rows, LANES), shared(rows, LANES), shared(8, LANES),
            whole_seq(rows, kvl * LANES), whole_seq(rows, kvl * LANES), whole_seq(rows, kvl * LANES),
        ],
        out_specs=[whole_seq(rows, width), whole_seq(8, LANES)],
        out_shape=[
            jax.ShapeDtypeStruct((1, rows, width), jnp.bfloat16),
            jax.ShapeDtypeStruct((1, 8, LANES), jnp.float32),
        ],
        scratch_shapes=[
            pltpu.VMEM((kvl, rows, LANES), jnp.bfloat16),
            pltpu.VMEM((kvl, rows, LANES), jnp.bfloat16),
            pltpu.VMEM((kvl, LANES, rows), jnp.bfloat16),
            pltpu.VMEM((kvl, rows, LANES), jnp.float32),
            pltpu.VMEM((kvl, rows, LANES), jnp.float32),
        ],
        compiler_params=pltpu.CompilerParams(vmem_limit_bytes=48 << 20),
        cost_estimate=slight(),
    )(proj, start, *tables, gains, att, lse, d_att)


def ffn_kernel(near_tiles, count, *refs):
    near_h, far_h, near_c, far_c = refs[:4]
    blocks = refs[4 : 4 + count]
    acts, turned_h, turned_c, near_d, far_d, near_o, far_o = refs[-9:-2]
    weights, sems = refs[-2:]
    wide = weights.shape[1] // 3
    step = pl.program_id(0)

    def copies(which):
        return column_copies(blocks, which * wide, (which + 1) * wide, weights, sems.at[which])

    @pl.when(step == 0)
    def _():
        for which in range(3):
            for copy in copies(which):
                copy.start()

    def ready(which):
        @pl.when(step == 0)
        def _():
            for copy in copies(which):
                copy.wait()

    near = step < near_tiles
    hidden = jnp.where(near, near_h[...], far_h[...])
    upstream = jnp.where(near, near_c[...], far_c[...])
    ready(0)
    gate_w = weights[:, :wide]
    gate = nn(hidden, gate_w)
    ready(1)
    up_w = weights[:, wide : 2 * wide]
    up = nn(hidden, up_w)
    ready(2)
    down_w = weights[:, 2 * wide :]
    d_inner = nn(upstream, down_w)
    sigmoid = 1.0 / (1.0 + jnp.exp(-gate))
    silu = gate * sigmoid
    inner = (silu * up).astype(jnp.bfloat16)
    d_gate = (d_inner * up * (sigmoid * (1.0 + gate * (1.0 - sigmoid)))).astype(jnp.bfloat16)
    d_up = (d_inner * silu).astype(jnp.bfloat16)
    turned_h[...] = jnp.transpose(hidden)
    turned_c[...] = jnp.transpose(upstream)
    acts[0] = d_gate
    acts[1] = d_up
    acts[2] = inner
    d_hidden = (nt(d_gate, gate_w) + nt(d_up, up_w)).astype(jnp.bfloat16)
    out = nt(inner, down_w).astype(jnp.bfloat16)

    @pl.when(near)
    def _():
        near_d[...] = d_hidden
        near_o[...] = out

    @pl.when(jnp.logical_not(near))
    def _():
        far_d[...] = d_hidden
        far_o[...] = out


def feed_forward(hidden, upstream, blocks, wide, chip, chips, kept):
    rows, width = hidden[0].shape
    tile = min(BLOCK, rows)
    tiles = rows // tile
    first = chip * 2 * tiles
    near = pl.BlockSpec((tile, width), lambda i: (jnp.minimum(i, tiles - 1), 0))
    far = pl.BlockSpec((tile, width), lambda i: (jnp.maximum(i - tiles, 0), 0))
    thin = pl.BlockSpec((3, tile, wide), lambda i: (0, first + i, 0))
    turned = pl.BlockSpec((width, tile), lambda i: (0, first + i))
    low = functools.partial(jax.ShapeDtypeStruct, dtype=jnp.bfloat16)
    everyone = 2 * rows * chips
    return pl.pallas_call(
        functools.partial(ffn_kernel, tiles, len(blocks)),
        grid=(2 * tiles,),
        in_specs=[near, far, near, far] + [pl.BlockSpec(memory_space=pl.ANY)] * (len(blocks) + len(kept)),
        out_specs=[thin, turned, turned, near, far, near, far],
        out_shape=[low((3, everyone, wide))] + [low((width, everyone))] * 2 + [low((rows, width))] * 4,
        input_output_aliases={4 + len(blocks) + n: n for n in range(len(kept))},
        scratch_shapes=[pltpu.VMEM((width, 3 * wide), jnp.bfloat16), pltpu.SemaphoreType.DMA((3, len(blocks)))],
        compiler_params=pltpu.CompilerParams(vmem_limit_bytes=56 << 20),
        cost_estimate=slight(),
    )(*hidden, *upstream, *blocks, *kept)


def grad_kernel(hidden, upstream, acts, out_ref):
    @pl.when(pl.program_id(0) < 2)
    def _():
        out_ref[...] = nn(hidden[...], acts[0]).astype(out_ref.dtype)

    @pl.when(pl.program_id(0) == 2)
    def _():
        out_ref[...] = nn(upstream[...], acts[0]).astype(out_ref.dtype)


def weight_grads(hidden, upstream, acts):
    width, rows = hidden.shape
    wide = acts.shape[2]
    tile = min(2 * BLOCK, width)
    last = width // tile - 1
    early = pl.BlockSpec((tile, rows), lambda w, i: (jnp.where(w < 2, i, last), 0))
    late = pl.BlockSpec((tile, rows), lambda w, i: (jnp.where(w < 2, 0, i), 0))
    return pl.pallas_call(
        grad_kernel,
        grid=(3, width // tile),
        in_specs=[early, late, pl.BlockSpec((1, rows, wide), lambda w, i: (w, 0, 0))],
        out_specs=pl.BlockSpec((tile, wide), lambda w, i: (i, w)),
        out_shape=jax.ShapeDtypeStruct((width, 3 * wide), jnp.bfloat16),
        compiler_params=pltpu.CompilerParams(vmem_limit_bytes=56 << 20),
        cost_estimate=slight(),
    )(hidden, upstream, acts)


def order_kernel(places_ref, value_ref, out_ref):
    size = places_ref.shape[0]
    wide = value_ref.shape[1] // size
    for k in range(size):
        out_ref[:, k * wide : (k + 1) * wide] = value_ref[:, pl.ds(pl.multiple_of(places_ref[k] * wide, wide), wide)]


def finish_kernel(places_ref, base_ref, *refs):
    out_ref = refs[-1]
    total = base_ref[...]
    for part in refs[:-1]:
        total = total + part[...].astype(jnp.float32)
    put_back(places_ref, total, out_ref)


def put_back(places_ref, total, out_ref):
    size = places_ref.shape[0]
    wide = total.shape[1] // size
    for k in range(size):
        at = pl.multiple_of(places_ref[k] * wide, wide)
        out_ref[:, pl.ds(at, wide)] = total[:, k * wide : (k + 1) * wide].astype(out_ref.dtype)


def input_grad_kernel(places_ref, base_ref, inputs_ref, gain_ref, *refs):
    out_ref = refs[-1]
    upstream = refs[0][...].astype(jnp.float32)
    for part in refs[1:-1]:
        upstream = upstream + part[...].astype(jnp.float32)
    normed, scaler = rms_parts(inputs_ref[...].astype(jnp.float32))
    put_back(places_ref, base_ref[...] + norm_back(normed, scaler, upstream, gain_ref[0:1, :]), out_ref)


def column_copies(blocks, first, last, target, sems, origin=0):
    rows = blocks[0].shape[0]
    columns = max(block.shape[1] for block in blocks)
    made, row, column = [], 0, 0
    for n, block in enumerate(blocks):
        low, high = max(first, column), min(last, column + block.shape[1])
        if low < high:
            source = block.at[:, pl.ds(low - column, high - low)]
            place = target.at[pl.ds(row, rows), pl.ds(low - origin, high - low)]
            made.append(pltpu.make_async_copy(source, place, sems.at[n]))
        column += block.shape[1]
        if column == columns:
            row, column = row + rows, 0
    return made


def assemble_kernel(count, edges, *refs):
    blocks, outs = refs[:count], refs[count:]
    rows, columns = blocks[0].shape[0], max(block.shape[1] for block in blocks)
    row, column = 0, 0
    for block in blocks:
        for out, first, last in zip(outs, edges, edges[1:]):
            low, high = max(first, column), min(last, column + block.shape[1])
            if low < high:
                out[row : row + rows, low - first : high - first] = block[:, low - column : high - column]
        column += block.shape[1]
        if column == columns:
            row, column = row + rows, 0


def assemble(blocks, edges):
    rows = blocks[0].shape[0] * (len(blocks) - 1)
    return pl.pallas_call(
        functools.partial(assemble_kernel, len(blocks), edges),
        out_shape=[
            jax.ShapeDtypeStruct((rows, last - first), blocks[0].dtype) for first, last in zip(edges, edges[1:])
        ],
        compiler_params=pltpu.CompilerParams(vmem_limit_bytes=48 << 20),
        cost_estimate=pl.CostEstimate(flops=0, bytes_accessed=4 * rows * edges[-1], transcendentals=0),
    )(*blocks)


def project_kernel(count, me_ref, gain_ref, weight_ref, *refs):
    blocks, hidden_ref, proj_ref = refs[:count], refs[-2], refs[-1]
    which = me_ref[0] ^ pl.program_id(0)
    value = blocks[0][...]
    for k in range(1, count):
        value = jnp.where(which == k, blocks[k][...], value)
    hidden = (rms_parts(value.astype(jnp.float32))[0] * gain_ref[0:1, :]).astype(jnp.bfloat16)
    hidden_ref[...] = hidden.reshape(hidden_ref.shape)
    proj_ref[...] = nn(hidden, weight_ref[...]).reshape(proj_ref.shape)


def project(blocks, gains, weight, me, span):
    rows, width = blocks[0].shape
    count, seqs, columns = len(blocks), rows // span, weight.shape[1]

    def held(value):
        return pl.BlockSpec(value.shape, lambda c, _: (0, 0))

    return pl.pallas_call(
        functools.partial(project_kernel, count),
        grid_spec=pltpu.PrefetchScalarGridSpec(
            num_scalar_prefetch=1,
            grid=(count,),
            in_specs=[held(value) for value in (gains, weight, *blocks)],
            out_specs=[
                pl.BlockSpec((seqs, span, width), lambda c, _: (0, c, 0)),
                pl.BlockSpec((seqs, span, columns), lambda c, _: (0, c, 0)),
            ],
        ),
        out_shape=[
            jax.ShapeDtypeStruct((seqs, count * span, width), jnp.bfloat16),
            jax.ShapeDtypeStruct((seqs, count * span, columns), jnp.float32),
        ],
        compiler_params=pltpu.CompilerParams(vmem_limit_bytes=48 << 20),
        cost_estimate=slight(),
    )(me.reshape(1).astype(jnp.int32), gains, weight, *blocks)


def by_rows(kernel, places, operands, dtype):
    rows, width = operands[0].shape
    tile = min(512 if kernel is order_kernel else 256, rows)
    if width // places.shape[0] % LANES != 0:
        return None

    def spec(shape):
        if shape[0] == rows:
            return pl.BlockSpec((tile, shape[1]), lambda i, places: (i, 0))
        return pl.BlockSpec(shape, lambda i, places: (0, 0))

    return pl.pallas_call(
        kernel,
        grid_spec=pltpu.PrefetchScalarGridSpec(
            num_scalar_prefetch=1,
            grid=(rows // tile,),
            in_specs=[spec(value.shape) for value in operands],
            out_specs=spec((rows, width)),
        ),
        out_shape=jax.ShapeDtypeStruct((rows, width), dtype),
        compiler_params=pltpu.CompilerParams(vmem_limit_bytes=48 << 20),
        cost_estimate=slight(),
    )(places, *operands)


def tied(*values):
    return lax.optimization_barrier(values)


def ring_of(size):
    return list(range(0, size, 2)) + list(range(size - 1, 0, -2))


def ring_step(value, size, way):
    order = ring_of(size)
    return lax.ppermute(value, "dp", [(order[i], order[(i + way) % size]) for i in range(size)])


def ring_places(size):
    order = ring_of(size)
    place = {d: i for i, d in enumerate(order)}
    table = [[order[(place[d] + k) % size] for k in range(size)] for d in range(size)]
    return jnp.array(table, jnp.int32)[lax.axis_index("dp")]


def to_ring_order(value, places):
    ordered = by_rows(order_kernel, places, [value], value.dtype)
    if ordered is not None:
        return ordered
    size = places.shape[0]
    return value.reshape(value.shape[0], size, -1)[:, places].reshape(value.shape)


def from_ring_order(value, places):
    size = places.shape[0]
    back = jnp.zeros((size,), jnp.int32).at[places].set(jnp.arange(size, dtype=jnp.int32))
    return value.reshape(value.shape[0], size, -1)[:, back].reshape(value.shape)


def finish(kernel, places, operands, dtype):
    done = by_rows(kernel, places, operands, dtype)
    if done is not None:
        return done
    if kernel is finish_kernel:
        total = operands[0] + total_of(operands[1:])
    else:
        normed, scaler = rms_parts(operands[1].astype(jnp.float32))
        total = operands[0] + norm_back(normed, scaler, total_of(operands[3:]), operands[2][0])
    return from_ring_order(total.astype(dtype), places)


class Gathering:
    def __init__(self, block, size):
        self.size, self.taken, self.columns = size, 0, block.shape[1]
        self.blocks = {0: block}
        self.up = self.down = block

    def step(self):
        self.taken += 1
        if self.taken < self.size // 2:
            self.up, self.down = ring_step(self.up, self.size, 1), ring_step(self.down, self.size, -1)
        else:
            half = self.columns // 2 // LANES * LANES
            self.up = ring_step(self.up[:, :half], self.size, 1)
            self.down = ring_step(self.down[:, half:], self.size, -1)
        self.keep()

    def keep(self):
        if self.taken < self.size // 2:
            self.blocks[self.size - self.taken], self.blocks[self.taken] = self.up, self.down
        else:
            self.blocks[self.taken] = (self.up, self.down)

    def hold(self, *others):
        self.up, self.down, *others = tied(self.up, self.down, *others)
        self.keep()
        return others

    def all(self):
        while self.taken < self.size // 2:
            self.step()
        whole = []
        for k in range(self.size):
            whole.extend(self.blocks[k] if k == self.size // 2 else [self.blocks[k]])
        return whole


class Summing:
    def __init__(self, terms, size):
        self.terms, self.size, self.taken = terms, size, 0
        self.rows, self.columns = terms.shape[0] // size, terms.shape[1]
        self.up = self.down = None

    def part(self, k):
        k = k % self.size
        return self.terms[k * self.rows : (k + 1) * self.rows]

    def send(self):
        self.taken += 1
        if self.taken == 1:
            half = self.columns // 2 // LANES * LANES
            far = self.part(self.size // 2)
            self.up, self.down = far[:, :half], far[:, half:]
        self.up, self.down = ring_step(self.up, self.size, 1), ring_step(self.down, self.size, -1)

    def hold(self, *others):
        self.up, self.down, *others = tied(self.up, self.down, *others)
        return others

    def add(self):
        f32 = jnp.float32
        up, down = self.up.astype(f32), self.down.astype(f32)
        if self.taken == 1:
            up = jnp.pad(up, ((0, 0), (0, self.columns - up.shape[1])))
            down = jnp.pad(down, ((0, 0), (self.columns - down.shape[1], 0)))
        k = self.size // 2 - self.taken
        if k == 0:
            return up + down + self.part(0).astype(f32)
        low = self.terms.dtype
        self.up, self.down = (up + self.part(k).astype(f32)).astype(low), (down + self.part(-k).astype(f32)).astype(low)

    def total(self):
        while self.taken < self.size // 2 - 1:
            self.send()
            self.add()
        if self.taken < self.size // 2:
            self.send()
        return self.add()


def sum_everywhere(value, size):
    sent = jnp.broadcast_to(value[None], (size,) + value.shape)
    return jnp.sum(lax.all_to_all(sent, ("dp", "ctx"), 0, 0, tiled=True), axis=0)


def ctx_send(value, k, size):
    return lax.ppermute(value, "ctx", [(i, i ^ k) for i in range(size)])


def to_chips(block, size):
    return {k: ctx_send(block, k, size) for k in range(2, size, 2)}


def from_pairs(far, size):
    return {k + 1: ctx_send(far[k], 1, size) for k in far}


def far_sums(blocks, chips, size):
    return {
        k: (blocks[k].astype(jnp.float32) + ctx_send(blocks[k + 1], 1, size).astype(jnp.float32)).astype(jnp.bfloat16)
        for k in chips
    }


def group_parts(blocks, size, far=None):
    far = far_sums(blocks, range(2, size, 2), size) if far is None else far
    return [blocks[0], ctx_send(blocks[1], 1, size)] + [ctx_send(far[k], k, size) for k in far]


def total_of(parts):
    total = parts[0].astype(jnp.float32)
    for part in parts[1:]:
        total = total + part.astype(jnp.float32)
    return total


def exchange(blocks):
    return lax.all_to_all(blocks, "ctx", 0, 0, tiled=True)


def rms_parts(values):
    scaler = lax.rsqrt(jnp.mean(values * values, axis=-1, keepdims=True) + epsilon)
    return values * scaler, scaler


def norm_back(normed, scaler, upstream, gain):
    scaled = upstream * gain
    return scaler * (scaled - normed * jnp.mean(scaled * normed, axis=-1, keepdims=True))


def tn(left, right):
    return lax.dot_general(left, right, (((0,), (0,)), ((), ())), preferred_element_type=jnp.float32)


def rope_tables(length):
    frequency = jnp.exp(jnp.arange(HEAD // 2, dtype=jnp.float32) * (-2.0 * math.log(rope_base) / HEAD))
    angles = jnp.arange(length, dtype=jnp.float32)[:, None] * frequency[None, :]
    cosine, sine = jnp.cos(angles), jnp.sin(angles)
    return (
        jnp.concatenate([cosine] * 4, axis=1),
        jnp.concatenate([-sine, sine, -sine, sine], axis=1),
    )


def split_heads(matrix, ctx):
    rows = matrix.shape[0]
    kvl = KV_HEADS // ctx
    pad = kvl % 2 * HEAD
    query, key, value = jnp.split(matrix, [HEADS * HEAD, (HEADS + KV_HEADS) * HEAD], axis=1)
    parts = [
        query.reshape(rows, ctx, -1),
        jnp.pad(key.reshape(rows, ctx, -1), ((0, 0), (0, 0), (0, pad))),
        jnp.pad(value.reshape(rows, ctx, -1), ((0, 0), (0, 0), (0, pad))),
    ]
    return jnp.concatenate(parts, axis=2).transpose(1, 0, 2)


def merge_heads(parts):
    ctx, rows, _ = parts.shape
    kvl = KV_HEADS // ctx
    wide = (kvl + 1) // 2 * LANES
    query = parts[:, :, : kvl * LANES]
    key = parts[:, :, kvl * LANES : kvl * LANES + kvl * HEAD]
    value = parts[:, :, kvl * LANES + wide : kvl * LANES + wide + kvl * HEAD]
    return jnp.concatenate([part.transpose(1, 0, 2).reshape(rows, -1) for part in (query, key, value)], axis=1)


def split_columns(matrix, ctx, wide):
    parts = matrix.reshape(matrix.shape[0], ctx, -1).transpose(1, 0, 2)
    return jnp.pad(parts, ((0, 0), (0, 0), (0, wide - parts.shape[2])))


def merge_columns(parts, keep):
    return parts[:, :, :keep].transpose(1, 0, 2).reshape(parts.shape[1], -1)


def local(
    dp, ctx, tokens, segments, qkv_weight, out_weight, gate_weight, up_weight, down_weight,
    norm_gains, head_gains, cotangent,
):
    seqs, span, width = tokens.shape
    rows = seqs * span
    length = segments.shape[1]
    kvl = KV_HEADS // ctx
    ffl = gate_weight.shape[1] // ctx
    shard = qkv_weight.shape[0]
    me = lax.axis_index("ctx")
    bf16, f32 = jnp.bfloat16, jnp.float32

    places = ring_places(dp)
    ffp = -(-ffl // LANES) * LANES
    hpl = HEADS * HEAD // ctx
    head_wide = (kvl + 2 * ((kvl + 1) // 2)) * LANES
    gain_rows = jnp.pad(jnp.transpose(norm_gains), ((0, 0), (0, LANES - 2)))
    first = [
        split_heads(qkv_weight, ctx),
        split_columns(jnp.transpose(out_weight), ctx, hpl),
        jnp.broadcast_to(gain_rows[None], (ctx, shard, LANES)),
    ]
    rest = [split_columns(part, ctx, ffp) for part in (gate_weight, up_weight, jnp.transpose(down_weight))]
    first, rest = jnp.concatenate(first, axis=2), jnp.concatenate(rest, axis=2)
    first = Gathering(exchange(first).reshape(ctx * shard, -1), dp)
    rest = exchange(rest).reshape(ctx * shard, -1)
    inputs_low = to_ring_order(tokens.reshape(rows, width), places)
    cotangent = to_ring_order(cotangent.reshape(rows, width), places)
    start = jnp.sum((segments[:, None, :] < segments[:, :, None]).astype(jnp.int32), axis=2)[:, None, :]
    tables = rope_tables(length)
    head_gain = head_gains.astype(f32)
    gains = jnp.pad(jnp.concatenate([head_gain, head_gain], axis=1), ((0, 6), (0, 0)))
    first.step()
    first.step()
    rest, start, tables, cotangent = first.hold(rest, start, tables, cotangent)
    inputs_low, rest = tied(inputs_low, rest)
    first.step()
    while first.taken < dp // 2:
        first.step()
    x_far, x_near = to_chips(inputs_low, ctx), ctx_send(inputs_low, 1, ctx)
    rest, x_near = first.hold(rest, x_near)
    rest = Gathering(rest, dp)
    rest.step()
    edges = (0, head_wide, head_wide + hpl, head_wide + hpl + LANES)
    qkv_full, out_own, gains_full = assemble(first.all(), edges)
    gains_full = jnp.transpose(gains_full[:, :2]).astype(f32)

    out_far, out_near = to_chips(out_own, ctx), ctx_send(out_own, 1, ctx)
    c_near = ctx_send(cotangent, 1, ctx)
    x_far, out_far, qkv_full, gains_full, c_near, out_near = rest.hold(
        x_far, out_far, qkv_full, gains_full, c_near, out_near
    )
    out_full = {0: out_own, 1: out_near, **out_far, **from_pairs(out_far, ctx)}
    x_far, cotangent = tied(x_far, cotangent)
    rest.step()
    x_all = {0: inputs_low, 1: x_near, **x_far, **from_pairs(x_far, ctx)}
    c_far = to_chips(cotangent, ctx)
    hidden_one, proj = project([x_all[k] for k in range(ctx)], gains_full, qkv_full, me, span)

    kept = [attend(proj, start, tables, gains, kvl, 0)]
    out_full = jnp.concatenate([out_full[k] for k in range(ctx)], axis=1)
    kept[0], proj, out_full = rest.hold(kept[0], proj, out_full)
    rest.step()
    kept.extend(attend(proj, start, tables, gains, kvl, n) for n in range(1, seqs))
    atts, c_far = tied([att for att, _ in kept], c_far)
    kept = [(att, lse) for att, (_, lse) in zip(atts, kept)]
    parts = jnp.concatenate(atts, axis=0).reshape(seqs, ctx, span, -1)
    parts = [lax.dynamic_index_in_dim(parts, me ^ k, 1, keepdims=False).reshape(rows, -1) for k in range(ctx)]
    parts = [parts[0]] + [ctx_send(parts[k], k, ctx) for k in range(1, ctx)]
    (parts,) = rest.hold(parts)
    att_rows = jnp.concatenate(parts, axis=1)
    inputs = inputs_low.astype(f32)
    middle = inputs + nt(att_rows, out_full)
    unit_two, scaler_two = rms_parts(middle)
    hidden_two = (unit_two * gains_full[1]).astype(bf16)
    hidden_two, c_far = tied(hidden_two, c_far)
    upstream = {0: cotangent, 1: c_near, **c_far, **from_pairs(c_far, ctx)}
    rest_blocks = rest.all()
    hidden_two = {k: ctx_send(hidden_two, k, ctx) if k else hidden_two for k in [0, 1, *range(2, ctx, 2)]}

    done, written = {}, []
    for k in range(0, ctx, 2):
        if k:
            written[0], hidden_two[k] = tied(written[0], hidden_two[k])
            hidden_two[k + 1] = ctx_send(hidden_two[k], 1, ctx)
        pairs = (hidden_two[k], hidden_two[k + 1]), (upstream[k], upstream[k + 1])
        outs = feed_forward(*pairs, rest_blocks, ffp, k // 2, ctx // 2, written)
        written, done[k] = list(outs[:3]), [None, *outs[3:]]
    chips = list(range(2, ctx, 2))
    far_two = far_sums({k + n: done[k][1 + n] for k in done for n in (0, 1)}, chips, ctx)
    two_near = ctx_send(done[0][2], 1, ctx)
    ffn_out = {k + n: done[k][3 + n] for k in done for n in (0, 1)}
    out_hop = {k: ctx_send(ffn_out[k + 1], 1, ctx) for k in chips}
    acts, far_two, two_near, out_hop = tied(written, far_two, two_near, out_hop)
    wide = weight_grads(acts[1], acts[2], acts[0])
    two_got = [ctx_send(far_two[k], k, ctx) for k in chips]
    wide, two_got = tied(wide, two_got)
    wide = Summing(wide, dp)
    wide.send()
    d_two = total_of([done[0][1], two_near, *two_got])
    d_middle = cotangent.astype(f32) + norm_back(unit_two, scaler_two, d_two, gains_full[1])
    d_low = d_middle.astype(bf16)
    d_att = nn(d_low, out_full).astype(bf16)
    d_att, d_low = tied([d_att[:, k * hpl : (k + 1) * hpl] for k in range(ctx)], d_low)
    d_att = [d_att[0]] + [ctx_send(d_att[k], k, ctx) for k in range(1, ctx)]
    out_terms = tn(d_low, att_rows).astype(bf16)
    out_terms = {k: out_terms[:, k * hpl : (k + 1) * hpl] for k in range(ctx)}
    (out_terms,) = wide.hold(out_terms)
    wide.add()
    (out_terms,) = wide.hold(out_terms)
    wide.send()
    far_out = {k: total_of([ffn_out[k], out_hop[k]]).astype(bf16) for k in chips}
    d_att, out_terms, far_out, near_out = tied(d_att, out_terms, far_out, ffn_out[1])
    out_got = [ctx_send(far_out[k], k, ctx) for k in chips]
    far_terms = far_sums(out_terms, chips, ctx)
    out_near = ctx_send(near_out, 1, ctx)

    def back(n):
        blocks = jnp.stack(d_att).reshape(ctx, seqs, span, -1)[:, n]
        blocks = [lax.dynamic_index_in_dim(blocks, me ^ c, 0, keepdims=False) for c in range(ctx)]
        grads = jnp.concatenate(blocks, axis=0)[None]
        return list(attend_back(proj, start, tables, gains, *kept[n], grads, kvl, n))

    backs = [back(0)]
    backs[0], far_terms, out_near = wide.hold(backs[0], far_terms, out_near)
    wide.add()
    (d_att,) = wide.hold(d_att)
    wide.send()
    terms_got = group_parts(out_terms, ctx, far_terms)
    backs.extend(back(n) for n in range(1, seqs))
    backs[1:], terms_got, out_got = wide.hold(backs[1:], terms_got, out_got)
    wide.add()
    (backs,) = wide.hold(backs)
    wide.send()

    d_proj = jnp.concatenate([part[0] for part in backs], axis=0).reshape(seqs * length, -1)
    d_one = nt(d_proj, qkv_full).astype(bf16).reshape(seqs, ctx, span, width)
    d_one = [lax.dynamic_index_in_dim(d_one, me ^ k, 1, keepdims=False).reshape(rows, width) for k in range(ctx)]
    far_one = far_sums(d_one, chips, ctx)
    d_proj, far_one = tied(d_proj, far_one)
    d_one = group_parts(d_one, ctx, far_one)
    out_terms = total_of(terms_got).astype(bf16)
    heads = sum(part[1][0] for part in backs)
    last = (tn(hidden_one.reshape(seqs * length, width), d_proj).astype(bf16))
    head_terms = sum_everywhere(heads, dp * ctx)
    last, head_terms = wide.hold(last, head_terms)
    last = Summing(jnp.concatenate([last, out_terms], axis=1), dp)
    last.send()
    output = finish(finish_kernel, places, [middle, done[0][3], out_near, *out_got], bf16)
    output, d_middle = tied(output, d_middle)
    input_grad = finish(input_grad_kernel, places, [d_middle, inputs_low, gains_full] + d_one, f32)
    last.add()
    last.send()
    (input_grad,) = last.hold(input_grad)
    (input_grad,) = wide.hold(input_grad)
    last.add()
    last.send()
    wide = wide.total().astype(bf16)
    wide = exchange(wide.reshape(ctx, shard, -1))
    while last.taken < dp // 2:
        last.hold()
        last.add()
        last.send()
    wide, head_terms = last.hold(wide, head_terms)
    last = last.add()
    head_terms = head_terms[:2]

    wide = wide.astype(f32)
    gate_grad = merge_columns(wide[:, :, :ffp], ffl)
    up_grad = merge_columns(wide[:, :, ffp : 2 * ffp], ffl)
    down_grad = merge_columns(wide[:, :, 2 * ffp :], ffl)
    last = exchange(last.astype(bf16).reshape(ctx, shard, -1)).astype(f32)
    qkv_grad = merge_heads(last[:, :, :head_wide])
    out_grad = merge_columns(last[:, :, head_wide:], hpl)

    own_gain = norm_gains.astype(f32)
    norm_one = jnp.sum(qkv_weight.astype(f32) * qkv_grad, axis=1) / own_gain[0]
    norm_two = jnp.sum(gate_weight.astype(f32) * gate_grad + up_weight.astype(f32) * up_grad, axis=1) / own_gain[1]
    head_grad = head_terms[:, :HEAD] + head_terms[:, HEAD:]
    return (
        output.reshape(seqs, span, width),
        input_grad.reshape(seqs, span, width),
        qkv_grad,
        jnp.transpose(out_grad),
        gate_grad,
        up_grad,
        jnp.transpose(down_grad),
        jnp.stack([norm_one, norm_two]),
        head_grad,
    )


def solution(mesh):
    both = ("dp", "ctx")
    in_specs = (
        P("dp", "ctx", None),
        P("dp", None),
        P(both, None),
        P(None, both),
        P(both, None),
        P(both, None),
        P(None, both),
        P(None, both),
        P(),
        P("dp", "ctx", None),
    )
    out_specs = (
        P("dp", "ctx", None),
        P("dp", "ctx", None),
        P(both, None),
        P(None, both),
        P(both, None),
        P(both, None),
        P(None, both),
        P(None, both),
        P(),
    )
    body = functools.partial(local, mesh.shape["dp"], mesh.shape["ctx"])
    return jax.shard_map(body, mesh=mesh, in_specs=in_specs, out_specs=out_specs, check_vma=False)
```
